32 devices in a mesh: batch: 8 (over z, y), proto: 4 (over x, core).
Axes of the slice: x: 2, y: 2, z: 4, core: 2. Of those that a mesh axis runs over, the one named last changes fastest.
Arguments:
- features: bfloat16 [1024, 1536], P('batch'), may hold values from -20 to 20
- w_first: bfloat16 [1536, 4096], P(None, 'proto'), may hold values from -0.15625 to 0.15625
- bn_gain: float32 [4096], P('proto'), may hold values from 0.1 to 1.9
- bn_shift: float32 [4096], P('proto'), may hold values from -3 to 3
- w_second: bfloat16 [4096, 256], P('proto'), may hold values from -1 to 1
- prototypes: bfloat16 [16384, 256], P('proto'), may hold values from -6 to 6
- partner: int32 [1024], P('batch'), may hold values from 0 to 127, as said below
Outputs:
- crop_penalty: float32 [1024], P('batch')
- grad_w1: float32 [1536, 4096], P('batch', 'proto')
- grad_gain: float32 [4096], P('proto')
- grad_shift: float32 [4096], P('proto')
- grad_w2: float32 [4096, 256], P('proto', 'batch')
The draws below stay inside these ranges and needn't reach their ends.
Inputs may be any that keep to these rules, and one draw needn't show every extreme that they name: partner_i is a crop index within crop i's group of 128 consecutive crops; the partner of partner_i is i, and partner_i is never i.
All inputs are finite; a program needn't handle non-finite values.
Results may differ from the reference program's by a relative error of at most 0.015.
Values sent between devices are 32-bit elements; how exact they have to be, the bound alone decides.
No kernel may reach another device: no remote copies, remote signals or barrier semaphores. Data moves between devices by JAX's collectives and lax.ppermute only.
A program may use at most 64 MiB of HBM per device.

```python
import jax
import jax.numpy as jnp
from jax import lax

D_IN = 1536
HIDDEN_UNITS = 4096
EMB = 256
CROP_DEV = 128
ITERS = 3
PROTOS = 16384
CROPS = 1024


def draw_features(key, part):
    first_key = jax.random.fold_in(key, 0)
    row_ramp = 1.0 + 2.0 * jnp.arange(CROPS, dtype=jnp.float32)[:, None] / max(CROPS - 1, 1)
    values = jax.random.normal(first_key, (CROPS, D_IN), jnp.float32) * row_ramp
    return jnp.clip(values, -20.0, 20.0).astype(jnp.bfloat16)


def shared_signs(key):
    flips = jax.random.bernoulli(jax.random.fold_in(key, 7), 0.5, (EMB,))
    return 2.0 * flips.astype(jnp.float32) - 1.0


def draw_w_second(key, part):
    signs = shared_signs(key)
    noise_key, along_key = jax.random.split(jax.random.fold_in(key, 11))
    noise = jnp.clip(jax.random.normal(noise_key, (HIDDEN_UNITS, EMB), jnp.float32), -4.0, 4.0)
    along = jnp.clip(jax.random.normal(along_key, (HIDDEN_UNITS,), jnp.float32), -3.0, 3.0)
    values = (noise + along[:, None] * signs[None, :]) * HIDDEN_UNITS ** (-0.5)
    return values.astype(jnp.bfloat16)


def draw_prototypes(key, part):
    signs = shared_signs(key)
    noise_key, along_key = jax.random.split(jax.random.fold_in(key, 13), 2)
    noise = jnp.clip(jax.random.normal(noise_key, (PROTOS, EMB), jnp.float32), -4.0, 4.0)
    along = jax.random.uniform(along_key, (PROTOS,), jnp.float32, -1.5, 1.5)
    values = noise + along[:, None] * signs[None, :]
    return values.astype(jnp.bfloat16)


def shuffle(subkey):
    return jax.random.permutation(subkey, CROP_DEV)


def draw_partner(key, part):
    groups = CROPS // CROP_DEV
    orders = jax.vmap(shuffle)(jax.random.split(key, groups))
    swapped = orders.reshape(groups, CROP_DEV // 2, 2)[:, :, ::-1].reshape(groups, CROP_DEV)
    inverse = jnp.argsort(orders, axis=1)
    paired = jnp.take_along_axis(swapped, inverse, axis=1)
    return paired.reshape(CROPS).astype(jnp.int32)


def shard_levels(key, shape, pieces, least, high):
    loudness, own = 1.0, jax.random.fold_in(key, 6)
    for dim, shards_of in pieces:
        heights = jnp.exp(jax.random.uniform(jax.random.fold_in(own, dim), (shards_of,), jnp.float32, least / len(pieces), high / len(pieces)))
        loudness = loudness * jnp.repeat(heights, shape[dim] // shards_of).reshape([-1 if axis == dim else 1 for axis in range(len(shape))])
    return loudness


def centred(rng, dims, scale, most, cuts=(), kind=jnp.bfloat16):
    factor_of = shard_levels(rng, dims, cuts, -0.22, 0.18) if cuts else 1.0
    values = jax.random.normal(rng, dims, jnp.float32) * scale * factor_of
    return jnp.minimum(jnp.maximum(values, -most), most).astype(kind)


def setup_inputs(seed: int = 0) -> dict:
    key_of = jax.random.split(jax.random.key(seed), 8)
    features = draw_features(jax.random.fold_in(key_of[7], 71), 0)
    w_first = centred(key_of[1], (D_IN, HIDDEN_UNITS), D_IN ** -0.5, 0.15625, ((1, 4),))
    bn_gain = jnp.clip(1.0 + 0.18 * jax.random.normal(key_of[2], (HIDDEN_UNITS,), jnp.float32), 0.1, 1.9)
    bn_shift = centred(key_of[3], (HIDDEN_UNITS,), 0.5, 3.0, ((0, 4),), jnp.float32)
    w_second = draw_w_second(jax.random.fold_in(key_of[7], 71), 0)
    prototypes = draw_prototypes(jax.random.fold_in(key_of[7], 71), 0)
    partner = draw_partner(jax.random.fold_in(key_of[7], 71), 0)
    return {"features": features, "w_first": w_first, "bn_gain": bn_gain, "bn_shift": bn_shift, "w_second": w_second, "prototypes": prototypes, "partner": partner}


balancing_epsilon = 0.05
sharpness_divisor = 0.1
penalty_weighting = 64.0

def reference(features, w_first, bn_gain, bn_shift, w_second, prototypes, partner):
    f32 = jnp.float32
    pre_act = jnp.dot(features, w_first, preferred_element_type=f32)
    batch_mean = lax.optimization_barrier(jnp.sum(pre_act, 0)) / CROPS
    batch_var = lax.optimization_barrier(jnp.sum(pre_act * pre_act, 0)) / CROPS - batch_mean * batch_mean
    inv_std = lax.rsqrt(batch_var + 1e-05)
    normed = (pre_act - batch_mean) * inv_std
    shifted = bn_gain * normed + bn_shift
    hidden = jnp.maximum(shifted, 0.0).astype(jnp.bfloat16)
    raw_emb = jnp.dot(hidden, w_second, preferred_element_type=f32)
    inv_norm = lax.rsqrt(lax.optimization_barrier(jnp.sum(raw_emb * raw_emb, 1, keepdims=True)) + 1e-06)
    embedded = raw_emb * inv_norm
    emb_low = embedded.astype(jnp.bfloat16)
    proto_float = prototypes.astype(f32)
    unit_protos = (proto_float * lax.rsqrt(lax.optimization_barrier(jnp.sum(proto_float * proto_float, 1, keepdims=True)) + 1e-06)).astype(jnp.bfloat16)
    groups = CROPS // CROP_DEV
    emb_blocks = emb_low.reshape(groups, CROP_DEV, EMB)
    partner_blocks = partner.reshape(groups, CROP_DEV)

    def scores_in_block(block_slice):
        return lax.dot_general(block_slice, unit_protos, (((1,), (1,)), ((), ())), preferred_element_type=f32)

    def first_step(running, block_slice):
        exponent_codes = jnp.exp(scores_in_block(block_slice) / balancing_epsilon)
        ones_rows = jnp.ones((CROP_DEV,), f32)
        return (running + jnp.dot(ones_rows, exponent_codes, precision=lax.Precision.HIGHEST), None)
    col_mass, unused = lax.scan(first_step, jnp.zeros((PROTOS,), f32), emb_blocks)
    scale_cols = 1.0 / col_mass

    def make_step(current_cols):

        def later_step(running, block_slice):
            exponent_codes = jnp.exp(scores_in_block(block_slice) / balancing_epsilon)
            rows = 1.0 / lax.optimization_barrier(jnp.sum(exponent_codes * current_cols, 1))
            return (running + jnp.dot(rows, exponent_codes, precision=lax.Precision.HIGHEST), None)
        return later_step
    for iteration in range(ITERS - 1):
        col_mass, unused = lax.scan(make_step(scale_cols), jnp.zeros((PROTOS,), f32), emb_blocks)
        scale_cols = 1.0 / col_mass

    def final_pass(pair):
        block_slice, partners = pair
        centroid_affinity = scores_in_block(block_slice)
        exponent_codes = jnp.exp(centroid_affinity / balancing_epsilon)
        weighted = exponent_codes * scale_cols
        rows = 1.0 / lax.optimization_barrier(jnp.sum(weighted, 1))
        codes = weighted * rows[:, None]
        desired_assignments = jnp.take(codes, partners, axis=0)
        raised_affinity = jnp.exp(centroid_affinity / sharpness_divisor)
        partition_total = lax.optimization_barrier(jnp.sum(raised_affinity, 1))
        penalty_array = jnp.log(partition_total) - lax.optimization_barrier(jnp.sum(desired_assignments * centroid_affinity, 1)) / sharpness_divisor
        normalized_likelihood = raised_affinity / partition_total[:, None]
        affinity_derivative = (penalty_weighting * (normalized_likelihood - desired_assignments) / sharpness_divisor).astype(jnp.bfloat16)
        emb_grad = jnp.dot(affinity_derivative, unit_protos, preferred_element_type=f32)
        return (penalty_array, emb_grad)
    loss_blocks, grad_blocks = lax.map(final_pass, (emb_blocks, partner_blocks))
    crop_penalty = loss_blocks.reshape(CROPS)
    emb_grad = grad_blocks.reshape(CROPS, EMB)
    inner_prod = lax.optimization_barrier(jnp.sum(embedded * emb_grad, 1, keepdims=True))
    raw_grad = ((emb_grad - embedded * inner_prod) * inv_norm).astype(jnp.bfloat16)
    grad_w2 = lax.dot_general(hidden, raw_grad, (((0,), (0,)), ((), ())), preferred_element_type=f32)
    hidden_grad = lax.dot_general(raw_grad, w_second, (((1,), (1,)), ((), ())), preferred_element_type=f32)
    bn_grad = jnp.where(shifted > 0, hidden_grad, 0.0)
    grad_shift = lax.optimization_barrier(jnp.sum(bn_grad, 0))
    grad_gain = lax.optimization_barrier(jnp.sum(bn_grad * normed, 0))
    pre_grad = (bn_gain * inv_std * (bn_grad - grad_shift / CROPS - normed * grad_gain / CROPS)).astype(jnp.bfloat16)
    grad_w1 = lax.dot_general(features, pre_grad, (((0,), (0,)), ((), ())), preferred_element_type=f32)
    return (crop_penalty, grad_w1, grad_gain, grad_shift, grad_w2)
```

```python
import functools

import jax
import jax.numpy as jnp
from jax import lax
from jax.experimental import pallas as pl
from jax.experimental.pallas import tpu as pltpu
from jax.sharding import PartitionSpec as P

ITERS = 3
F32 = jnp.float32
BF16 = jnp.bfloat16
HIGHEST = lax.Precision.HIGHEST

balancing_epsilon = 0.05
sharpness_divisor = 0.1
penalty_weighting = 64.0

VMEM_BYTES = 48 * 1024 * 1024


def stages(n, first):
    out, stride = [], 1
    while stride < n:
        left = n // stride
        radix = first if stride == 1 else (4 if left % 4 == 0 else 2)
        radix = min(radix, left)
        out.append((stride, radix))
        stride *= radix
    return out


def swap(v, axis, mask):
    n = lax.axis_size(axis)
    return lax.ppermute(v, axis, [(i, i ^ mask) for i in range(n)])


def add_parts(parts):
    if len(parts) == 1:
        return parts[0]
    if len(parts) == 2:
        return parts[0] + parts[1]
    return (parts[0] + parts[1]) + (parts[2] + parts[3])


def exchange(v, axis, first):
    n = lax.axis_size(axis)
    if n & (n - 1):
        return [lax.psum(v, axis)]
    parts = [v]
    for stride, radix in stages(n, first):
        v = add_parts(parts)
        parts = [v] + [swap(v, axis, k * stride) for k in range(1, radix)]
    return parts


def batch_parts(v):
    n = lax.axis_size("batch")
    return exchange(v, "batch", 2 if (n.bit_length() - 1) % 2 else 4)


def proto_parts(v):
    return exchange(v, "proto", 2)


def whole(shape):
    return pl.BlockSpec(shape, lambda *_: (0,) * len(shape))


def params(**kw):
    return pltpu.CompilerParams(vmem_limit_bytes=VMEM_BYTES, **kw)


def cost(flops, nbytes, trans=0):
    return pl.CostEstimate(flops=int(flops), bytes_accessed=int(nbytes), transcendentals=int(trans))


def dot(a, b, dims, precision=None):
    return lax.dot_general(a, b, ((dims[0], dims[1]), ((), ())), precision=precision, preferred_element_type=F32)


def eye(n):
    return lax.broadcasted_iota(jnp.int32, (n, n), 0) == lax.broadcasted_iota(jnp.int32, (n, n), 1)


def to_lanes(col):
    n = col.shape[0]
    return jnp.sum(jnp.where(eye(n), col, 0.0), axis=0, keepdims=True)


def to_column(row):
    n = row.shape[1]
    return jnp.sum(jnp.where(eye(n), row, 0.0), axis=1, keepdims=True)


def first_kernel(f_ref, w_ref, pre_ref, mom_ref):
    pre = jnp.dot(f_ref[...], w_ref[...], preferred_element_type=F32)
    pre_ref[...] = pre
    mom_ref[0:1, :] = jnp.sum(pre, axis=0, keepdims=True)
    mom_ref[1:2, :] = jnp.sum(pre * pre, axis=0, keepdims=True)


def first_layer(features, w_first):
    rows, depth = features.shape
    hidden = w_first.shape[1]
    blk = min(256, hidden)
    return pl.pallas_call(
        first_kernel,
        grid=(hidden // blk,),
        in_specs=[whole((rows, depth)), pl.BlockSpec((depth, blk), lambda j: (0, j))],
        out_specs=[pl.BlockSpec((rows, blk), lambda j: (0, j)), pl.BlockSpec((2, blk), lambda j: (0, j))],
        out_shape=[jax.ShapeDtypeStruct((rows, hidden), F32), jax.ShapeDtypeStruct((2, hidden), F32)],
        compiler_params=params(),
        cost_estimate=cost(2 * rows * depth * hidden, 2 * depth * hidden + 4 * rows * hidden),
        name="first_layer",
    )(features, w_first)


def batch_norm(pre, stats, gain, shift):
    normed = (pre - stats[0:1, :]) * stats[1:2, :]
    return normed, gain * normed + shift


def second_kernel(crops_all, n_parts, *refs):
    parts = refs[:n_parts]
    pre_ref, gain_ref, shift_ref, w_ref, emb_ref, stats_ref = refs[n_parts:]
    moments = add_parts([p[...] for p in parts]) / crops_all
    mean = moments[0:1, :]
    var = moments[1:2, :] - mean * mean
    stats_ref[0:1, :] = mean
    stats_ref[1:2, :] = lax.rsqrt(var + 1e-05)
    _, shifted = batch_norm(pre_ref[...], stats_ref[...], gain_ref[...], shift_ref[...])
    low = jnp.maximum(shifted, 0.0).astype(BF16)
    emb_ref[...] = jnp.dot(low, w_ref[...], preferred_element_type=F32)


def second_layer(crops_all, parts, pre, gain, shift, w_second):
    rows, hidden = pre.shape
    width = w_second.shape[1]
    return pl.pallas_call(
        functools.partial(second_kernel, crops_all, len(parts)),
        out_shape=[jax.ShapeDtypeStruct((rows, width), F32), jax.ShapeDtypeStruct((2, hidden), F32)],
        compiler_params=params(),
        cost_estimate=cost(2 * rows * hidden * width, 4 * rows * hidden + 2 * hidden * width),
        name="second_layer",
    )(*parts, pre, gain, shift, w_second)


def unit_kernel(p_ref, u_ref):
    wide = p_ref[...].astype(F32)
    u_ref[...] = (wide * lax.rsqrt(jnp.sum(wide * wide, 1, keepdims=True) + 1e-06)).astype(BF16)


def unit_rows(prototypes):
    rows, width = prototypes.shape
    blk = min(1024, rows)
    return pl.pallas_call(
        unit_kernel,
        grid=(rows // blk,),
        in_specs=[pl.BlockSpec((blk, width), lambda j: (j, 0))],
        out_specs=pl.BlockSpec((blk, width), lambda j: (j, 0)),
        out_shape=jax.ShapeDtypeStruct((rows, width), BF16),
        compiler_params=params(),
        cost_estimate=cost(4 * rows * width, 4 * rows * width),
        name="unit_rows",
    )(prototypes)


def embed(raw):
    inv_norm = lax.rsqrt(jnp.sum(raw * raw, 1, keepdims=True) + 1e-06)
    return raw * inv_norm, inv_norm


def score_kernel(n_parts, *refs):
    parts = refs[:n_parts]
    u_ref, codes_ref, logits_ref, col_ref, denom_ref, total = refs[n_parts:]
    j = pl.program_id(0)
    raw = add_parts([p[...] for p in parts])
    embedded, _ = embed(raw)
    scores = dot(embedded.astype(BF16), u_ref[...], ((1,), (1,)))
    logits = jnp.exp(scores / sharpness_divisor)
    codes = logits * logits
    codes_ref[...] = codes
    logits_ref[...] = logits.astype(BF16)
    col_ref[...] = jnp.sum(codes, axis=0, keepdims=True)

    @pl.when(j == 0)
    def _():
        total[...] = jnp.zeros_like(total)

    total[...] += jnp.sum(logits, axis=1, keepdims=True)

    @pl.when(j == pl.num_programs(0) - 1)
    def _():
        denom_ref[...] = to_lanes(total[...])


def score(parts, units):
    rows, width = parts[0].shape
    protos = units.shape[0]
    blk = min(1024, protos)
    return pl.pallas_call(
        functools.partial(score_kernel, len(parts)),
        grid=(protos // blk,),
        in_specs=[whole((rows, width))] * len(parts) + [pl.BlockSpec((blk, width), lambda j: (j, 0))],
        out_specs=[
            pl.BlockSpec((rows, blk), lambda j: (0, j)),
            pl.BlockSpec((rows, blk), lambda j: (0, j)),
            pl.BlockSpec((1, blk), lambda j: (0, j)),
            whole((1, rows)),
        ],
        out_shape=[
            jax.ShapeDtypeStruct((rows, protos), F32),
            jax.ShapeDtypeStruct((rows, protos), BF16),
            jax.ShapeDtypeStruct((1, protos), F32),
            jax.ShapeDtypeStruct((1, rows), F32),
        ],
        scratch_shapes=[pltpu.VMEM((rows, 1), F32)],
        compiler_params=params(),
        cost_estimate=cost(2 * rows * protos * width, 6 * rows * protos, rows * protos),
        name="score",
    )(*parts, units)


def pack(table, lane_row, out_ref):
    rows, width = table.shape
    out_ref[0:rows, :] = table
    out_ref[rows:, :] = jnp.zeros((8, width), F32)
    out_ref[rows : rows + 1, 0:rows] = lane_row


def logit_kernel(l_ref, u_ref, d_ref, out_ref):
    pack(jnp.dot(l_ref[...], u_ref[...], preferred_element_type=F32), d_ref[...], out_ref)


def logit_sum(logits, units, denom):
    rows, protos = logits.shape
    width = units.shape[1]
    return pl.pallas_call(
        logit_kernel,
        out_shape=jax.ShapeDtypeStruct((rows + 8, width), F32),
        compiler_params=params(),
        cost_estimate=cost(2 * rows * protos * width, 2 * rows * protos + 2 * protos * width),
        name="logit_sum",
    )(logits, units, denom)


def row_kernel(n_parts, *refs):
    parts = refs[:n_parts]
    codes_ref, out_ref = refs[n_parts:]
    scale = 1.0 / add_parts([p[...] for p in parts])
    out_ref[...] = to_lanes(jnp.sum(codes_ref[...] * scale, axis=1, keepdims=True))


def row_pass(parts, codes):
    rows, protos = codes.shape
    return pl.pallas_call(
        functools.partial(row_kernel, len(parts)),
        out_shape=jax.ShapeDtypeStruct((1, rows), F32),
        compiler_params=params(),
        cost_estimate=cost(2 * rows * protos, 4 * rows * protos),
        name="row_pass",
    )(*parts, codes)


def col_kernel(n_parts, *refs):
    parts = refs[:n_parts]
    codes_ref, out_ref = refs[n_parts:]
    scale = to_column(1.0 / add_parts([p[...] for p in parts]))
    out_ref[...] = jnp.sum(codes_ref[...] * scale, axis=0, keepdims=True)


def col_pass(parts, codes):
    rows, protos = codes.shape
    return pl.pallas_call(
        functools.partial(col_kernel, len(parts)),
        out_shape=jax.ShapeDtypeStruct((1, protos), F32),
        compiler_params=params(),
        cost_estimate=cost(2 * rows * protos, 4 * rows * protos),
        name="col_pass",
    )(*parts, codes)


def target_kernel(n_parts, *refs):
    parts = refs[:n_parts]
    codes_ref, u_ref, partner_ref, out_ref = refs[n_parts:]
    rows = codes_ref.shape[0]
    scale = 1.0 / add_parts([p[...] for p in parts])
    weighted = codes_ref[...] * scale
    mass = jnp.sum(weighted, axis=1, keepdims=True)
    table = jnp.dot(weighted.astype(BF16), u_ref[...], preferred_element_type=F32)
    chosen = partner_ref[...] == lax.broadcasted_iota(jnp.int32, (rows, rows), 1)
    moved = dot(jnp.where(chosen, 1.0, 0.0).astype(F32), table, ((1,), (0,)), HIGHEST)
    pack(moved, jnp.sum(jnp.where(chosen, mass, 0.0), axis=0, keepdims=True), out_ref)


def target_sum(parts, codes, units, partner):
    rows, protos = codes.shape
    width = units.shape[1]
    return pl.pallas_call(
        functools.partial(target_kernel, len(parts)),
        out_shape=jax.ShapeDtypeStruct((rows + 8, width), F32),
        compiler_params=params(),
        cost_estimate=cost(2 * rows * protos * width, 4 * rows * protos + 2 * protos * width),
        name="target_sum",
    )(*parts, codes, units, partner)


def loss_kernel(n_raw, n_logit, n_target, *refs):
    raw = add_parts([p[...] for p in refs[:n_raw]])
    refs = refs[n_raw:]
    logit = add_parts([p[...] for p in refs[:n_logit]])
    refs = refs[n_logit:]
    target = add_parts([p[...] for p in refs[:n_target]])
    grad_ref, loss_ref = refs[n_target:]
    rows = raw.shape[0]
    embedded, inv_norm = embed(raw)
    denom_lanes = logit[rows : rows + 1, 0:rows]
    denom = to_column(denom_lanes)
    row_scale = to_column(1.0 / target[rows : rows + 1, 0:rows])
    wanted = target[0:rows, :] * row_scale
    emb_low = embedded.astype(BF16).astype(F32)
    cross = jnp.sum(wanted * emb_low, axis=1, keepdims=True)
    loss_ref[...] = jnp.log(denom_lanes) - to_lanes(cross) / sharpness_divisor
    emb_grad = penalty_weighting * (logit[0:rows, :] / denom - wanted) / sharpness_divisor
    inner = jnp.sum(embedded * emb_grad, 1, keepdims=True)
    grad_ref[...] = (emb_grad - embedded * inner) * inv_norm


def loss_grad(raw_parts, logit_parts, target_parts):
    rows, width = raw_parts[0].shape
    return pl.pallas_call(
        functools.partial(loss_kernel, len(raw_parts), len(logit_parts), len(target_parts)),
        out_shape=[jax.ShapeDtypeStruct((rows, width), F32), jax.ShapeDtypeStruct((1, rows), F32)],
        compiler_params=params(),
        cost_estimate=cost(20 * rows * width, 24 * rows * width),
        name="loss_grad",
    )(*raw_parts, *logit_parts, *target_parts)


def tail_kernel(crops_all, n_feat, n_grad, e_cols, *refs):
    feat_at, grad_at, pre_ref, stats_ref, gain_ref, shift_ref, w_ref = refs[:7]
    refs = refs[7:]
    feats, refs = refs[:n_feat], refs[n_feat:]
    grads, refs = refs[:n_grad], refs[n_grad:]
    w1_ref, w2_ref, gain_grad_ref, shift_grad_ref, feat_all, grad_all, grad_cols = refs

    @pl.when(pl.program_id(0) == 0)
    def _():
        for k in range(n_feat):
            rows = feats[k].shape[0]
            start = pl.multiple_of(feat_at[k] * rows, rows)
            feat_all[pl.ds(start, rows), :] = feats[k][...].astype(BF16)
        for k in range(n_grad):
            rows = grads[k].shape[0]
            start = pl.multiple_of(grad_at[k] * rows, rows)
            grad_all[pl.ds(start, rows), :] = grads[k][...].astype(BF16)
        shape = (grad_cols.shape[0], grad_all.shape[1])
        mine = lax.broadcasted_iota(jnp.int32, shape, 0) + grad_at[n_grad] * e_cols
        chosen = mine == lax.broadcasted_iota(jnp.int32, shape, 1)
        picked = dot(jnp.where(chosen, 1.0, 0.0).astype(BF16), grad_all[...], ((1,), (1,)))
        grad_cols[...] = picked.astype(BF16)

    stats = stats_ref[...]
    gain = gain_ref[...]
    normed, shifted = batch_norm(pre_ref[...], stats, gain, shift_ref[...])
    hidden = jnp.maximum(shifted, 0.0).astype(BF16)
    w2_ref[...] = jnp.dot(grad_cols[...], hidden, preferred_element_type=F32)[0:e_cols, :]
    hidden_grad = dot(grad_all[...], w_ref[...], ((1,), (1,)))
    bn_grad = jnp.where(shifted > 0, hidden_grad, 0.0)
    shift_grad = jnp.sum(bn_grad, axis=0, keepdims=True)
    gain_grad = jnp.sum(bn_grad * normed, axis=0, keepdims=True)
    shift_grad_ref[...] = shift_grad
    gain_grad_ref[...] = gain_grad
    pre_grad = gain * stats[1:2, :] * (bn_grad - shift_grad / crops_all - normed * (gain_grad / crops_all))
    w1_ref[...] = dot(feat_all[...], pre_grad.astype(BF16), ((0,), (0,)))


def tail(pre_all, stats, gain, shift, w_second, feats, feat_at, grads, grad_at, d_cols, e_cols):
    crops_all, hidden = pre_all.shape
    width = w_second.shape[1]
    blk = min(hidden, max(128, 256 * 1024 // crops_all))
    smem = pl.BlockSpec(memory_space=pltpu.SMEM)
    vmem = pl.BlockSpec(memory_space=pltpu.VMEM)

    def cols(n):
        return pl.BlockSpec((n, blk), lambda j: (0, j))

    return pl.pallas_call(
        functools.partial(tail_kernel, crops_all, len(feats), len(grads), e_cols),
        grid=(hidden // blk,),
        in_specs=[smem, smem, cols(crops_all), cols(2), cols(1), cols(1), pl.BlockSpec((blk, width), lambda j: (j, 0))]
        + [vmem] * (len(feats) + len(grads)),
        out_specs=[cols(d_cols), cols(e_cols), cols(1), cols(1)],
        out_shape=[
            jax.ShapeDtypeStruct((d_cols, hidden), F32),
            jax.ShapeDtypeStruct((e_cols, hidden), F32),
            jax.ShapeDtypeStruct((1, hidden), F32),
            jax.ShapeDtypeStruct((1, hidden), F32),
        ],
        scratch_shapes=[
            pltpu.VMEM((crops_all, d_cols), BF16),
            pltpu.VMEM((crops_all, width), BF16),
            pltpu.VMEM((-(-e_cols // 16) * 16, crops_all), BF16),
        ],
        compiler_params=params(),
        cost_estimate=cost(2 * crops_all * hidden * (width + d_cols), 4 * crops_all * hidden),
        name="tail",
    )(feat_at, grad_at, pre_all, stats, gain, shift, w_second, *feats, *grads)


def rotate(v, axis, k):
    n = lax.axis_size(axis)
    return lax.ppermute(v, axis, [(i, (i + k) % n) for i in range(n)])


def body(features, w_first, bn_gain, bn_shift, w_second, prototypes, partner):
    n_batch = lax.axis_size("batch")
    me = lax.axis_index("batch")
    rows, depth = features.shape
    width = w_second.shape[1]
    crops_all = rows * n_batch
    d_cols, e_cols = depth // n_batch, width // n_batch
    small = n_batch <= 8
    gain, shift = bn_gain[None, :], bn_shift[None, :]

    pre, moments = first_layer(features, w_first)
    pre_all = lax.all_gather(pre, "batch", tiled=True)
    moment_parts = batch_parts(moments)
    emb_part, stats = second_layer(crops_all, moment_parts, pre, gain, shift, w_second)
    raw_parts = proto_parts(emb_part)

    by_owner = jnp.swapaxes(features.astype(F32).reshape(rows, n_batch, d_cols), 0, 1)
    by_owner, _ = lax.optimization_barrier((by_owner, emb_part))
    if small:
        feats = [lax.dynamic_index_in_dim(by_owner, me, 0, False)]
        for k in range(1, n_batch):
            piece = lax.dynamic_index_in_dim(by_owner, lax.rem(me + k, n_batch), 0, False)
            feats.append(rotate(piece, "batch", k))
        feat_at = lax.rem(me - jnp.arange(n_batch, dtype=jnp.int32) + n_batch, n_batch)
    else:
        feats = [lax.all_to_all(by_owner, "batch", 0, 0).reshape(crops_all, d_cols)]
        feat_at = jnp.zeros((1,), jnp.int32)

    units = unit_rows(prototypes)
    codes, logits, col_part, denom = score(raw_parts, units)
    logit_parts = proto_parts(logit_sum(logits, units, denom))
    for iteration in range(ITERS - 1):
        row_part = row_pass(batch_parts(col_part), codes)
        col_part = col_pass(proto_parts(row_part), codes)
    target_parts = proto_parts(target_sum(batch_parts(col_part), codes, units, partner[:, None]))
    raw_grad, penalty = loss_grad(raw_parts, logit_parts, target_parts)

    if small:
        grads = [raw_grad] + [rotate(raw_grad, "batch", k) for k in range(1, n_batch)]
        grad_at = lax.rem(me - jnp.arange(n_batch, dtype=jnp.int32) + n_batch, n_batch)
    else:
        grads = [lax.all_gather(raw_grad, "batch", tiled=True)]
        grad_at = jnp.zeros((1,), jnp.int32)
    grad_at = jnp.concatenate([grad_at, me[None].astype(jnp.int32)])
    grad_w1, grad_w2, grad_gain, grad_shift = tail(
        pre_all, stats, gain, shift, w_second, feats, feat_at, grads, grad_at, d_cols, e_cols
    )
    return (penalty[0], grad_w1, grad_gain[0], grad_shift[0], grad_w2.T)


def solution(mesh):
    return jax.shard_map(
        body,
        mesh=mesh,
        in_specs=(
            P("batch", None),
            P(None, "proto"),
            P("proto"),
            P("proto"),
            P("proto", None),
            P("proto", None),
            P("batch"),
        ),
        out_specs=(P("batch"), P("batch", "proto"), P("proto"), P("proto"), P("proto", "batch")),
        check_vma=False,
    )
```

```python
import functools

import jax
import jax.numpy as jnp
from jax import lax
from jax.experimental import pallas as pl
from jax.experimental.pallas import tpu as pltpu
from jax.sharding import PartitionSpec as P

ITERS = 3
F32 = jnp.float32
BF16 = jnp.bfloat16
HIGHEST = lax.Precision.HIGHEST

balancing_epsilon = 0.05
sharpness_divisor = 0.1
penalty_weighting = 64.0


def stages(n, first, stride=1):
    out, radix = [], first
    while stride < n:
        radix = min(radix, n // stride)
        out.append((stride, radix))
        stride *= radix
        radix = 4 if (n // stride) % 4 == 0 else 2
    return out


def swap(v, axis, mask):
    n = lax.axis_size(axis)
    return lax.ppermute(v, axis, [(i, i ^ mask) for i in range(n)])


def add_parts(parts):
    if len(parts) == 4:
        return (parts[0] + parts[1]) + (parts[2] + parts[3])
    return functools.reduce(lambda x, y: x + y, parts)


def exchange(v, axis, first, stride=1):
    n = lax.axis_size(axis)
    parts = [v]
    for step, radix in stages(n, first, stride):
        v = add_parts(parts)
        parts = [v] + [swap(v, axis, k * step) for k in range(1, radix)]
    return parts


def batch_parts(v, stride=1):
    steps = (lax.axis_size("batch") // stride).bit_length() - 1
    return exchange(v, "batch", 2 if steps % 2 else 4, stride)


def proto_parts(v, stride=1):
    return exchange(v, "proto", 2, stride)


def whole(shape):
    return pl.BlockSpec(shape, lambda *_: (0,) * len(shape))


def params(mib=24):
    return pltpu.CompilerParams(vmem_limit_bytes=mib * 1024 * 1024)


def cost(flops, nbytes, trans=0):
    return pl.CostEstimate(flops=int(flops), bytes_accessed=int(nbytes), transcendentals=int(trans))


def dot(a, b, dims, precision=None):
    return lax.dot_general(a, b, ((dims[0], dims[1]), ((), ())), precision=precision, preferred_element_type=F32)


def eye(n):
    return lax.broadcasted_iota(jnp.int32, (n, n), 0) == lax.broadcasted_iota(jnp.int32, (n, n), 1)


def to_lanes(col):
    n = col.shape[0]
    return jnp.sum(jnp.where(eye(n), col, 0.0), axis=0, keepdims=True)


def to_column(row):
    n = row.shape[1]
    return jnp.sum(jnp.where(eye(n), row, 0.0), axis=1, keepdims=True)


def first_kernel(f_hbm, w_hbm, pre_ref, again_ref, mom_ref, f_ref, w_ref, sems):
    depth, hidden = w_ref.shape
    n = sems.shape[0] - 1
    step = depth // n
    copies = [pltpu.make_async_copy(f_hbm, f_ref, sems.at[n])]
    for k in range(n):
        at = pl.ds(k * step, step)
        copies.append(pltpu.make_async_copy(w_hbm.at[at, :], w_ref.at[at, :], sems.at[k]))
    for copy in copies:
        copy.start()
    copies[0].wait()
    for k in range(n):
        copies[k + 1].wait()
        at = slice(k * step, (k + 1) * step)
        part = jnp.dot(f_ref[:, at], w_ref[at, :], preferred_element_type=F32)
        if k == 0:
            pre_ref[...] = part
        else:
            pre_ref[...] += part
    pre = pre_ref[...]
    again_ref[...] = pre
    mom_ref[:, 0:hidden] = jnp.sum(pre, axis=0, keepdims=True)
    mom_ref[:, hidden:] = jnp.sum(pre * pre, axis=0, keepdims=True)


def first_layer(features, w_first):
    rows, depth = features.shape
    hidden = w_first.shape[1]
    steps = 6 if depth % (6 * 128) == 0 else 1
    return pl.pallas_call(
        first_kernel,
        in_specs=[pl.BlockSpec(memory_space=pl.ANY)] * 2,
        out_shape=[jax.ShapeDtypeStruct((rows, hidden), F32)] * 2 + [jax.ShapeDtypeStruct((1, 2 * hidden), F32)],
        scratch_shapes=[
            pltpu.VMEM((rows, depth), BF16),
            pltpu.VMEM((depth, hidden), BF16),
            pltpu.SemaphoreType.DMA((steps + 1,)),
        ],
        compiler_params=params(60),
        cost_estimate=cost(2 * rows * depth * hidden, 2 * depth * hidden + 4 * rows * hidden),
        name="first_layer",
    )(features, w_first)


def batch_norm(pre, stats, gain, shift):
    normed = (pre - stats[0:1, :]) * stats[1:2, :]
    return normed, gain * normed + shift


def second_kernel(crops_all, n_parts, *refs):
    parts = refs[:n_parts]
    pre_ref, gain_ref, shift_ref, w_ref, emb_ref, stats_ref = refs[n_parts:]
    hidden = pre_ref.shape[1]
    moments = add_parts([p[...] for p in parts]) / crops_all
    mean = moments[:, 0:hidden]
    var = moments[:, hidden:] - mean * mean
    stats_ref[0:1, :] = mean
    stats_ref[1:2, :] = lax.rsqrt(var + 1e-05)
    _, shifted = batch_norm(pre_ref[...], stats_ref[...], gain_ref[...], shift_ref[...])
    low = jnp.maximum(shifted, 0.0).astype(BF16)
    emb_ref[...] = jnp.dot(low, w_ref[...], preferred_element_type=F32)


def second_layer(crops_all, parts, pre, gain, shift, w_second):
    rows, hidden = pre.shape
    width = w_second.shape[1]
    return pl.pallas_call(
        functools.partial(second_kernel, crops_all, len(parts)),
        out_shape=[jax.ShapeDtypeStruct((rows, width), F32), jax.ShapeDtypeStruct((2, hidden), F32)],
        compiler_params=params(),
        cost_estimate=cost(2 * rows * hidden * width, 4 * rows * hidden + 2 * hidden * width),
        name="second_layer",
    )(*parts, pre, gain, shift, w_second)


def unit_kernel(p_ref, u_ref):
    wide = p_ref[...].astype(F32)
    u_ref[...] = (wide * lax.rsqrt(jnp.sum(wide * wide, 1, keepdims=True) + 1e-06)).astype(BF16)


def unit_rows(prototypes):
    rows, width = prototypes.shape
    blk = min(1024, rows)
    return pl.pallas_call(
        unit_kernel,
        grid=(rows // blk,),
        in_specs=[pl.BlockSpec((blk, width), lambda j: (j, 0))],
        out_specs=pl.BlockSpec((blk, width), lambda j: (j, 0)),
        out_shape=jax.ShapeDtypeStruct((rows, width), BF16),
        compiler_params=params(),
        cost_estimate=cost(4 * rows * width, 4 * rows * width),
        name="unit_rows",
    )(prototypes)


def embed(raw):
    inv_norm = lax.rsqrt(jnp.sum(raw * raw, 1, keepdims=True) + 1e-06)
    return raw * inv_norm, inv_norm


def embed_kernel(*refs):
    refs[-1][...] = embed(add_parts([p[...] for p in refs[:-1]]))[0]


def embed_rows(parts):
    return pl.pallas_call(
        embed_kernel,
        out_shape=jax.ShapeDtypeStruct(parts[0].shape, F32),
        compiler_params=params(),
        cost_estimate=cost(8 * parts[0].size, 12 * parts[0].size),
        name="embed_rows",
    )(*parts)


def score_kernel(n, *refs):
    pieces, u_ref, codes, col_ref = refs[:n], refs[n], refs[n + 1 : 2 * n + 1], refs[2 * n + 1]
    units = u_ref[...]
    col = 0.0
    for piece, out in zip(pieces, codes):
        code = jnp.exp(dot(piece[...].astype(BF16), units, ((1,), (1,))) / balancing_epsilon)
        out[...] = code
        col = col + jnp.sum(code, axis=0, keepdims=True)
    col_ref[...] = col


def score(pieces, units):
    rows, width = pieces[0].shape
    protos, n = units.shape[0], len(pieces)
    blk = min(1024, protos)
    *codes, col = pl.pallas_call(
        functools.partial(score_kernel, n),
        grid=(protos // blk,),
        in_specs=[whole((rows, width))] * n + [pl.BlockSpec((blk, width), lambda j: (j, 0))],
        out_specs=[pl.BlockSpec((rows, blk), lambda j: (0, j))] * n + [pl.BlockSpec((1, blk), lambda j: (0, j))],
        out_shape=[jax.ShapeDtypeStruct((rows, protos), F32)] * n + [jax.ShapeDtypeStruct((1, protos), F32)],
        compiler_params=params(),
        cost_estimate=cost(2 * n * rows * protos * width, 4 * n * rows * protos, n * rows * protos),
        name="score",
    )(*pieces, units)
    return codes, col


def pack(table, lane_row, out_ref):
    rows, width = table.shape
    out_ref[0:rows, :] = table
    out_ref[rows:, :] = jnp.zeros((8, width), F32)
    out_ref[rows : rows + 1, 0:rows] = lane_row


def logit_kernel(emb_ref, u_ref, out_ref, total, mass):
    j = pl.program_id(0)

    @pl.when(j == 0)
    def _():
        total[...] = jnp.zeros_like(total)
        mass[...] = jnp.zeros_like(mass)

    units = u_ref[...]
    logits = jnp.exp(dot(emb_ref[...].astype(BF16), units, ((1,), (1,))) / sharpness_divisor)
    total[...] += jnp.dot(logits.astype(BF16), units, preferred_element_type=F32)
    mass[...] += jnp.sum(logits, axis=1, keepdims=True)

    @pl.when(j == pl.num_programs(0) - 1)
    def _():
        pack(total[...], to_lanes(mass[...]), out_ref)


def logit_sum(embedded, units):
    rows, width = embedded.shape
    protos = units.shape[0]
    blk = min(1024, protos)
    return pl.pallas_call(
        logit_kernel,
        grid=(protos // blk,),
        in_specs=[whole((rows, width)), pl.BlockSpec((blk, width), lambda j: (j, 0))],
        out_specs=whole((rows + 8, width)),
        out_shape=jax.ShapeDtypeStruct((rows + 8, width), F32),
        scratch_shapes=[pltpu.VMEM((rows, width), F32), pltpu.VMEM((rows, 1), F32)],
        compiler_params=params(),
        cost_estimate=cost(4 * rows * protos * width, 2 * protos * width, rows * protos),
        name="logit_sum",
    )(embedded, units)


def row_kernel(n_parts, *refs):
    parts, codes, out_ref = refs[:n_parts], refs[n_parts:-1], refs[-1]
    scale = 1.0 / add_parts([p[...] for p in parts])
    for k, code in enumerate(codes):
        out_ref[k : k + 1, :] = to_lanes(jnp.sum(code[...] * scale, axis=1, keepdims=True))


def row_pass(parts, codes):
    rows, protos = codes[0].shape
    n = len(codes)
    return pl.pallas_call(
        functools.partial(row_kernel, len(parts)),
        out_shape=jax.ShapeDtypeStruct((n, rows), F32),
        compiler_params=params(),
        cost_estimate=cost(2 * n * rows * protos, 4 * n * rows * protos),
        name="row_pass",
    )(*parts, *codes)


def col_kernel(n_parts, *refs):
    parts, codes, out_ref = refs[:n_parts], refs[n_parts:-1], refs[-1]
    scale = 1.0 / add_parts([p[...] for p in parts])
    total = 0.0
    for k, code in enumerate(codes):
        total = total + jnp.sum(code[...] * to_column(scale[k : k + 1, :]), axis=0, keepdims=True)
    out_ref[...] = total


def col_pass(parts, codes):
    rows, protos = codes[0].shape
    n = len(codes)
    return pl.pallas_call(
        functools.partial(col_kernel, len(parts)),
        out_shape=jax.ShapeDtypeStruct((1, protos), F32),
        compiler_params=params(),
        cost_estimate=cost(2 * n * rows * protos, 4 * n * rows * protos),
        name="col_pass",
    )(*parts, *codes)


def target_kernel(n_parts, halves, *refs):
    parts = refs[:n_parts]
    codes_ref, u_ref, partner_ref, core_ref = refs[n_parts : n_parts + 4]
    outs, table_all, mass_all = refs[n_parts + 4 : -2], refs[-2], refs[-1]
    rows = codes_ref.shape[0]
    scale = 1.0 / add_parts([p[...] for p in parts])
    weighted = codes_ref[...] * scale
    mass = jnp.sum(weighted, axis=1, keepdims=True)
    table = jnp.dot(weighted.astype(BF16), u_ref[...], preferred_element_type=F32)
    chosen = partner_ref[...] == lax.broadcasted_iota(jnp.int32, (rows, rows), 0)
    table_all[...] = dot(jnp.where(chosen, 1.0, 0.0).astype(F32), table, ((1,), (0,)), HIGHEST)
    mass_all[...] = jnp.sum(jnp.where(chosen, to_lanes(mass), 0.0), axis=1, keepdims=True)
    size = rows // halves
    for k in range(halves):
        at = pl.ds(pl.multiple_of((core_ref[2] ^ k) * size, size), size)
        pack(table_all[at, :], to_lanes(mass_all[at, :]), outs[k])


def target_sum(parts, codes, units, partner, core, halves):
    rows, protos = codes.shape
    width = units.shape[1]
    n_vmem = len(parts) + 3
    return pl.pallas_call(
        functools.partial(target_kernel, len(parts), halves),
        in_specs=[pl.BlockSpec(memory_space=pltpu.VMEM)] * n_vmem + [pl.BlockSpec(memory_space=pltpu.SMEM)],
        out_shape=[jax.ShapeDtypeStruct((rows // halves + 8, width), F32)] * halves,
        scratch_shapes=[pltpu.VMEM((rows, width), F32), pltpu.VMEM((rows, 1), F32)],
        compiler_params=params(),
        cost_estimate=cost(2 * rows * protos * width, 4 * rows * protos + 2 * protos * width),
        name="target_sum",
    )(*parts, codes, units, partner, core)


def loss_kernel(n_raw, n_logit, n_target, *refs):
    core_ref, refs = refs[0], refs[1:]
    raws, refs = refs[:n_raw], refs[n_raw:]
    logits, refs = refs[:n_logit], refs[n_logit:]
    target = add_parts([p[...] for p in refs[:n_target]])
    grad_ref, loss_ref = refs[n_target:]
    rows = raws[0].shape[0]
    size = grad_ref.shape[0]
    at = pl.ds(pl.multiple_of(core_ref[2] * size, size), size)
    raw = add_parts([p[at, :] for p in raws])
    logit = add_parts([p[at, :] for p in logits])
    denoms = to_column(add_parts([p[rows : rows + 1, 0:rows] for p in logits]))
    denom = jnp.where(core_ref[2] == 0, denoms[0:size], denoms[rows - size :])
    embedded, inv_norm = embed(raw)
    row_scale = to_column(1.0 / target[size : size + 1, 0:size])
    wanted = target[0:size, :] * row_scale
    emb_low = embedded.astype(BF16).astype(F32)
    cross = jnp.sum(wanted * emb_low, axis=1, keepdims=True)
    loss_ref[...] = to_lanes(jnp.log(denom) - cross / sharpness_divisor)
    emb_grad = penalty_weighting * (logit / denom - wanted) / sharpness_divisor
    inner = jnp.sum(embedded * emb_grad, 1, keepdims=True)
    grad_ref[...] = (emb_grad - embedded * inner) * inv_norm


def loss_grad(raw_parts, logit_parts, target_parts, core):
    width = raw_parts[0].shape[1]
    rows = target_parts[0].shape[0] - 8
    n_vmem = len(raw_parts) + len(logit_parts) + len(target_parts)
    return pl.pallas_call(
        functools.partial(loss_kernel, len(raw_parts), len(logit_parts), len(target_parts)),
        in_specs=[pl.BlockSpec(memory_space=pltpu.SMEM)] + [pl.BlockSpec(memory_space=pltpu.VMEM)] * n_vmem,
        out_shape=[jax.ShapeDtypeStruct((rows, width), F32), jax.ShapeDtypeStruct((1, rows), F32)],
        compiler_params=params(),
        cost_estimate=cost(20 * rows * width, 24 * rows * width),
        name="loss_grad",
    )(core, *raw_parts, *logit_parts, *target_parts)


def pick_kernel(f_ref, at_ref, keep_ref, send_ref):
    n_z, height, rows = keep_ref.shape
    depth = f_ref.shape[1]
    shape = (n_z * height, depth)
    row = lax.broadcasted_iota(jnp.int32, shape, 0)
    col = lax.broadcasted_iota(jnp.int32, shape, 1)
    d_cols = depth // (2 * n_z)
    me, share = at_ref[0], at_ref[1] * height
    for out, y in ((keep_ref, me & 1), (send_ref, (me & 1) ^ 1)):
        first = jnp.zeros(shape, jnp.int32)
        for k in range(n_z):
            owner = (((me >> 1) ^ k) << 1) + y
            first = jnp.where(row >= k * height, owner * d_cols + share - k * height, first)
        chosen = jnp.where(col == first + row, 1.0, 0.0).astype(BF16)
        out[...] = dot(chosen, f_ref[...], ((1,), (1,))).reshape(n_z, height, rows)


def columns_pick(features, at, n_batch, n_proto):
    rows, depth = features.shape
    shape = jax.ShapeDtypeStruct((n_batch // 2, depth // (n_batch * n_proto), rows), F32)
    return pl.pallas_call(
        pick_kernel,
        in_specs=[pl.BlockSpec(memory_space=pltpu.VMEM), pl.BlockSpec(memory_space=pltpu.SMEM)],
        out_shape=[shape, shape],
        compiler_params=params(),
        cost_estimate=cost(2 * depth * depth // n_proto * rows, 8 * rows * depth),
        name="columns_pick",
    )(features, at)


def columns_z(keep, got):
    both = [jnp.stack([keep[k], got[k]]) for k in range(keep.shape[0])]
    return [both[0]] + [swap(both[k], "batch", 2 * k) for k in range(1, len(both))]


def columns_kernel(masks, at_ref, *refs):
    out_ref = refs[-1]
    inner = len(masks) // (len(refs) - 1)
    for k, mask in enumerate(masks):
        _, n_batch, height, rows = refs[k // inner].shape
        row = pl.multiple_of((at_ref[1] ^ mask) * height, height)
        for i in range(n_batch):
            col = pl.multiple_of((at_ref[0] ^ i) * rows, rows)
            out_ref[pl.ds(row, height), pl.ds(col, rows)] = refs[k // inner][k % inner, i].astype(BF16)


def columns_all(own, other, at):
    n_proto = 2 * own.shape[0]
    _, n_batch, height, rows = own.shape
    smem = pl.BlockSpec(memory_space=pltpu.SMEM)
    vmem = pl.BlockSpec(memory_space=pltpu.VMEM)
    return pl.pallas_call(
        functools.partial(columns_kernel, (0, 2, 1, 3)),
        in_specs=[smem, vmem, vmem],
        out_shape=jax.ShapeDtypeStruct((n_proto * height, n_batch * rows), BF16),
        compiler_params=params(),
        cost_estimate=cost(0, 6 * n_proto * height * n_batch * rows),
        name="columns_all",
    )(at, own, other)


def cast_kernel(in_ref, out_ref):
    out_ref[...] = in_ref[...].T.astype(BF16)


def columns_cast(columns):
    return pl.pallas_call(
        cast_kernel,
        out_shape=jax.ShapeDtypeStruct(columns.shape[::-1], BF16),
        compiler_params=params(),
        name="columns_cast",
    )(columns)


def tail_kernel(crops_all, places, e_cols, *refs):
    n_grad = len(places)
    at_ref, pre_ref, cols_ref, stats_ref, gain_ref, shift_ref, w_ref = refs[:7]
    grads, refs = refs[7 : 7 + n_grad], refs[7 + n_grad :]
    w1_ref, w2_ref, gain_grad_ref, shift_grad_ref, grad_all, grad_cols = refs
    width = grad_all.shape[1]

    @pl.when(pl.program_id(0) == 0)
    def _():
        for piece, (masks, flip) in zip(grads, places):
            rows = piece.shape[1]
            for k, mask in enumerate(masks):
                place = 0 if mask is None else ((at_ref[0] ^ mask) << 1) + (at_ref[2] ^ flip)
                grad_all[pl.ds(pl.multiple_of(place * rows, rows), rows), :] = piece[k].astype(BF16)
        shape = (grad_cols.shape[0], width)
        mine = lax.broadcasted_iota(jnp.int32, shape, 0) + at_ref[0] * e_cols
        chosen = jnp.where(mine == lax.broadcasted_iota(jnp.int32, shape, 1), 1.0, 0.0).astype(BF16)
        grad_cols[...] = dot(chosen, grad_all[...], ((1,), (1,))).astype(BF16)

    stats, gain = stats_ref[...], gain_ref[...]
    normed, shifted = batch_norm(pre_ref[...], stats, gain, shift_ref[...])
    hidden = jnp.maximum(shifted, 0.0).astype(BF16)
    w2_ref[...] = jnp.dot(grad_cols[...], hidden, preferred_element_type=F32)[0:e_cols, :]
    hidden_grad = dot(grad_all[...], w_ref[...], ((1,), (1,)))
    bn_grad = jnp.where(shifted > 0, hidden_grad, 0.0)
    shift_grad = jnp.sum(bn_grad, axis=0, keepdims=True)
    gain_grad = jnp.sum(bn_grad * normed, axis=0, keepdims=True)
    shift_grad_ref[...] = shift_grad
    gain_grad_ref[...] = gain_grad
    scale = gain * stats[1:2, :]
    pre_grad = scale * (bn_grad - shift_grad / crops_all - normed * (gain_grad / crops_all))
    w1_ref[...] = jnp.dot(cols_ref[...], pre_grad.astype(BF16), preferred_element_type=F32)


def tail(pre_all, columns, stats, gain, shift, w_second, grads, places, at, e_cols):
    crops_all, hidden = pre_all.shape
    width, d_cols = w_second.shape[1], columns.shape[0]
    blk = min(hidden, max(128, 256 * 1024 // crops_all))
    smem = pl.BlockSpec(memory_space=pltpu.SMEM)
    vmem = pl.BlockSpec(memory_space=pltpu.VMEM)

    def cols(n):
        return pl.BlockSpec((n, blk), lambda j: (0, j))

    return pl.pallas_call(
        functools.partial(tail_kernel, crops_all, places, e_cols),
        grid=(hidden // blk,),
        in_specs=[smem, cols(crops_all), vmem, cols(2), cols(1), cols(1)]
        + [pl.BlockSpec((blk, width), lambda j: (j, 0))]
        + [vmem] * len(grads),
        out_specs=[cols(d_cols), cols(e_cols), cols(1), cols(1)],
        out_shape=[
            jax.ShapeDtypeStruct((d_cols, hidden), F32),
            jax.ShapeDtypeStruct((e_cols, hidden), F32),
            jax.ShapeDtypeStruct((1, hidden), F32),
            jax.ShapeDtypeStruct((1, hidden), F32),
        ],
        scratch_shapes=[
            pltpu.VMEM((crops_all, width), BF16),
            pltpu.VMEM((-(-e_cols // 16) * 16, crops_all), BF16),
        ],
        compiler_params=params(24 if crops_all <= 1024 else 56),
        cost_estimate=cost(2 * crops_all * hidden * (width + d_cols), 4 * crops_all * hidden),
        name="tail",
    )(at, pre_all, columns, stats, gain, shift, w_second, *grads)


def after(value, *others):
    return lax.optimization_barrier((value,) + others)[0]


def body(features, w_first, bn_gain, bn_shift, w_second, prototypes, partner):
    n_batch, n_proto = lax.axis_size("batch"), lax.axis_size("proto")
    me, proto_me = lax.axis_index("batch").astype(jnp.int32), lax.axis_index("proto").astype(jnp.int32)
    rows, depth = features.shape
    width = w_second.shape[1]
    crops_all = rows * n_batch
    d_cols, e_cols = depth // n_batch, width // n_batch
    gain, shift = bn_gain[None, :], bn_shift[None, :]
    short = n_batch == 8 and n_proto == 4 and depth % 512 == 0
    at = jnp.stack([me, proto_me, proto_me & 1 if short else proto_me * 0])

    pre, pre_again, moments = first_layer(features, w_first)
    pre_all = lax.all_gather(pre, "batch", tiled=True)
    moment_parts = batch_parts(moments)
    units = unit_rows(prototypes)
    if short:
        keep, send = columns_pick(after(features, moments), at, n_batch, n_proto)
        moment_parts[0], keep, send, units = lax.optimization_barrier((moment_parts[0], keep, send, units))
    emb_part, stats = second_layer(crops_all, moment_parts, pre_again, gain, shift, w_second)
    raw_parts = proto_parts(emb_part)
    embedded = embed_rows(raw_parts)

    if short:
        partner_emb = swap(embedded, "batch", 1)
        got = swap(after(send, embedded), "batch", 1)
        own_codes, own_col = score([embedded], units)
        partner_emb, own_col = lax.optimization_barrier((partner_emb, own_col))
        more_codes, more_col = score([partner_emb], units)
        codes, col_part = own_codes + more_codes, own_col + more_col
        got = after(got, col_part)
        z_stride = 2
    else:
        codes, col_part = score([embedded], units)
        z_stride = 1
    logit = logit_sum(after(embedded, col_part), units)
    col_parts = batch_parts(col_part, z_stride)
    if short:
        col_parts[0], got, logit = lax.optimization_barrier((col_parts[0], got, logit))
    for iteration in range(ITERS - 1):
        row_part = row_pass(col_parts, codes)
        row_parts = proto_parts(row_part)
        if short and iteration == 0:
            columns = columns_z(after(keep, row_parts[0]), after(got, row_parts[0]))
        col_part = col_pass(row_parts, codes)
        col_parts = batch_parts(col_part, z_stride)
        if iteration == 0:
            logit_parts = proto_parts(after(logit, col_part))
        if short and iteration == 0:
            col_parts[0], *rest = lax.optimization_barrier((col_parts[0], *columns, *logit_parts))
            columns, logit_parts = rest[: len(columns)], rest[len(columns) :]
    if short:
        keep, send = target_sum(col_parts, codes[0], units, partner[None, :], at, 2)
        target_parts = proto_parts(keep + swap(send, "proto", 1), 2)
    else:
        target_parts = proto_parts(target_sum(col_parts, codes[0], units, partner[None, :], at, 1)[0])
    raw_grad, penalty = loss_grad(raw_parts, logit_parts, target_parts, at)

    if short:
        pre_all, *columns = lax.optimization_barrier((pre_all, *columns, raw_grad))[:-1]
        near = jnp.stack([raw_grad] + [swap(raw_grad, "batch", k) for k in (2, 4, 6)])
        columns = jnp.concatenate(columns)[None]
        columns = jnp.concatenate([columns, swap(columns, "proto", 2)])
        columns = columns_all(columns, swap(columns, "proto", 1), at)
        far = swap(near, "batch", 1)
        grads = [near, far, swap(near, "proto", 1), swap(far, "proto", 1)]
        places = [((0, 2, 4, 6), 0), ((1, 3, 5, 7), 0), ((0, 2, 4, 6), 1), ((1, 3, 5, 7), 1)]
        other_penalty = swap(penalty, "proto", 1)
        first = at[2] == 0
        penalty = jnp.concatenate(
            [jnp.where(first, penalty, other_penalty), jnp.where(first, other_penalty, penalty)], axis=1
        )
    else:
        by_owner = jnp.swapaxes(features.astype(F32).reshape(rows, n_batch, d_cols), 0, 1)
        columns = columns_cast(lax.all_to_all(by_owner, "batch", 0, 0).reshape(crops_all, d_cols))
        grads = [lax.all_gather(raw_grad, "batch", tiled=True)[None]]
        places = [((None,), 0)]
    grad_w1, grad_w2, grad_gain, grad_shift = tail(
        pre_all, columns, stats, gain, shift, w_second, grads, places, at, e_cols
    )
    return (penalty[0], grad_w1, grad_gain[0], grad_shift[0], grad_w2.T)


def solution(mesh):
    return jax.shard_map(
        body,
        mesh=mesh,
        in_specs=(
            P("batch", None),
            P(None, "proto"),
            P("proto"),
            P("proto"),
            P("proto", None),
            P("proto", None),
            P("batch"),
        ),
        out_specs=(P("batch"), P("batch", "proto"), P("proto"), P("proto"), P("proto", "batch")),
        check_vma=False,
    )
```

```python
import functools

import jax
import jax.numpy as jnp
from jax import lax
from jax.experimental import pallas as pl
from jax.experimental.pallas import tpu as pltpu
from jax.sharding import PartitionSpec as P

ITERS = 3
F32 = jnp.float32
BF16 = jnp.bfloat16
HIGHEST = lax.Precision.HIGHEST

balancing_epsilon = 0.05
sharpness_divisor = 0.1
penalty_weighting = 64.0


def stages(n, first, stride=1):
    out, radix = [], first
    while stride < n:
        radix = min(radix, n // stride)
        out.append((stride, radix))
        stride *= radix
        radix = 4 if (n // stride) % 4 == 0 else 2
    return out


def swap(v, axis, mask):
    n = lax.axis_size(axis)
    return lax.ppermute(v, axis, [(i, i ^ mask) for i in range(n)])


def add_parts(parts):
    if len(parts) == 4:
        return (parts[0] + parts[1]) + (parts[2] + parts[3])
    return functools.reduce(lambda x, y: x + y, parts)


def exchange(v, axis, first, stride=1):
    n = lax.axis_size(axis)
    parts = [v]
    for step, radix in stages(n, first, stride):
        v = add_parts(parts)
        parts = [v] + [swap(v, axis, k * step) for k in range(1, radix)]
    return parts


def batch_parts(v, stride=1):
    steps = (lax.axis_size("batch") // stride).bit_length() - 1
    return exchange(v, "batch", 2 if steps % 2 else 4, stride)


def proto_parts(v, stride=1):
    return exchange(v, "proto", 2, stride)


def whole(shape):
    return pl.BlockSpec(shape, lambda *_: (0,) * len(shape))


def params(mib=24):
    return pltpu.CompilerParams(vmem_limit_bytes=mib * 1024 * 1024)


def cost(flops, nbytes, trans=0):
    return pl.CostEstimate(flops=int(flops), bytes_accessed=int(nbytes), transcendentals=int(trans))


def dot(a, b, dims, precision=None):
    return lax.dot_general(a, b, ((dims[0], dims[1]), ((), ())), precision=precision, preferred_element_type=F32)


def eye(n):
    return lax.broadcasted_iota(jnp.int32, (n, n), 0) == lax.broadcasted_iota(jnp.int32, (n, n), 1)


def to_lanes(col):
    n = col.shape[0]
    return jnp.sum(jnp.where(eye(n), col, 0.0), axis=0, keepdims=True)


def to_column(row):
    n = row.shape[1]
    return jnp.sum(jnp.where(eye(n), row, 0.0), axis=1, keepdims=True)


def first_kernel(f_hbm, w_hbm, pre_ref, again_ref, mom_ref, f_ref, w_ref, sems):
    depth, hidden = w_ref.shape
    n = sems.shape[0] - 1
    step = depth // n
    copies = [pltpu.make_async_copy(f_hbm, f_ref, sems.at[n])]
    for k in range(n):
        at = pl.ds(k * step, step)
        copies.append(pltpu.make_async_copy(w_hbm.at[at, :], w_ref.at[at, :], sems.at[k]))
    for copy in copies:
        copy.start()
    copies[0].wait()
    for k in range(n):
        copies[k + 1].wait()
        at = slice(k * step, (k + 1) * step)
        part = jnp.dot(f_ref[:, at], w_ref[at, :], preferred_element_type=F32)
        if k == 0:
            pre_ref[...] = part
        else:
            pre_ref[...] += part
    pre = pre_ref[...]
    again_ref[...] = pre
    first = jnp.sum(pre, axis=0, keepdims=True)
    second = jnp.sum(pre * pre, axis=0, keepdims=True)
    for k in range(mom_ref.shape[0]):
        mom_ref[k, :, 0:hidden] = first
        mom_ref[k, :, hidden:] = second


def first_layer(features, w_first, spread):
    rows, depth = features.shape
    hidden = w_first.shape[1]
    steps = 6 if depth % (6 * 128) == 0 else 1
    return pl.pallas_call(
        first_kernel,
        in_specs=[pl.BlockSpec(memory_space=pl.ANY)] * 2,
        out_shape=[jax.ShapeDtypeStruct((rows, hidden), F32)] * 2
        + [jax.ShapeDtypeStruct((spread, 1, 2 * hidden), F32)],
        scratch_shapes=[
            pltpu.VMEM((rows, depth), BF16),
            pltpu.VMEM((depth, hidden), BF16),
            pltpu.SemaphoreType.DMA((steps + 1,)),
        ],
        compiler_params=params(52),
        cost_estimate=cost(2 * rows * depth * hidden, 2 * depth * hidden + 4 * rows * hidden),
        name="first_layer",
    )(features, w_first)


def batch_norm(pre, stats, gain, shift):
    normed = (pre - stats[0:1, :]) * stats[1:2, :]
    return normed, gain * normed + shift


def second_kernel(crops_all, n_parts, *refs):
    parts = refs[:n_parts]
    pre_ref, gain_ref, shift_ref, w_ref, emb_ref, stats_ref = refs[n_parts:]
    hidden = pre_ref.shape[1]
    moments = add_parts([p[k] for p in parts for k in range(p.shape[0])]) / crops_all
    mean = moments[:, 0:hidden]
    var = moments[:, hidden:] - mean * mean
    stats_ref[0:1, :] = mean
    stats_ref[1:2, :] = lax.rsqrt(var + 1e-05)
    _, shifted = batch_norm(pre_ref[...], stats_ref[...], gain_ref[...], shift_ref[...])
    low = jnp.maximum(shifted, 0.0).astype(BF16)
    emb_ref[...] = jnp.dot(low, w_ref[...], preferred_element_type=F32)


def second_layer(crops_all, parts, pre, gain, shift, w_second):
    rows, hidden = pre.shape
    width = w_second.shape[1]
    return pl.pallas_call(
        functools.partial(second_kernel, crops_all, len(parts)),
        out_shape=[jax.ShapeDtypeStruct((rows, width), F32), jax.ShapeDtypeStruct((2, hidden), F32)],
        compiler_params=params(),
        cost_estimate=cost(2 * rows * hidden * width, 4 * rows * hidden + 2 * hidden * width),
        name="second_layer",
    )(*parts, pre, gain, shift, w_second)


def unit_kernel(p_ref, u_ref):
    wide = p_ref[...].astype(F32)
    u_ref[...] = (wide * lax.rsqrt(jnp.sum(wide * wide, 1, keepdims=True) + 1e-06)).astype(BF16)


def unit_rows(prototypes):
    rows, width = prototypes.shape
    blk = min(1024, rows)
    return pl.pallas_call(
        unit_kernel,
        grid=(rows // blk,),
        in_specs=[pl.BlockSpec((blk, width), lambda j: (j, 0))],
        out_specs=pl.BlockSpec((blk, width), lambda j: (j, 0)),
        out_shape=jax.ShapeDtypeStruct((rows, width), BF16),
        compiler_params=params(),
        cost_estimate=cost(4 * rows * width, 4 * rows * width),
        name="unit_rows",
    )(prototypes)


def embed(raw):
    inv_norm = lax.rsqrt(jnp.sum(raw * raw, 1, keepdims=True) + 1e-06)
    return raw * inv_norm, inv_norm


def embed_kernel(*refs):
    refs[-1][...] = embed(add_parts([p[...] for p in refs[:-1]]))[0]


def embed_rows(parts):
    return pl.pallas_call(
        embed_kernel,
        out_shape=jax.ShapeDtypeStruct(parts[0].shape, F32),
        compiler_params=params(),
        cost_estimate=cost(8 * parts[0].size, 12 * parts[0].size),
        name="embed_rows",
    )(*parts)


def put_blocks(out_ref, row, value):
    for k in range(value.shape[1] // 128):
        out_ref[row + k : row + k + 1, :] = value[:, k * 128 : (k + 1) * 128]


def score_kernel(n, *refs):
    piece, u_ref = refs[:2]
    code_ref, col_ref = refs[-2:] if n == 0 else refs[4:6]
    j = pl.program_id(0)
    code = jnp.exp(dot(piece[...].astype(BF16), u_ref[...], ((1,), (1,))) / balancing_epsilon)
    code_ref[...] = code
    put_blocks(col_ref, 0, jnp.sum(code, axis=0, keepdims=True))
    if n:
        col_ref[...] += refs[2][...]
        size = col_ref.shape[0]
        at = pl.ds(pl.multiple_of(j * size, size), size)
        for k, out in enumerate(refs[6:]):
            out[at, :] = col_ref[...]

            @pl.when(j == 0)
            def _():
                out[out.shape[0] - refs[3].shape[1] :, :] = refs[3][k + 1]


def score(piece, units, more=None):
    rows, width = piece.shape
    protos = units.shape[0]
    blk = min(1024, protos)
    lines, step = protos // 128, blk // 128
    by_step = pl.BlockSpec((step, 128), lambda j: (j, 0))
    in_specs = [whole((rows, width)), pl.BlockSpec((blk, width), lambda j: (j, 0))]
    out_specs = [pl.BlockSpec((rows, blk), lambda j: (0, j)), by_step]
    out_shape = [jax.ShapeDtypeStruct((rows, protos), F32), jax.ShapeDtypeStruct((lines, 128), F32)]
    n, extra = 0, ()
    if more is not None:
        n, extra = more[1].shape[0] - 1, more
        sent = (lines + more[1].shape[1], 128)
        in_specs += [by_step, whole(more[1].shape)]
        out_specs += [whole(sent)] * n
        out_shape += [jax.ShapeDtypeStruct(sent, F32)] * n
    return pl.pallas_call(
        functools.partial(score_kernel, n),
        grid=(protos // blk,),
        in_specs=in_specs,
        out_specs=out_specs,
        out_shape=out_shape,
        compiler_params=params(),
        cost_estimate=cost(2 * rows * protos * width, 4 * rows * protos, rows * protos),
        name="score",
    )(piece, units, *extra)


def col_scale(parts):
    lines = parts[0].shape[0]
    return 1.0 / add_parts([p[0:lines, :] for p in parts])


def pack(table, lane_row, out_ref):
    rows, width = table.shape
    out_ref[0:rows, :] = table
    out_ref[rows:, :] = jnp.zeros((8, width), F32)
    out_ref[rows : rows + 1, 0:rows] = lane_row


def logit_kernel(emb_ref, u_ref, out_ref, total, mass):
    j = pl.program_id(0)

    @pl.when(j == 0)
    def _():
        total[...] = jnp.zeros_like(total)
        mass[...] = jnp.zeros_like(mass)

    units = u_ref[...]
    logits = jnp.exp(dot(emb_ref[...].astype(BF16), units, ((1,), (1,))) / sharpness_divisor)
    total[...] += jnp.dot(logits.astype(BF16), units, preferred_element_type=F32)
    mass[...] += jnp.sum(logits, axis=1, keepdims=True)

    @pl.when(j == pl.num_programs(0) - 1)
    def _():
        pack(total[...], to_lanes(mass[...]), out_ref)


def logit_sum(embedded, units):
    rows, width = embedded.shape
    protos = units.shape[0]
    blk = min(1024, protos)
    return pl.pallas_call(
        logit_kernel,
        grid=(protos // blk,),
        in_specs=[whole((rows, width)), pl.BlockSpec((blk, width), lambda j: (j, 0))],
        out_specs=whole((rows + 8, width)),
        out_shape=jax.ShapeDtypeStruct((rows + 8, width), F32),
        scratch_shapes=[pltpu.VMEM((rows, width), F32), pltpu.VMEM((rows, 1), F32)],
        compiler_params=params(),
        cost_estimate=cost(4 * rows * protos * width, 2 * protos * width, rows * protos),
        name="logit_sum",
    )(embedded, units)


def row_kernel(n_parts, *refs):
    parts, codes, out_ref = refs[:n_parts], refs[n_parts:-1], refs[-1]
    scale = col_scale(parts)
    for k, code in enumerate(codes):
        total = 0.0
        for j in range(scale.shape[0]):
            total = total + code[:, j * 128 : (j + 1) * 128] * scale[j : j + 1, :]
        out_ref[k : k + 1, :] = to_lanes(jnp.sum(total, axis=1, keepdims=True))


def row_pass(parts, codes):
    rows, protos = codes[0].shape
    n = len(codes)
    return pl.pallas_call(
        functools.partial(row_kernel, len(parts)),
        out_shape=jax.ShapeDtypeStruct((n, rows), F32),
        compiler_params=params(),
        cost_estimate=cost(2 * n * rows * protos, 4 * n * rows * protos),
        name="row_pass",
    )(*parts, *codes)


def col_kernel(n_parts, n_codes, *refs):
    parts, codes, refs = refs[:n_parts], refs[n_parts : n_parts + n_codes], refs[n_parts + n_codes :]
    scale = 1.0 / add_parts([p[...] for p in parts])
    total = 0.0
    for k, code in enumerate(codes):
        total = total + jnp.sum(code[...] * to_column(scale[k : k + 1, :]), axis=0, keepdims=True)
    if len(refs) == 1:
        put_blocks(refs[0], 0, total)
    else:
        put_blocks(refs[1], 0, total)
        for k, out in enumerate(refs[2:]):
            out[0 : refs[1].shape[0], :] = refs[1][...]
            out[refs[1].shape[0] :, :] = refs[0][k + 1]


def col_pass(parts, codes, columns=None):
    rows, protos = codes[0].shape
    n = len(codes)
    lines = protos // 128
    extra = () if columns is None else (columns,)
    shapes = [(lines, 128)] + [(lines + c.shape[1], 128) for c in extra for _ in range(c.shape[0] - 1)]
    return pl.pallas_call(
        functools.partial(col_kernel, len(parts), n),
        out_shape=[jax.ShapeDtypeStruct(shape, F32) for shape in shapes],
        compiler_params=params(),
        cost_estimate=cost(2 * n * rows * protos, 4 * n * rows * protos),
        name="col_pass",
    )(*parts, *codes, *extra)


def target_kernel(n_parts, halves, *refs):
    parts = refs[:n_parts]
    codes_ref, u_ref, partner_ref, at_ref = refs[n_parts : n_parts + 4]
    outs, table_all, mass_all, low = refs[n_parts + 4 : -3], refs[-3], refs[-2], refs[-1]
    rows = codes_ref.shape[0]
    scale = col_scale(parts)
    total = 0.0
    for j in range(scale.shape[0]):
        weighted = codes_ref[:, j * 128 : (j + 1) * 128] * scale[j : j + 1, :]
        low[:, j * 128 : (j + 1) * 128] = weighted.astype(BF16)
        total = total + weighted
    mass = jnp.sum(total, axis=1, keepdims=True)
    table = jnp.dot(low[...], u_ref[...], preferred_element_type=F32)
    chosen = partner_ref[...] == lax.broadcasted_iota(jnp.int32, (rows, rows), 0)
    table_all[...] = dot(jnp.where(chosen, 1.0, 0.0).astype(F32), table, ((1,), (0,)), HIGHEST)
    mass_all[...] = jnp.sum(jnp.where(chosen, to_lanes(mass), 0.0), axis=1, keepdims=True)
    size = rows // halves
    for k in range(halves):
        at = pl.ds(pl.multiple_of((at_ref[2] ^ k) * size, size), size)
        pack(table_all[at, :], to_lanes(mass_all[at, :]), outs[k])


def target_sum(parts, codes, units, partner, at, halves):
    rows, protos = codes.shape
    width = units.shape[1]
    n_vmem = len(parts) + 3
    return pl.pallas_call(
        functools.partial(target_kernel, len(parts), halves),
        in_specs=[pl.BlockSpec(memory_space=pltpu.VMEM)] * n_vmem + [pl.BlockSpec(memory_space=pltpu.SMEM)],
        out_shape=[jax.ShapeDtypeStruct((rows // halves + 8, width), F32)] * halves,
        scratch_shapes=[
            pltpu.VMEM((rows, width), F32),
            pltpu.VMEM((rows, 1), F32),
            pltpu.VMEM((rows, protos), BF16),
        ],
        compiler_params=params(),
        cost_estimate=cost(2 * rows * protos * width, 4 * rows * protos + 2 * protos * width),
        name="target_sum",
    )(*parts, codes, units, partner, at)


def loss_kernel(n_raw, n_logit, n_target, *refs):
    core_ref, refs = refs[0], refs[1:]
    raws, refs = refs[:n_raw], refs[n_raw:]
    logits, refs = refs[:n_logit], refs[n_logit:]
    target = add_parts([p[...] for p in refs[:n_target]])
    grad_ref, loss_ref = refs[n_target:]
    rows = raws[0].shape[0]
    size = grad_ref.shape[0]
    at = pl.ds(pl.multiple_of(core_ref[2] * size, size), size)
    raw = add_parts([p[at, :] for p in raws])
    logit = add_parts([p[at, :] for p in logits])
    denoms = to_column(add_parts([p[rows : rows + 1, 0:rows] for p in logits]))
    denom = jnp.where(core_ref[2] == 0, denoms[0:size], denoms[rows - size :])
    embedded, inv_norm = embed(raw)
    row_scale = to_column(1.0 / target[size : size + 1, 0:size])
    wanted = target[0:size, :] * row_scale
    emb_low = embedded.astype(BF16).astype(F32)
    cross = jnp.sum(wanted * emb_low, axis=1, keepdims=True)
    loss_ref[...] = to_lanes(jnp.log(denom) - cross / sharpness_divisor)
    emb_grad = penalty_weighting * (logit / denom - wanted) / sharpness_divisor
    inner = jnp.sum(embedded * emb_grad, 1, keepdims=True)
    grad_ref[...] = (emb_grad - embedded * inner) * inv_norm


def loss_grad(raw_parts, logit_parts, target_parts, core):
    width = raw_parts[0].shape[1]
    rows = target_parts[0].shape[0] - 8
    n_vmem = len(raw_parts) + len(logit_parts) + len(target_parts)
    return pl.pallas_call(
        functools.partial(loss_kernel, len(raw_parts), len(logit_parts), len(target_parts)),
        in_specs=[pl.BlockSpec(memory_space=pltpu.SMEM)] + [pl.BlockSpec(memory_space=pltpu.VMEM)] * n_vmem,
        out_shape=[jax.ShapeDtypeStruct((rows, width), F32), jax.ShapeDtypeStruct((1, rows), F32)],
        compiler_params=params(),
        cost_estimate=cost(20 * rows * width, 24 * rows * width),
        name="loss_grad",
    )(core, *raw_parts, *logit_parts, *target_parts)


def pick_kernel(f_ref, at_ref, keep_ref, send_ref):
    n_z, height, rows = keep_ref.shape
    depth = f_ref.shape[1]
    shape = (n_z * height, depth)
    row = lax.broadcasted_iota(jnp.int32, shape, 0)
    col = lax.broadcasted_iota(jnp.int32, shape, 1)
    d_cols = depth // (2 * n_z)
    me, share = at_ref[0], at_ref[1] * height
    for out, y in ((keep_ref, me & 1), (send_ref, (me & 1) ^ 1)):
        first = jnp.zeros(shape, jnp.int32)
        for k in range(n_z):
            owner = (((me >> 1) ^ k) << 1) + y
            first = jnp.where(row >= k * height, owner * d_cols + share - k * height, first)
        chosen = jnp.where(col == first + row, 1.0, 0.0).astype(BF16)
        out[...] = dot(chosen, f_ref[...], ((1,), (1,))).reshape(n_z, height, rows)


def columns_pick(features, at, n_batch, n_proto):
    rows, depth = features.shape
    shape = jax.ShapeDtypeStruct((n_batch // 2, depth // (n_batch * n_proto), rows), F32)
    return pl.pallas_call(
        pick_kernel,
        in_specs=[pl.BlockSpec(memory_space=pltpu.VMEM), pl.BlockSpec(memory_space=pltpu.SMEM)],
        out_shape=[shape, shape],
        compiler_params=params(),
        cost_estimate=cost(2 * depth * depth // n_proto * rows, 8 * rows * depth),
        name="columns_pick",
    )(features, at)


def join_kernel(n_z, keep_ref, got_ref, *refs):
    out_ref, height = refs[-1], keep_ref.shape[1]
    out_ref[0, 0] = keep_ref[0]
    out_ref[0, 1] = got_ref[0]
    for k in range(2 * n_z - 2):
        out_ref[0, 2 + k] = refs[k][refs[k].shape[0] - height :, :]


def columns_join(keep, got, first, second):
    n_z, height, rows = keep.shape
    return pl.pallas_call(
        functools.partial(join_kernel, n_z),
        out_shape=jax.ShapeDtypeStruct((1, 2 * n_z, height, rows), F32),
        compiler_params=params(),
        cost_estimate=cost(0, 16 * n_z * height * rows),
        name="columns_join",
    )(keep, got, *[m for pair in zip(first, second) for m in pair])


def columns_kernel(masks, at_ref, *refs):
    out_ref = refs[-1]
    inner = len(masks) // (len(refs) - 1)
    for k, mask in enumerate(masks):
        _, n_batch, height, rows = refs[k // inner].shape
        row = pl.multiple_of((at_ref[1] ^ mask) * height, height)
        for i in range(n_batch):
            out_ref[at_ref[0] ^ i, pl.ds(row, height), :] = refs[k // inner][k % inner, i].astype(BF16)


def columns_all(own, other, at):
    n_proto = 2 * own.shape[0]
    _, n_batch, height, rows = own.shape
    smem = pl.BlockSpec(memory_space=pltpu.SMEM)
    vmem = pl.BlockSpec(memory_space=pltpu.VMEM)
    return pl.pallas_call(
        functools.partial(columns_kernel, (0, 2, 1, 3)),
        in_specs=[smem, vmem, vmem],
        out_shape=jax.ShapeDtypeStruct((n_batch, n_proto * height, rows), BF16),
        compiler_params=params(),
        cost_estimate=cost(0, 6 * n_proto * height * n_batch * rows),
        name="columns_all",
    )(at, own, other)


def cast_kernel(in_ref, out_ref):
    out_ref[...] = in_ref[...].T.astype(BF16)


def columns_cast(columns):
    return pl.pallas_call(
        cast_kernel,
        out_shape=jax.ShapeDtypeStruct(columns.shape[::-1], BF16),
        compiler_params=params(),
        name="columns_cast",
    )(columns)


def tail_step(refs, w1_ref, w2_ref, sums_ref, grad_all):
    at_ref, pre_ref, cols_ref, stats, gain, shift, w_ref, grads, masks = refs
    k = pl.program_id(0)
    block = at_ref[0] ^ (2 * k + masks[0])
    size = pre_ref.shape[1] // 2
    for flip, piece in enumerate(grads):
        place = pl.multiple_of((at_ref[2] ^ flip) * size, size)
        grad_all[pl.ds(place, size), :] = piece[k]
    grad = grad_all[...].astype(BF16)
    e_rows = w2_ref.shape[0]
    shape = (e_rows, grad.shape[1])
    mine = lax.broadcasted_iota(jnp.int32, shape, 0) + at_ref[0] * (grad.shape[1] // masks[1])
    chosen = jnp.where(mine == lax.broadcasted_iota(jnp.int32, shape, 1), 1.0, 0.0).astype(BF16)
    picked = dot(chosen, grad, ((1,), (1,))).astype(BF16)
    normed, shifted = batch_norm(pre_ref[block], stats, gain, shift)
    hidden_grad = dot(grad, w_ref[...], ((1,), (1,)))
    bn_grad = jnp.where(shifted > 0, hidden_grad, 0.0)
    sums_ref[0, pl.ds(block, 1), :] = jnp.sum(bn_grad, axis=0, keepdims=True)
    sums_ref[1, pl.ds(block, 1), :] = jnp.sum(bn_grad * normed, axis=0, keepdims=True)
    hidden = jnp.maximum(shifted, 0.0).astype(BF16)
    w2_ref[...] += jnp.dot(picked, hidden, preferred_element_type=F32)
    w1_ref[...] += jnp.dot(cols_ref[block], bn_grad.astype(BF16), preferred_element_type=F32)


def near_kernel(masks, *refs):
    at_ref, pre_ref, cols_ref, stats_ref, gain_ref, shift_ref, w_ref = refs[:7]
    grads, (w1_ref, w2_ref, sums_ref, grad_all) = refs[7:9], refs[9:]

    @pl.when(pl.program_id(0) == 0)
    def _():
        w1_ref[...] = jnp.zeros_like(w1_ref)
        w2_ref[...] = jnp.zeros_like(w2_ref)
        sums_ref[...] = jnp.zeros_like(sums_ref)

    ins = (at_ref, pre_ref, cols_ref, stats_ref[...], gain_ref[...], shift_ref[...], w_ref, grads, masks)
    tail_step(ins, w1_ref, w2_ref, sums_ref, grad_all)


def far_kernel(crops_all, e_cols, masks, *refs):
    at_ref, pre_ref, cols_ref, stats_ref, gain_ref, shift_ref, w_ref = refs[:7]
    grads, (near_w1, near_w2, near_sums, flat_ref, total_ref) = refs[7:9], refs[9:14]
    w1_ref, w2_ref, gain_grad_ref, shift_grad_ref, grad_all, sums, w2_all = refs[14:]

    @pl.when(pl.program_id(0) == 0)
    def _():
        w1_ref[...] = near_w1[...]
        w2_all[...] = near_w2[...]
        sums[...] = near_sums[...]

    stats, gain = stats_ref[...], gain_ref[...]
    ins = (at_ref, pre_ref, cols_ref, stats, gain, shift_ref[...], w_ref, grads, masks)
    tail_step(ins, w1_ref, w2_all, sums, grad_all)

    @pl.when(pl.program_id(0) == pl.num_programs(0) - 1)
    def _():
        w2_ref[...] = w2_all[0:e_cols, :]
        shift_grad = jnp.sum(sums[0], axis=0, keepdims=True)
        gain_grad = jnp.sum(sums[1], axis=0, keepdims=True)
        shift_grad_ref[...] = shift_grad
        gain_grad_ref[...] = gain_grad
        flat = total_ref[...] * (shift_grad / crops_all) + flat_ref[...] * (gain_grad / crops_all)
        w1_ref[...] = gain * stats[1:2, :] * (w1_ref[...] - flat)


def tail_call(kernel, odd, outs, scratch, at, pre_all, columns, stats, gain, shift, w_second, grads, more, name):
    n_batch, unit, hidden = pre_all.shape
    width = w_second.shape[1]
    crops = n_batch * unit // 2
    return pl.pallas_call(
        functools.partial(kernel, (odd, n_batch)),
        grid_spec=pltpu.PrefetchScalarGridSpec(
            num_scalar_prefetch=1,
            grid=(n_batch // 2,),
            in_specs=[pl.BlockSpec(memory_space=pltpu.VMEM)] * (6 + len(grads) + len(more)),
            out_specs=[whole(n) for n in outs],
            scratch_shapes=[pltpu.VMEM((unit, width), F32)] + [pltpu.VMEM(n, F32) for n in scratch],
        ),
        out_shape=[jax.ShapeDtypeStruct(n, F32) for n in outs],
        compiler_params=params(20),
        cost_estimate=cost(2 * crops * hidden * (width + 256), 4 * crops * hidden),
        name=name,
    )(at, pre_all, columns, stats, gain, shift, w_second, *grads, *more)


def flat_kernel(pre_hbm, cols_ref, stats_ref, gain_ref, shift_ref, pre_ref, flat_ref, total_ref, sems):
    n_batch = pre_ref.shape[0]
    copies = [pltpu.make_async_copy(pre_hbm.at[k], pre_ref.at[k], sems.at[k]) for k in range(n_batch)]
    for copy in copies:
        copy.start()
    stats, gain, shift = stats_ref[...], gain_ref[...], shift_ref[...]
    total = 0.0
    for k in range(n_batch):
        total = total + jnp.sum(cols_ref[k].astype(F32), axis=1, keepdims=True)
        copies[k].wait()
        normed, _ = batch_norm(pre_ref[k], stats, gain, shift)
        part = jnp.dot(cols_ref[k], normed.astype(BF16), preferred_element_type=F32)
        if k == 0:
            flat_ref[...] = part
        else:
            flat_ref[...] += part
    total_ref[...] = total


def flat_sums(pre_all, columns, stats, gain, shift):
    n_batch, unit, hidden = pre_all.shape
    d_cols = columns.shape[1]
    vmem = pl.BlockSpec(memory_space=pltpu.VMEM)
    return pl.pallas_call(
        flat_kernel,
        in_specs=[pl.BlockSpec(memory_space=pltpu.HBM)] + [vmem] * 4,
        out_specs=[vmem] * 3,
        out_shape=[
            jax.ShapeDtypeStruct((n_batch, unit, hidden), F32),
            jax.ShapeDtypeStruct((d_cols, hidden), F32),
            jax.ShapeDtypeStruct((d_cols, 1), F32),
        ],
        scratch_shapes=[pltpu.SemaphoreType.DMA((n_batch,))],
        compiler_params=params(20),
        cost_estimate=cost(2 * n_batch * unit * hidden * d_cols, 4 * n_batch * unit * hidden),
        name="flat_sums",
    )(pre_all, columns, stats, gain, shift)


def whole_tail_kernel(crops_all, e_cols, *refs):
    at_ref, pre_ref, cols_ref, stats_ref, gain_ref, shift_ref, w_ref, raw_ref = refs[:8]
    w1_ref, w2_ref, gain_grad_ref, shift_grad_ref, grad_all, grad_cols = refs[8:]

    @pl.when(pl.program_id(0) == 0)
    def _():
        grad_all[...] = raw_ref[...].astype(BF16)
        shape = (grad_cols.shape[0], grad_all.shape[1])
        mine = lax.broadcasted_iota(jnp.int32, shape, 0) + at_ref[0] * e_cols
        chosen = jnp.where(mine == lax.broadcasted_iota(jnp.int32, shape, 1), 1.0, 0.0).astype(BF16)
        grad_cols[...] = dot(chosen, grad_all[...], ((1,), (1,))).astype(BF16)

    stats, gain = stats_ref[...], gain_ref[...]
    normed, shifted = batch_norm(pre_ref[...], stats, gain, shift_ref[...])
    hidden = jnp.maximum(shifted, 0.0).astype(BF16)
    w2_ref[...] = jnp.dot(grad_cols[...], hidden, preferred_element_type=F32)[0:e_cols, :]
    hidden_grad = dot(grad_all[...], w_ref[...], ((1,), (1,)))
    bn_grad = jnp.where(shifted > 0, hidden_grad, 0.0)
    shift_grad = jnp.sum(bn_grad, axis=0, keepdims=True)
    gain_grad = jnp.sum(bn_grad * normed, axis=0, keepdims=True)
    shift_grad_ref[...] = shift_grad
    gain_grad_ref[...] = gain_grad
    scale = gain * stats[1:2, :]
    pre_grad = scale * (bn_grad - shift_grad / crops_all - normed * (gain_grad / crops_all))
    w1_ref[...] = jnp.dot(cols_ref[...], pre_grad.astype(BF16), preferred_element_type=F32)


def whole_tail(pre_all, columns, stats, gain, shift, w_second, raw, at, e_cols):
    crops_all, hidden = pre_all.shape
    width, d_cols = w_second.shape[1], columns.shape[0]
    blk = min(hidden, max(128, 256 * 1024 // crops_all))
    smem = pl.BlockSpec(memory_space=pltpu.SMEM)
    vmem = pl.BlockSpec(memory_space=pltpu.VMEM)

    def cols(n):
        return pl.BlockSpec((n, blk), lambda j: (0, j))

    return pl.pallas_call(
        functools.partial(whole_tail_kernel, crops_all, e_cols),
        grid=(hidden // blk,),
        in_specs=[smem, cols(crops_all), vmem, cols(2), cols(1), cols(1)]
        + [pl.BlockSpec((blk, width), lambda j: (j, 0)), vmem],
        out_specs=[cols(d_cols), cols(e_cols), cols(1), cols(1)],
        out_shape=[jax.ShapeDtypeStruct((n, hidden), F32) for n in (d_cols, e_cols, 1, 1)],
        scratch_shapes=[
            pltpu.VMEM((crops_all, width), BF16),
            pltpu.VMEM((-(-e_cols // 16) * 16, crops_all), BF16),
        ],
        compiler_params=params(58),
        cost_estimate=cost(2 * crops_all * hidden * (width + d_cols), 4 * crops_all * hidden),
        name="whole_tail",
    )(at, pre_all, columns, stats, gain, shift, w_second, raw)


def after(value, *others):
    return lax.optimization_barrier((value,) + others)[0]


def body(features, w_first, bn_gain, bn_shift, w_second, prototypes, partner):
    n_batch, n_proto = lax.axis_size("batch"), lax.axis_size("proto")
    me, proto_me = lax.axis_index("batch").astype(jnp.int32), lax.axis_index("proto").astype(jnp.int32)
    rows, depth = features.shape
    width = w_second.shape[1]
    crops_all = rows * n_batch
    d_cols, e_cols = depth // n_batch, width // n_batch
    gain, shift = bn_gain[None, :], bn_shift[None, :]
    short = n_batch == 8 and n_proto == 4 and depth % 512 == 0
    at = jnp.stack([me, proto_me, proto_me & 1 if short else proto_me * 0])

    pre, pre_again, moments = first_layer(features, w_first, n_batch if short else 1)
    pre_all = lax.all_gather(pre, "batch", tiled=True)
    moment_parts = [lax.all_to_all(moments, "batch", 0, 0)] if short else batch_parts(moments)
    units = unit_rows(prototypes)
    emb_part, stats = second_layer(crops_all, moment_parts, pre_again, gain, shift, w_second)
    raw_parts = proto_parts(emb_part)
    if short:
        keep, send = columns_pick(after(features, emb_part), at, n_batch, n_proto)
        raw_parts[0], keep, send, units = lax.optimization_barrier((raw_parts[0], keep, send, units))
    embedded = embed_rows(raw_parts)

    if short:
        partner_emb = swap(embedded, "batch", 1)
        own_codes, own_col = score(embedded, units)
        logit = logit_sum(embedded, units)
        partner_emb, own_col, logit = lax.optimization_barrier((partner_emb, own_col, logit))
        more_codes, *cols = score(partner_emb, units, (own_col, keep))
        codes = [own_codes, more_codes]
    else:
        codes, *cols = score(embedded, units)
        codes = [codes]
        logit = logit_sum(embedded, units)
    moved = []
    for iteration in range(ITERS):
        if short and iteration < 2:
            moved.append([swap(c, "batch", 2 * k + 2) for k, c in enumerate(cols[1:])])
            col_parts = [cols[0]] + moved[-1]
        else:
            col_parts = batch_parts(cols[0], 2 if short else 1)
        if iteration == 0:
            logit = logit + swap(after(logit, cols[0]), "proto", 1)
            col_parts[0], logit = lax.optimization_barrier((col_parts[0], logit))
            if short:
                got = swap(after(send, cols[0]), "batch", 1)
                col_parts[0], got = lax.optimization_barrier((col_parts[0], got))
        if iteration == 1:
            logit_parts = proto_parts(after(logit, cols[0]), 2)
            col_parts[0], *logit_parts = lax.optimization_barrier((col_parts[0], *logit_parts))
        if short and iteration == 2:
            columns = columns_join(after(keep, cols[0]), got, *moved)
            columns = [columns, swap(columns, "proto", 2)]
            col_parts[0], *columns = lax.optimization_barrier((col_parts[0], *columns))
        if iteration < ITERS - 1:
            row_parts = proto_parts(row_pass(col_parts, codes))
            cols = col_pass(row_parts, codes, got if short and iteration == 0 else None)
    if short:
        mine, send = target_sum(col_parts, codes[0], units, partner[None, :], at, 2)
        target_parts = proto_parts(mine + swap(send, "proto", 1), 2)
    else:
        target_parts = proto_parts(target_sum(col_parts, codes[0], units, partner[None, :], at, 1)[0])
    raw_grad, penalty = loss_grad(raw_parts, logit_parts, target_parts, at)

    if short:
        columns = after(jnp.concatenate(columns), raw_grad)
        columns = columns_all(columns, swap(columns, "proto", 1), at)
        pre_all = after(pre_all, raw_grad)
        near = jnp.stack([raw_grad] + [swap(raw_grad, "batch", k) for k in (2, 4, 6)])
        other_penalty = swap(penalty, "proto", 1)
        first = at[2] == 0
        penalty = jnp.concatenate(
            [jnp.where(first, penalty, other_penalty), jnp.where(first, other_penalty, penalty)], axis=1
        )
        ins = (at, pre_all.reshape(n_batch, rows, -1), columns, stats, gain, shift, w_second)
        e_rows, hidden = -(-e_cols // 16) * 16, w_second.shape[0]
        table = (2, n_batch, hidden)
        pre_near, *flat = flat_sums(*ins[1:-1])
        ins = (at, pre_near) + ins[2:]
        far = swap(near, "batch", 1)
        half = tail_call(
            near_kernel, 0, [(d_cols, hidden), (e_rows, hidden), table], [], *ins, [near, swap(near, "proto", 1)], [], "tail_near"
        )
        far, penalty, *half = lax.optimization_barrier((far, penalty, *half, *flat))
        grad_w1, grad_w2, grad_gain, grad_shift = tail_call(
            functools.partial(far_kernel, crops_all, e_cols), 1,
            [(d_cols, hidden), (e_cols, hidden), (1, hidden), (1, hidden)], [table, (e_rows, hidden)],
            *ins, [far, swap(far, "proto", 1)], half, "tail_far",
        )
    else:
        by_owner = jnp.swapaxes(features.astype(F32).reshape(rows, n_batch, d_cols), 0, 1)
        columns = columns_cast(lax.all_to_all(by_owner, "batch", 0, 0).reshape(crops_all, d_cols))
        raw_all = lax.all_gather(raw_grad, "batch", tiled=True)
        grad_w1, grad_w2, grad_gain, grad_shift = whole_tail(
            pre_all, columns, stats, gain, shift, w_second, raw_all, at, e_cols
        )
    return (penalty[0], grad_w1, grad_gain[0], grad_shift[0], grad_w2.T)


def solution(mesh):
    return jax.shard_map(
        body,
        mesh=mesh,
        in_specs=(
            P("batch", None),
            P(None, "proto"),
            P("proto"),
            P("proto"),
            P("proto", None),
            P("proto", None),
            P("batch"),
        ),
        out_specs=(P("batch"), P("batch", "proto"), P("proto"), P("proto"), P("proto", "batch")),
        check_vma=False,
    )
```

```python
import functools

import jax
import jax.numpy as jnp
from jax import lax
from jax.experimental import pallas as pl
from jax.experimental.pallas import tpu as pltpu
from jax.sharding import PartitionSpec as P

ITERS = 3
F32 = jnp.float32
BF16 = jnp.bfloat16
HIGHEST = lax.Precision.HIGHEST

balancing_epsilon = 0.05
sharpness_divisor = 0.1
penalty_weighting = 64.0


def stages(n, first, stride=1):
    out, radix = [], first
    while stride < n:
        radix = min(radix, n // stride)
        out.append((stride, radix))
        stride *= radix
        radix = 4 if (n // stride) % 4 == 0 else 2
    return out


def swap(v, axis, mask):
    n = lax.axis_size(axis)
    return lax.ppermute(v, axis, [(i, i ^ mask) for i in range(n)])


def add_parts(parts):
    if len(parts) == 4:
        return (parts[0] + parts[1]) + (parts[2] + parts[3])
    return functools.reduce(lambda x, y: x + y, parts)


def exchange(v, axis, first, stride=1):
    n = lax.axis_size(axis)
    parts = [v]
    for step, radix in stages(n, first, stride):
        v = add_parts(parts)
        parts = [v] + [swap(v, axis, k * step) for k in range(1, radix)]
    return parts


def batch_parts(v, stride=1):
    steps = (lax.axis_size("batch") // stride).bit_length() - 1
    return exchange(v, "batch", 2 if steps % 2 else 4, stride)


def proto_parts(v, stride=1):
    return exchange(v, "proto", 2, stride)


def proto_small(v):
    return exchange(v, "proto", 4 if lax.axis_size("proto") == 4 else 2)


def whole(shape):
    return pl.BlockSpec(shape, lambda *_: (0,) * len(shape))


def params(mib=24):
    return pltpu.CompilerParams(vmem_limit_bytes=mib * 1024 * 1024)


def cost(flops, nbytes, trans=0):
    return pl.CostEstimate(flops=int(flops), bytes_accessed=int(nbytes), transcendentals=int(trans))


def dot(a, b, dims, precision=None):
    return lax.dot_general(a, b, ((dims[0], dims[1]), ((), ())), precision=precision, preferred_element_type=F32)


def eye(n):
    return lax.broadcasted_iota(jnp.int32, (n, n), 0) == lax.broadcasted_iota(jnp.int32, (n, n), 1)


def to_lanes(col):
    n = col.shape[0]
    return jnp.sum(jnp.where(eye(n), col, 0.0), axis=0, keepdims=True)


def to_column(row):
    n = row.shape[1]
    return jnp.sum(jnp.where(eye(n), row, 0.0), axis=1, keepdims=True)


def first_kernel(f_hbm, w_hbm, pre_ref, again_ref, mom_ref, f_ref, w_ref, sems):
    depth, hidden = w_ref.shape
    n = sems.shape[0] - 1
    step = depth // n
    copies = [pltpu.make_async_copy(f_hbm, f_ref, sems.at[n])]
    for k in range(n):
        at = pl.ds(k * step, step)
        copies.append(pltpu.make_async_copy(w_hbm.at[at, :], w_ref.at[at, :], sems.at[k]))
    for copy in copies:
        copy.start()
    copies[0].wait()
    for k in range(n):
        copies[k + 1].wait()
        at = slice(k * step, (k + 1) * step)
        part = jnp.dot(f_ref[:, at], w_ref[at, :], preferred_element_type=F32)
        if k == 0:
            pre_ref[...] = part
        else:
            pre_ref[...] += part
    pre = pre_ref[...]
    again_ref[...] = pre
    first = jnp.sum(pre, axis=0, keepdims=True)
    second = jnp.sum(pre * pre, axis=0, keepdims=True)
    for k in range(mom_ref.shape[0]):
        mom_ref[k, :, 0:hidden] = first
        mom_ref[k, :, hidden:] = second


def first_layer(features, w_first, spread):
    rows, depth = features.shape
    hidden = w_first.shape[1]
    steps = 6 if depth % (6 * 128) == 0 else 1
    return pl.pallas_call(
        first_kernel,
        in_specs=[pl.BlockSpec(memory_space=pl.ANY)] * 2,
        out_shape=[jax.ShapeDtypeStruct((rows, hidden), F32)] * 2
        + [jax.ShapeDtypeStruct((spread, 1, 2 * hidden), F32)],
        scratch_shapes=[
            pltpu.VMEM((rows, depth), BF16),
            pltpu.VMEM((depth, hidden), BF16),
            pltpu.SemaphoreType.DMA((steps + 1,)),
        ],
        compiler_params=params(52),
        cost_estimate=cost(2 * rows * depth * hidden, 2 * depth * hidden + 4 * rows * hidden),
        name="first_layer",
    )(features, w_first)


def batch_norm(pre, stats, gain, shift):
    normed = (pre - stats[0:1, :]) * stats[1:2, :]
    return normed, gain * normed + shift


def second_kernel(crops_all, n_parts, *refs):
    parts = refs[:n_parts]
    pre_ref, gain_ref, shift_ref, w_ref, emb_ref, stats_ref = refs[n_parts:]
    hidden = pre_ref.shape[1]
    moments = add_parts([p[k] for p in parts for k in range(p.shape[0])]) / crops_all
    mean = moments[:, 0:hidden]
    var = moments[:, hidden:] - mean * mean
    stats_ref[0:1, :] = mean
    stats_ref[1:2, :] = lax.rsqrt(var + 1e-05)
    _, shifted = batch_norm(pre_ref[...], stats_ref[...], gain_ref[...], shift_ref[...])
    low = jnp.maximum(shifted, 0.0).astype(BF16)
    emb_ref[...] = jnp.dot(low, w_ref[...], preferred_element_type=F32)


def second_layer(crops_all, parts, pre, gain, shift, w_second):
    rows, hidden = pre.shape
    width = w_second.shape[1]
    return pl.pallas_call(
        functools.partial(second_kernel, crops_all, len(parts)),
        out_shape=[jax.ShapeDtypeStruct((rows, width), F32), jax.ShapeDtypeStruct((2, hidden), F32)],
        compiler_params=params(),
        cost_estimate=cost(2 * rows * hidden * width, 4 * rows * hidden + 2 * hidden * width),
        name="second_layer",
    )(*parts, pre, gain, shift, w_second)


def unit_kernel(p_ref, u_ref):
    wide = p_ref[...].astype(F32)
    u_ref[...] = (wide * lax.rsqrt(jnp.sum(wide * wide, 1, keepdims=True) + 1e-06)).astype(BF16)


def unit_rows(prototypes):
    rows, width = prototypes.shape
    blk = min(1024, rows)
    return pl.pallas_call(
        unit_kernel,
        grid=(rows // blk,),
        in_specs=[pl.BlockSpec((blk, width), lambda j: (j, 0))],
        out_specs=pl.BlockSpec((blk, width), lambda j: (j, 0)),
        out_shape=jax.ShapeDtypeStruct((rows, width), BF16),
        compiler_params=params(),
        cost_estimate=cost(4 * rows * width, 4 * rows * width),
        name="unit_rows",
    )(prototypes)


def embed(raw):
    inv_norm = lax.rsqrt(jnp.sum(raw * raw, 1, keepdims=True) + 1e-06)
    return raw * inv_norm, inv_norm


def embed_kernel(*refs):
    refs[-1][...] = embed(add_parts([p[...] for p in refs[:-1]]))[0]


def embed_rows(parts):
    return pl.pallas_call(
        embed_kernel,
        out_shape=jax.ShapeDtypeStruct(parts[0].shape, F32),
        compiler_params=params(),
        cost_estimate=cost(8 * parts[0].size, 12 * parts[0].size),
        name="embed_rows",
    )(*parts)


def put_blocks(out_ref, row, value):
    for k in range(value.shape[1] // 128):
        out_ref[row + k : row + k + 1, :] = value[:, k * 128 : (k + 1) * 128]


def score_kernel(n, *refs):
    piece, u_ref = refs[:2]
    code_ref, col_ref = refs[-2:] if n == 0 else refs[4:6]
    j = pl.program_id(0)
    code = jnp.exp(dot(piece[...].astype(BF16), u_ref[...], ((1,), (1,))) / balancing_epsilon)
    code_ref[...] = code
    put_blocks(col_ref, 0, jnp.sum(code, axis=0, keepdims=True))
    if n:
        col_ref[...] += refs[2][...]
        size = col_ref.shape[0]
        at = pl.ds(pl.multiple_of(j * size, size), size)
        for k, out in enumerate(refs[6:]):
            out[at, :] = col_ref[...]

            @pl.when(j == 0)
            def _():
                out[out.shape[0] - refs[3].shape[1] :, :] = refs[3][k + 1]


def score(piece, units, more=None):
    rows, width = piece.shape
    protos = units.shape[0]
    blk = min(1024, protos)
    lines, step = protos // 128, blk // 128
    by_step = pl.BlockSpec((step, 128), lambda j: (j, 0))
    in_specs = [whole((rows, width)), pl.BlockSpec((blk, width), lambda j: (j, 0))]
    out_specs = [pl.BlockSpec((rows, blk), lambda j: (0, j)), by_step]
    out_shape = [jax.ShapeDtypeStruct((rows, protos), F32), jax.ShapeDtypeStruct((lines, 128), F32)]
    n, extra = 0, ()
    if more is not None:
        n, extra = more[1].shape[0] - 1, more
        sent = (lines + more[1].shape[1], 128)
        in_specs += [by_step, whole(more[1].shape)]
        out_specs += [whole(sent)] * n
        out_shape += [jax.ShapeDtypeStruct(sent, F32)] * n
    return pl.pallas_call(
        functools.partial(score_kernel, n),
        grid=(protos // blk,),
        in_specs=in_specs,
        out_specs=out_specs,
        out_shape=out_shape,
        compiler_params=params(),
        cost_estimate=cost(2 * rows * protos * width, 4 * rows * protos, rows * protos),
        name="score",
    )(piece, units, *extra)


def col_scale(parts):
    lines = parts[0].shape[0]
    return 1.0 / add_parts([p[0:lines, :] for p in parts])


def pack(table, lane_row, out_ref):
    rows, width = table.shape
    out_ref[0:rows, :] = table
    out_ref[rows:, :] = jnp.zeros((8, width), F32)
    out_ref[rows : rows + 1, 0:rows] = lane_row


def logit_kernel(emb_ref, u_ref, out_ref, total, mass):
    j = pl.program_id(0)

    @pl.when(j == 0)
    def _():
        total[...] = jnp.zeros_like(total)
        mass[...] = jnp.zeros_like(mass)

    units = u_ref[...]
    logits = jnp.exp(dot(emb_ref[...].astype(BF16), units, ((1,), (1,))) / sharpness_divisor)
    total[...] += jnp.dot(logits.astype(BF16), units, preferred_element_type=F32)
    mass[...] += jnp.sum(logits, axis=1, keepdims=True)

    @pl.when(j == pl.num_programs(0) - 1)
    def _():
        pack(total[...], to_lanes(mass[...]), out_ref)


def logit_sum(embedded, units):
    rows, width = embedded.shape
    protos = units.shape[0]
    blk = min(1024, protos)
    return pl.pallas_call(
        logit_kernel,
        grid=(protos // blk,),
        in_specs=[whole((rows, width)), pl.BlockSpec((blk, width), lambda j: (j, 0))],
        out_specs=whole((rows + 8, width)),
        out_shape=jax.ShapeDtypeStruct((rows + 8, width), F32),
        scratch_shapes=[pltpu.VMEM((rows, width), F32), pltpu.VMEM((rows, 1), F32)],
        compiler_params=params(),
        cost_estimate=cost(4 * rows * protos * width, 2 * protos * width, rows * protos),
        name="logit_sum",
    )(embedded, units)


def row_kernel(n_parts, *refs):
    parts, codes, out_ref = refs[:n_parts], refs[n_parts:-1], refs[-1]
    scale = col_scale(parts)
    for k, code in enumerate(codes):
        total = 0.0
        for j in range(scale.shape[0]):
            total = total + code[:, j * 128 : (j + 1) * 128] * scale[j : j + 1, :]
        out_ref[k : k + 1, :] = to_lanes(jnp.sum(total, axis=1, keepdims=True))


def row_pass(parts, codes):
    rows, protos = codes[0].shape
    n = len(codes)
    return pl.pallas_call(
        functools.partial(row_kernel, len(parts)),
        out_shape=jax.ShapeDtypeStruct((n, rows), F32),
        compiler_params=params(),
        cost_estimate=cost(2 * n * rows * protos, 4 * n * rows * protos),
        name="row_pass",
    )(*parts, *codes)


def col_kernel(n_parts, n_codes, *refs):
    parts, codes, refs = refs[:n_parts], refs[n_parts : n_parts + n_codes], refs[n_parts + n_codes :]
    scale = 1.0 / add_parts([p[...] for p in parts])
    total = 0.0
    for k, code in enumerate(codes):
        total = total + jnp.sum(code[...] * to_column(scale[k : k + 1, :]), axis=0, keepdims=True)
    if len(refs) == 1:
        put_blocks(refs[0], 0, total)
    else:
        put_blocks(refs[1], 0, total)
        for k, out in enumerate(refs[2:]):
            out[0 : refs[1].shape[0], :] = refs[1][...]
            out[refs[1].shape[0] :, :] = refs[0][k + 1]


def col_pass(parts, codes, columns=None):
    rows, protos = codes[0].shape
    n = len(codes)
    lines = protos // 128
    extra = () if columns is None else (columns,)
    shapes = [(lines, 128)] + [(lines + c.shape[1], 128) for c in extra for _ in range(c.shape[0] - 1)]
    return pl.pallas_call(
        functools.partial(col_kernel, len(parts), n),
        out_shape=[jax.ShapeDtypeStruct(shape, F32) for shape in shapes],
        compiler_params=params(),
        cost_estimate=cost(2 * n * rows * protos, 4 * n * rows * protos),
        name="col_pass",
    )(*parts, *codes, *extra)


def target_kernel(n_parts, halves, *refs):
    parts = refs[:n_parts]
    codes_ref, u_ref, partner_ref, at_ref = refs[n_parts : n_parts + 4]
    outs, table_all, mass_all, low = refs[n_parts + 4 : -3], refs[-3], refs[-2], refs[-1]
    rows = codes_ref.shape[0]
    scale = col_scale(parts)
    total = 0.0
    for j in range(scale.shape[0]):
        weighted = codes_ref[:, j * 128 : (j + 1) * 128] * scale[j : j + 1, :]
        low[:, j * 128 : (j + 1) * 128] = weighted.astype(BF16)
        total = total + weighted
    mass = jnp.sum(total, axis=1, keepdims=True)
    table = jnp.dot(low[...], u_ref[...], preferred_element_type=F32)
    chosen = partner_ref[...] == lax.broadcasted_iota(jnp.int32, (rows, rows), 0)
    table_all[...] = dot(jnp.where(chosen, 1.0, 0.0).astype(F32), table, ((1,), (0,)), HIGHEST)
    mass_all[...] = jnp.sum(jnp.where(chosen, to_lanes(mass), 0.0), axis=1, keepdims=True)
    size = rows // halves
    for k in range(halves):
        at = pl.ds(pl.multiple_of((at_ref[2] ^ k) * size, size), size)
        pack(table_all[at, :], to_lanes(mass_all[at, :]), outs[k])


def target_sum(parts, codes, units, partner, at, halves):
    rows, protos = codes.shape
    width = units.shape[1]
    n_vmem = len(parts) + 3
    return pl.pallas_call(
        functools.partial(target_kernel, len(parts), halves),
        in_specs=[pl.BlockSpec(memory_space=pltpu.VMEM)] * n_vmem + [pl.BlockSpec(memory_space=pltpu.SMEM)],
        out_shape=[jax.ShapeDtypeStruct((rows // halves + 8, width), F32)] * halves,
        scratch_shapes=[
            pltpu.VMEM((rows, width), F32),
            pltpu.VMEM((rows, 1), F32),
            pltpu.VMEM((rows, protos), BF16),
        ],
        compiler_params=params(),
        cost_estimate=cost(2 * rows * protos * width, 4 * rows * protos + 2 * protos * width),
        name="target_sum",
    )(*parts, codes, units, partner, at)


def loss_kernel(n_raw, n_logit, n_target, *refs):
    core_ref, refs = refs[0], refs[1:]
    raws, refs = refs[:n_raw], refs[n_raw:]
    logits, refs = refs[:n_logit], refs[n_logit:]
    target = add_parts([p[...] for p in refs[:n_target]])
    grad_ref, loss_ref = refs[n_target:]
    rows = raws[0].shape[0]
    size = grad_ref.shape[0]
    at = pl.ds(pl.multiple_of(core_ref[2] * size, size), size)
    raw = add_parts([p[at, :] for p in raws])
    logit = add_parts([p[at, :] for p in logits])
    denoms = to_column(add_parts([p[rows : rows + 1, 0:rows] for p in logits]))
    denom = jnp.where(core_ref[2] == 0, denoms[0:size], denoms[rows - size :])
    embedded, inv_norm = embed(raw)
    row_scale = to_column(1.0 / target[size : size + 1, 0:size])
    wanted = target[0:size, :] * row_scale
    emb_low = embedded.astype(BF16).astype(F32)
    cross = jnp.sum(wanted * emb_low, axis=1, keepdims=True)
    loss_ref[...] = to_lanes(jnp.log(denom) - cross / sharpness_divisor)
    emb_grad = penalty_weighting * (logit / denom - wanted) / sharpness_divisor
    inner = jnp.sum(embedded * emb_grad, 1, keepdims=True)
    grad_ref[...] = (emb_grad - embedded * inner) * inv_norm


def loss_grad(raw_parts, logit_parts, target_parts, core):
    width = raw_parts[0].shape[1]
    rows = target_parts[0].shape[0] - 8
    n_vmem = len(raw_parts) + len(logit_parts) + len(target_parts)
    return pl.pallas_call(
        functools.partial(loss_kernel, len(raw_parts), len(logit_parts), len(target_parts)),
        in_specs=[pl.BlockSpec(memory_space=pltpu.SMEM)] + [pl.BlockSpec(memory_space=pltpu.VMEM)] * n_vmem,
        out_shape=[jax.ShapeDtypeStruct((rows, width), F32), jax.ShapeDtypeStruct((1, rows), F32)],
        compiler_params=params(),
        cost_estimate=cost(20 * rows * width, 24 * rows * width),
        name="loss_grad",
    )(core, *raw_parts, *logit_parts, *target_parts)


def pick_kernel(f_ref, at_ref, keep_ref, send_ref):
    n_z, height, rows = keep_ref.shape
    depth = f_ref.shape[1]
    shape = (n_z * height, depth)
    row = lax.broadcasted_iota(jnp.int32, shape, 0)
    col = lax.broadcasted_iota(jnp.int32, shape, 1)
    d_cols = depth // (2 * n_z)
    me, share = at_ref[0], at_ref[1] * height
    for out, y in ((keep_ref, me & 1), (send_ref, (me & 1) ^ 1)):
        first = jnp.zeros(shape, jnp.int32)
        for k in range(n_z):
            owner = (((me >> 1) ^ k) << 1) + y
            first = jnp.where(row >= k * height, owner * d_cols + share - k * height, first)
        chosen = jnp.where(col == first + row, 1.0, 0.0).astype(BF16)
        out[...] = dot(chosen, f_ref[...], ((1,), (1,))).reshape(n_z, height, rows)


def columns_pick(features, at, n_batch, n_proto):
    rows, depth = features.shape
    shape = jax.ShapeDtypeStruct((n_batch // 2, depth // (n_batch * n_proto), rows), F32)
    return pl.pallas_call(
        pick_kernel,
        in_specs=[pl.BlockSpec(memory_space=pltpu.VMEM), pl.BlockSpec(memory_space=pltpu.SMEM)],
        out_shape=[shape, shape],
        compiler_params=params(),
        cost_estimate=cost(2 * depth * depth // n_proto * rows, 8 * rows * depth),
        name="columns_pick",
    )(features, at)


def join_kernel(n_z, keep_ref, got_ref, *refs):
    out_ref, height = refs[-1], keep_ref.shape[1]
    out_ref[0, 0] = keep_ref[0]
    out_ref[0, 1] = got_ref[0]
    for k in range(2 * n_z - 2):
        out_ref[0, 2 + k] = refs[k][refs[k].shape[0] - height :, :]


def columns_join(keep, got, first, second):
    n_z, height, rows = keep.shape
    return pl.pallas_call(
        functools.partial(join_kernel, n_z),
        out_shape=jax.ShapeDtypeStruct((1, 2 * n_z, height, rows), F32),
        compiler_params=params(),
        cost_estimate=cost(0, 16 * n_z * height * rows),
        name="columns_join",
    )(keep, got, *[m for pair in zip(first, second) for m in pair])


def columns_kernel(masks, at_ref, *refs):
    out_ref = refs[-1]
    inner = len(masks) // (len(refs) - 1)
    for k, mask in enumerate(masks):
        _, n_batch, height, rows = refs[k // inner].shape
        row = pl.multiple_of((at_ref[1] ^ mask) * height, height)
        for i in range(n_batch):
            out_ref[at_ref[0] ^ i, pl.ds(row, height), :] = refs[k // inner][k % inner, i].astype(BF16)


def columns_all(own, other, at):
    n_proto = 2 * own.shape[0]
    _, n_batch, height, rows = own.shape
    smem = pl.BlockSpec(memory_space=pltpu.SMEM)
    vmem = pl.BlockSpec(memory_space=pltpu.VMEM)
    return pl.pallas_call(
        functools.partial(columns_kernel, (0, 2, 1, 3)),
        in_specs=[smem, vmem, vmem],
        out_shape=jax.ShapeDtypeStruct((n_batch, n_proto * height, rows), BF16),
        compiler_params=params(),
        cost_estimate=cost(0, 6 * n_proto * height * n_batch * rows),
        name="columns_all",
    )(at, own, other)


def cast_kernel(in_ref, out_ref):
    out_ref[...] = in_ref[...].T.astype(BF16)


def columns_cast(columns):
    return pl.pallas_call(
        cast_kernel,
        out_shape=jax.ShapeDtypeStruct(columns.shape[::-1], BF16),
        compiler_params=params(),
        name="columns_cast",
    )(columns)


def tail_half(refs, grads, odd, n_batch, sums_ref, grad_all, low_all, cols_all):
    at_ref, pre_ref, cols_ref, stats, gain, shift, w_ref = refs
    unit, width = pre_ref.shape[1], grad_all.shape[1]
    size, n = unit // 2, n_batch // 2
    e_rows = 16 * (-(-(width // n_batch) // 16))
    for k in range(n):
        for flip in range(2):
            place = pl.multiple_of(k * unit + (at_ref[2] ^ flip) * size, size)
            grad_all[pl.ds(place, size), :] = grads[flip][k].astype(BF16)
    mine = lax.broadcasted_iota(jnp.int32, (e_rows, width), 0) + at_ref[0] * (width // n_batch)
    chosen = jnp.where(mine == lax.broadcasted_iota(jnp.int32, (e_rows, width), 1), 1.0, 0.0).astype(BF16)
    w2 = 0.0
    for k in range(n):
        rows = slice(k * unit, (k + 1) * unit)
        block = at_ref[0] ^ (2 * k + odd)
        normed, shifted = batch_norm(pre_ref[block], stats, gain, shift)
        grad = grad_all[rows, :]
        picked = dot(chosen, grad, ((1,), (1,))).astype(BF16)
        hidden = jnp.maximum(shifted, 0.0).astype(BF16)
        w2 = w2 + jnp.dot(picked, hidden, preferred_element_type=F32)
        hidden_grad = dot(grad, w_ref[...], ((1,), (1,)))
        bn_grad = jnp.where(shifted > 0, hidden_grad, 0.0)
        sums_ref[0, pl.ds(block, 1), :] = jnp.sum(bn_grad, axis=0, keepdims=True)
        sums_ref[1, pl.ds(block, 1), :] = jnp.sum(bn_grad * normed, axis=0, keepdims=True)
        low_all[rows, :] = bn_grad.astype(BF16)
        cols_all[:, rows] = cols_ref[block]
    return jnp.dot(cols_all[...], low_all[...], preferred_element_type=F32), w2


def near_kernel(n_batch, n_grads, *refs):
    ins, refs = refs[:7], refs[7:]
    grads, (w1_ref, w2_ref, sums_ref, *scratch) = refs[:2], refs[2:]
    sums_ref[...] = jnp.zeros_like(sums_ref)
    ins = ins[:3] + tuple(r[...] for r in ins[3:6]) + ins[6:]
    w1_ref[...], w2_ref[...] = tail_half(ins, grads, 0, n_batch, sums_ref, *scratch)


def far_kernel(crops_all, n_batch, n_grads, *refs):
    ins, refs = refs[:7], refs[7:]
    grads, refs = (refs[: n_grads // 2], refs[n_grads // 2 : n_grads]), refs[n_grads:]
    near_w1, near_w2, near_sums, flat_ref, total_ref = refs[:5]
    w1_ref, w2_ref, gain_grad_ref, shift_grad_ref, sums, *scratch = refs[5:]
    ins = ins[:3] + tuple(r[...] for r in ins[3:6]) + ins[6:]
    stats, gain = ins[3:5]
    sums[...] = near_sums[...]
    w1, w2 = tail_half(ins, [half[0] for half in grads], 1, n_batch, sums, *scratch)
    w2_ref[...] = (near_w2[...] + w2)[0 : w2_ref.shape[0], :]
    shift_grad = jnp.sum(sums[0], axis=0, keepdims=True)
    gain_grad = jnp.sum(sums[1], axis=0, keepdims=True)
    shift_grad_ref[...] = shift_grad
    gain_grad_ref[...] = gain_grad
    flat = total_ref[...] * (shift_grad / crops_all) + flat_ref[...] * (gain_grad / crops_all)
    w1_ref[...] = gain * stats[1:2, :] * (near_w1[...] + w1 - flat)


def tail_call(kernel, outs, scratch, at, pre_all, columns, stats, gain, shift, w_second, grads, more, name):
    n_batch, unit, hidden = pre_all.shape
    width, d_cols = w_second.shape[1], columns.shape[1]
    crops = n_batch * unit // 2
    vmem = pl.BlockSpec(memory_space=pltpu.VMEM)
    return pl.pallas_call(
        functools.partial(kernel, n_batch, len(grads)),
        in_specs=[pl.BlockSpec(memory_space=pltpu.SMEM)] + [vmem] * (6 + len(grads) + len(more)),
        out_shape=[jax.ShapeDtypeStruct(n, F32) for n in outs],
        scratch_shapes=[pltpu.VMEM(n, F32) for n in scratch]
        + [
            pltpu.VMEM((crops, width), BF16),
            pltpu.VMEM((crops, hidden), BF16),
            pltpu.VMEM((d_cols, crops), BF16),
        ],
        compiler_params=params(20),
        cost_estimate=cost(2 * crops * hidden * (width + 256), 4 * crops * hidden),
        name=name,
    )(at, pre_all, columns, stats, gain, shift, w_second, *grads, *more)


def flat_kernel(pre_hbm, cols_ref, stats_ref, gain_ref, shift_ref, pre_ref, flat_ref, total_ref, sems):
    n_batch = pre_ref.shape[0]
    copies = [pltpu.make_async_copy(pre_hbm.at[k], pre_ref.at[k], sems.at[k]) for k in range(n_batch)]
    for copy in copies:
        copy.start()
    stats, gain, shift = stats_ref[...], gain_ref[...], shift_ref[...]
    total = 0.0
    for k in range(n_batch):
        total = total + jnp.sum(cols_ref[k].astype(F32), axis=1, keepdims=True)
        copies[k].wait()
        normed, _ = batch_norm(pre_ref[k], stats, gain, shift)
        part = jnp.dot(cols_ref[k], normed.astype(BF16), preferred_element_type=F32)
        if k == 0:
            flat_ref[...] = part
        else:
            flat_ref[...] += part
    total_ref[...] = total


def flat_sums(pre_all, columns, stats, gain, shift):
    n_batch, unit, hidden = pre_all.shape
    d_cols = columns.shape[1]
    vmem = pl.BlockSpec(memory_space=pltpu.VMEM)
    return pl.pallas_call(
        flat_kernel,
        in_specs=[pl.BlockSpec(memory_space=pltpu.HBM)] + [vmem] * 4,
        out_specs=[vmem] * 3,
        out_shape=[
            jax.ShapeDtypeStruct((n_batch, unit, hidden), F32),
            jax.ShapeDtypeStruct((d_cols, hidden), F32),
            jax.ShapeDtypeStruct((d_cols, 1), F32),
        ],
        scratch_shapes=[pltpu.SemaphoreType.DMA((n_batch,))],
        compiler_params=params(20),
        cost_estimate=cost(2 * n_batch * unit * hidden * d_cols, 4 * n_batch * unit * hidden),
        name="flat_sums",
    )(pre_all, columns, stats, gain, shift)


def whole_tail_kernel(crops_all, e_cols, *refs):
    at_ref, pre_ref, cols_ref, stats_ref, gain_ref, shift_ref, w_ref, raw_ref = refs[:8]
    w1_ref, w2_ref, gain_grad_ref, shift_grad_ref, grad_all, grad_cols = refs[8:]

    @pl.when(pl.program_id(0) == 0)
    def _():
        grad_all[...] = raw_ref[...].astype(BF16)
        shape = (grad_cols.shape[0], grad_all.shape[1])
        mine = lax.broadcasted_iota(jnp.int32, shape, 0) + at_ref[0] * e_cols
        chosen = jnp.where(mine == lax.broadcasted_iota(jnp.int32, shape, 1), 1.0, 0.0).astype(BF16)
        grad_cols[...] = dot(chosen, grad_all[...], ((1,), (1,))).astype(BF16)

    stats, gain = stats_ref[...], gain_ref[...]
    normed, shifted = batch_norm(pre_ref[...], stats, gain, shift_ref[...])
    hidden = jnp.maximum(shifted, 0.0).astype(BF16)
    w2_ref[...] = jnp.dot(grad_cols[...], hidden, preferred_element_type=F32)[0:e_cols, :]
    hidden_grad = dot(grad_all[...], w_ref[...], ((1,), (1,)))
    bn_grad = jnp.where(shifted > 0, hidden_grad, 0.0)
    shift_grad = jnp.sum(bn_grad, axis=0, keepdims=True)
    gain_grad = jnp.sum(bn_grad * normed, axis=0, keepdims=True)
    shift_grad_ref[...] = shift_grad
    gain_grad_ref[...] = gain_grad
    scale = gain * stats[1:2, :]
    pre_grad = scale * (bn_grad - shift_grad / crops_all - normed * (gain_grad / crops_all))
    w1_ref[...] = jnp.dot(cols_ref[...], pre_grad.astype(BF16), preferred_element_type=F32)


def whole_tail(pre_all, columns, stats, gain, shift, w_second, raw, at, e_cols):
    crops_all, hidden = pre_all.shape
    width, d_cols = w_second.shape[1], columns.shape[0]
    blk = min(hidden, max(128, 256 * 1024 // crops_all))
    smem = pl.BlockSpec(memory_space=pltpu.SMEM)
    vmem = pl.BlockSpec(memory_space=pltpu.VMEM)

    def cols(n):
        return pl.BlockSpec((n, blk), lambda j: (0, j))

    return pl.pallas_call(
        functools.partial(whole_tail_kernel, crops_all, e_cols),
        grid=(hidden // blk,),
        in_specs=[smem, cols(crops_all), vmem, cols(2), cols(1), cols(1)]
        + [pl.BlockSpec((blk, width), lambda j: (j, 0)), vmem],
        out_specs=[cols(d_cols), cols(e_cols), cols(1), cols(1)],
        out_shape=[jax.ShapeDtypeStruct((n, hidden), F32) for n in (d_cols, e_cols, 1, 1)],
        scratch_shapes=[
            pltpu.VMEM((crops_all, width), BF16),
            pltpu.VMEM((-(-e_cols // 16) * 16, crops_all), BF16),
        ],
        compiler_params=params(58),
        cost_estimate=cost(2 * crops_all * hidden * (width + d_cols), 4 * crops_all * hidden),
        name="whole_tail",
    )(at, pre_all, columns, stats, gain, shift, w_second, raw)


def after(value, *others):
    return lax.optimization_barrier((value,) + others)[0]


def body(features, w_first, bn_gain, bn_shift, w_second, prototypes, partner):
    n_batch, n_proto = lax.axis_size("batch"), lax.axis_size("proto")
    me, proto_me = lax.axis_index("batch").astype(jnp.int32), lax.axis_index("proto").astype(jnp.int32)
    rows, depth = features.shape
    width = w_second.shape[1]
    crops_all = rows * n_batch
    d_cols, e_cols = depth // n_batch, width // n_batch
    gain, shift = bn_gain[None, :], bn_shift[None, :]
    short = n_batch == 8 and n_proto == 4 and depth % 512 == 0
    at = jnp.stack([me, proto_me, proto_me & 1 if short else proto_me * 0])

    pre, pre_again, moments = first_layer(features, w_first, n_batch if short else 1)
    pre_all = lax.all_gather(pre, "batch", tiled=True)
    moment_parts = [lax.all_to_all(moments, "batch", 0, 0)] if short else batch_parts(moments)
    units = unit_rows(prototypes)
    emb_part, stats = second_layer(crops_all, moment_parts, pre_again, gain, shift, w_second)
    raw_parts = proto_parts(emb_part)
    if short:
        keep, send = columns_pick(after(features, emb_part), at, n_batch, n_proto)
        raw_parts[0], keep, send, units = lax.optimization_barrier((raw_parts[0], keep, send, units))
    embedded = embed_rows(raw_parts)

    if short:
        partner_emb = swap(embedded, "batch", 1)
        own_codes, own_col = score(embedded, units)
        logit = logit_sum(embedded, units)
        partner_emb, own_col, logit = lax.optimization_barrier((partner_emb, own_col, logit))
        logit = logit + swap(logit, "proto", 1)
        more_codes, *cols = score(partner_emb, units, (own_col, keep))
        cols[0], logit = lax.optimization_barrier((cols[0], logit))
        codes = [own_codes, more_codes]
    else:
        codes, *cols = score(embedded, units)
        codes = [codes]
        logit = logit_sum(embedded, units)
    moved = []
    for iteration in range(ITERS):
        if short and iteration < 2:
            moved.append([swap(c, "batch", 2 * k + 2) for k, c in enumerate(cols[1:])])
            col_parts = [cols[0]] + moved[-1]
        else:
            col_parts = batch_parts(cols[0], 2 if short else 1)
        if iteration == 0:
            logit_parts = proto_parts(logit, 2 if short else 1)
            col_parts[0], *logit_parts = lax.optimization_barrier((col_parts[0], *logit_parts))
        if short and iteration == 0:
            got = swap(after(send, cols[0]), "batch", 1)
            col_parts[0], got = lax.optimization_barrier((col_parts[0], got))
        if short and iteration == 2:
            columns = columns_join(after(keep, cols[0]), got, *moved)
            columns = [columns, swap(columns, "proto", 2)]
            col_parts[0], *columns = lax.optimization_barrier((col_parts[0], *columns))
        if iteration < ITERS - 1:
            row_parts = proto_small(row_pass(col_parts, codes))
            cols = col_pass(row_parts, codes, got if short and iteration == 0 else None)
    if short:
        own_half, send = target_sum(col_parts, codes[0], units, partner[None, :], at, 2)
        columns = after(jnp.concatenate(columns), own_half)
        own_half = own_half + swap(send, "proto", 1)
        columns = [columns, swap(columns, "proto", 1)]
        target_parts = proto_parts(own_half, 2)
        target_parts[0], *columns = lax.optimization_barrier((target_parts[0], *columns))
    else:
        target_parts = proto_parts(target_sum(col_parts, codes[0], units, partner[None, :], at, 1)[0])
    raw_grad, penalty = loss_grad(raw_parts, logit_parts, target_parts, at)

    if short:
        columns = columns_all(*(after(c, raw_grad) for c in columns), at)
        pre_all = after(pre_all, raw_grad)
        near = [raw_grad] + [swap(raw_grad, "batch", k) for k in (2, 4, 6)]
        near = jnp.stack(near)
        far = swap(near, "batch", 1)
        other_penalty = swap(penalty, "proto", 1)
        first = at[2] == 0
        penalty = jnp.concatenate(
            [jnp.where(first, penalty, other_penalty), jnp.where(first, other_penalty, penalty)], axis=1
        )
        ins = (at, pre_all.reshape(n_batch, rows, -1), columns, stats, gain, shift, w_second)
        e_rows, hidden = -(-e_cols // 16) * 16, w_second.shape[0]
        table = (2, n_batch, hidden)
        pre_near, *flat = flat_sums(*ins[1:-1])
        ins = (at, pre_near) + ins[2:]
        half = tail_call(
            near_kernel, [(d_cols, hidden), (e_rows, hidden), table], [], *ins, [near, swap(near, "proto", 1)], [], "tail_near"
        )
        far, penalty, *half = lax.optimization_barrier((far, penalty, *half, *flat))
        grad_w1, grad_w2, grad_gain, grad_shift = tail_call(
            functools.partial(far_kernel, crops_all),
            [(d_cols, hidden), (e_cols, hidden), (1, hidden), (1, hidden)], [table],
            *ins, [far, swap(far, "proto", 1)], half, "tail_far",
        )
    else:
        by_owner = jnp.swapaxes(features.astype(F32).reshape(rows, n_batch, d_cols), 0, 1)
        columns = columns_cast(lax.all_to_all(by_owner, "batch", 0, 0).reshape(crops_all, d_cols))
        raw_all = lax.all_gather(raw_grad, "batch", tiled=True)
        grad_w1, grad_w2, grad_gain, grad_shift = whole_tail(
            pre_all, columns, stats, gain, shift, w_second, raw_all, at, e_cols
        )
    return (penalty[0], grad_w1, grad_gain[0], grad_shift[0], grad_w2.T)


def solution(mesh):
    return jax.shard_map(
        body,
        mesh=mesh,
        in_specs=(
            P("batch", None),
            P(None, "proto"),
            P("proto"),
            P("proto"),
            P("proto", None),
            P("proto", None),
            P("batch"),
        ),
        out_specs=(P("batch"), P("batch", "proto"), P("proto"), P("proto"), P("proto", "batch")),
        check_vma=False,
    )
```

```python
import functools

import jax
import jax.numpy as jnp
from jax import lax
from jax.experimental import pallas as pl
from jax.experimental.pallas import tpu as pltpu
from jax.sharding import PartitionSpec as P

ITERS = 3
F32 = jnp.float32
BF16 = jnp.bfloat16
HIGHEST = lax.Precision.HIGHEST

balancing_epsilon = 0.05
sharpness_divisor = 0.1
penalty_weighting = 64.0


def stages(n, first, stride=1):
    out, radix = [], first
    while stride < n:
        radix = min(radix, n // stride)
        out.append((stride, radix))
        stride *= radix
        radix = 4 if (n // stride) % 4 == 0 else 2
    return out


def swap(v, axis, mask):
    n = lax.axis_size(axis)
    return lax.ppermute(v, axis, [(i, i ^ mask) for i in range(n)])


def add_parts(parts):
    if len(parts) == 4:
        return (parts[0] + parts[1]) + (parts[2] + parts[3])
    return functools.reduce(lambda x, y: x + y, parts)


def exchange(v, axis, first, stride=1):
    n = lax.axis_size(axis)
    parts = [v]
    for step, radix in stages(n, first, stride):
        v = add_parts(parts)
        parts = [v] + [swap(v, axis, k * step) for k in range(1, radix)]
    return parts


def batch_parts(v, stride=1):
    steps = (lax.axis_size("batch") // stride).bit_length() - 1
    return exchange(v, "batch", 2 if steps % 2 else 4, stride)


def proto_parts(v, stride=1):
    return exchange(v, "proto", 2, stride)


def proto_small(v):
    return exchange(v, "proto", 4 if lax.axis_size("proto") == 4 else 2)


def whole(shape):
    return pl.BlockSpec(shape, lambda *_: (0,) * len(shape))


def params(mib=24):
    return pltpu.CompilerParams(vmem_limit_bytes=mib * 1024 * 1024)


def cost(flops, nbytes, trans=0):
    return pl.CostEstimate(flops=int(flops), bytes_accessed=int(nbytes), transcendentals=int(trans))


def dot(a, b, dims, precision=None):
    return lax.dot_general(a, b, ((dims[0], dims[1]), ((), ())), precision=precision, preferred_element_type=F32)


def eye(n):
    return lax.broadcasted_iota(jnp.int32, (n, n), 0) == lax.broadcasted_iota(jnp.int32, (n, n), 1)


def to_lanes(col):
    n = col.shape[0]
    return jnp.sum(jnp.where(eye(n), col, 0.0), axis=0, keepdims=True)


def to_column(row):
    n = row.shape[1]
    return jnp.sum(jnp.where(eye(n), row, 0.0), axis=1, keepdims=True)


def first_kernel(f_hbm, w_hbm, pre_ref, again_ref, mom_ref, f_ref, w_ref, sems):
    depth, hidden = w_ref.shape
    n = sems.shape[0] - 1
    step = depth // n
    copies = [pltpu.make_async_copy(f_hbm, f_ref, sems.at[n])]
    for k in range(n):
        at = pl.ds(k * step, step)
        copies.append(pltpu.make_async_copy(w_hbm.at[at, :], w_ref.at[at, :], sems.at[k]))
    for copy in copies:
        copy.start()
    copies[0].wait()
    for k in range(n):
        copies[k + 1].wait()
        at = slice(k * step, (k + 1) * step)
        part = jnp.dot(f_ref[:, at], w_ref[at, :], preferred_element_type=F32)
        if k == 0:
            pre_ref[...] = part
        else:
            pre_ref[...] += part
    pre = pre_ref[...]
    again_ref[...] = pre
    first = jnp.sum(pre, axis=0, keepdims=True)
    second = jnp.sum(pre * pre, axis=0, keepdims=True)
    for k in range(mom_ref.shape[0]):
        mom_ref[k, :, 0:hidden] = first
        mom_ref[k, :, hidden:] = second


def first_layer(features, w_first, spread):
    rows, depth = features.shape
    hidden = w_first.shape[1]
    steps = 6 if depth % (6 * 128) == 0 else 1
    return pl.pallas_call(
        first_kernel,
        in_specs=[pl.BlockSpec(memory_space=pl.ANY)] * 2,
        out_shape=[jax.ShapeDtypeStruct((rows, hidden), F32)] * 2
        + [jax.ShapeDtypeStruct((spread, 1, 2 * hidden), F32)],
        scratch_shapes=[
            pltpu.VMEM((rows, depth), BF16),
            pltpu.VMEM((depth, hidden), BF16),
            pltpu.SemaphoreType.DMA((steps + 1,)),
        ],
        compiler_params=params(52),
        cost_estimate=cost(2 * rows * depth * hidden, 2 * depth * hidden + 4 * rows * hidden),
        name="first_layer",
    )(features, w_first)


def batch_norm(pre, stats, gain, shift):
    normed = (pre - stats[0:1, :]) * stats[1:2, :]
    return normed, gain * normed + shift


def second_kernel(crops_all, n_parts, *refs):
    parts = refs[:n_parts]
    pre_ref, gain_ref, shift_ref, w_ref, emb_ref, stats_ref = refs[n_parts:]
    hidden = pre_ref.shape[1]
    moments = add_parts([p[k] for p in parts for k in range(p.shape[0])]) / crops_all
    mean = moments[:, 0:hidden]
    var = moments[:, hidden:] - mean * mean
    stats_ref[0:1, :] = mean
    stats_ref[1:2, :] = lax.rsqrt(var + 1e-05)
    _, shifted = batch_norm(pre_ref[...], stats_ref[...], gain_ref[...], shift_ref[...])
    low = jnp.maximum(shifted, 0.0).astype(BF16)
    emb_ref[...] = jnp.dot(low, w_ref[...], preferred_element_type=F32)


def second_layer(crops_all, parts, pre, gain, shift, w_second):
    rows, hidden = pre.shape
    width = w_second.shape[1]
    return pl.pallas_call(
        functools.partial(second_kernel, crops_all, len(parts)),
        out_shape=[jax.ShapeDtypeStruct((rows, width), F32), jax.ShapeDtypeStruct((2, hidden), F32)],
        compiler_params=params(),
        cost_estimate=cost(2 * rows * hidden * width, 4 * rows * hidden + 2 * hidden * width),
        name="second_layer",
    )(*parts, pre, gain, shift, w_second)


def unit_kernel(p_ref, u_ref):
    wide = p_ref[...].astype(F32)
    u_ref[...] = (wide * lax.rsqrt(jnp.sum(wide * wide, 1, keepdims=True) + 1e-06)).astype(BF16)


def unit_rows(prototypes):
    rows, width = prototypes.shape
    blk = min(1024, rows)
    return pl.pallas_call(
        unit_kernel,
        grid=(rows // blk,),
        in_specs=[pl.BlockSpec((blk, width), lambda j: (j, 0))],
        out_specs=pl.BlockSpec((blk, width), lambda j: (j, 0)),
        out_shape=jax.ShapeDtypeStruct((rows, width), BF16),
        compiler_params=params(),
        cost_estimate=cost(4 * rows * width, 4 * rows * width),
        name="unit_rows",
    )(prototypes)


def embed(raw):
    inv_norm = lax.rsqrt(jnp.sum(raw * raw, 1, keepdims=True) + 1e-06)
    return raw * inv_norm, inv_norm


def embed_kernel(*refs):
    refs[-1][...] = embed(add_parts([p[...] for p in refs[:-1]]))[0]


def embed_rows(parts):
    return pl.pallas_call(
        embed_kernel,
        out_shape=jax.ShapeDtypeStruct(parts[0].shape, F32),
        compiler_params=params(),
        cost_estimate=cost(8 * parts[0].size, 12 * parts[0].size),
        name="embed_rows",
    )(*parts)


def put_blocks(out_ref, row, value):
    for k in range(value.shape[1] // 128):
        out_ref[row + k : row + k + 1, :] = value[:, k * 128 : (k + 1) * 128]


def score_kernel(n, *refs):
    piece, u_ref = refs[:2]
    code_ref, col_ref = refs[-2:] if n == 0 else refs[4:6]
    j = pl.program_id(0)
    code = jnp.exp(dot(piece[...].astype(BF16), u_ref[...], ((1,), (1,))) / balancing_epsilon)
    code_ref[...] = code
    put_blocks(col_ref, 0, jnp.sum(code, axis=0, keepdims=True))
    if n:
        col_ref[...] += refs[2][...]
        size = col_ref.shape[0]
        at = pl.ds(pl.multiple_of(j * size, size), size)
        for k, out in enumerate(refs[6:]):
            out[at, :] = col_ref[...]

            @pl.when(j == 0)
            def _():
                out[out.shape[0] - refs[3].shape[1] :, :] = refs[3][k + 1]


def score(piece, units, more=None):
    rows, width = piece.shape
    protos = units.shape[0]
    blk = min(1024, protos)
    lines, step = protos // 128, blk // 128
    by_step = pl.BlockSpec((step, 128), lambda j: (j, 0))
    in_specs = [whole((rows, width)), pl.BlockSpec((blk, width), lambda j: (j, 0))]
    out_specs = [pl.BlockSpec((rows, blk), lambda j: (0, j)), by_step]
    out_shape = [jax.ShapeDtypeStruct((rows, protos), F32), jax.ShapeDtypeStruct((lines, 128), F32)]
    n, extra = 0, ()
    if more is not None:
        n, extra = more[1].shape[0] - 1, more
        sent = (lines + more[1].shape[1], 128)
        in_specs += [by_step, whole(more[1].shape)]
        out_specs += [whole(sent)] * n
        out_shape += [jax.ShapeDtypeStruct(sent, F32)] * n
    return pl.pallas_call(
        functools.partial(score_kernel, n),
        grid=(protos // blk,),
        in_specs=in_specs,
        out_specs=out_specs,
        out_shape=out_shape,
        compiler_params=params(),
        cost_estimate=cost(2 * rows * protos * width, 4 * rows * protos, rows * protos),
        name="score",
    )(piece, units, *extra)


def col_scale(parts):
    lines = parts[0].shape[0]
    return 1.0 / add_parts([p[0:lines, :] for p in parts])


def pack(table, lane_row, out_ref):
    rows, width = table.shape
    out_ref[0:rows, :] = table
    out_ref[rows:, :] = jnp.zeros((8, width), F32)
    out_ref[rows : rows + 1, 0:rows] = lane_row


def logit_kernel(emb_ref, u_ref, out_ref, total, mass):
    j = pl.program_id(0)

    @pl.when(j == 0)
    def _():
        total[...] = jnp.zeros_like(total)
        mass[...] = jnp.zeros_like(mass)

    units = u_ref[...]
    logits = jnp.exp(dot(emb_ref[...].astype(BF16), units, ((1,), (1,))) / sharpness_divisor)
    total[...] += jnp.dot(logits.astype(BF16), units, preferred_element_type=F32)
    mass[...] += jnp.sum(logits, axis=1, keepdims=True)

    @pl.when(j == pl.num_programs(0) - 1)
    def _():
        pack(total[...], to_lanes(mass[...]), out_ref)


def logit_sum(embedded, units):
    rows, width = embedded.shape
    protos = units.shape[0]
    blk = min(1024, protos)
    return pl.pallas_call(
        logit_kernel,
        grid=(protos // blk,),
        in_specs=[whole((rows, width)), pl.BlockSpec((blk, width), lambda j: (j, 0))],
        out_specs=whole((rows + 8, width)),
        out_shape=jax.ShapeDtypeStruct((rows + 8, width), F32),
        scratch_shapes=[pltpu.VMEM((rows, width), F32), pltpu.VMEM((rows, 1), F32)],
        compiler_params=params(),
        cost_estimate=cost(4 * rows * protos * width, 2 * protos * width, rows * protos),
        name="logit_sum",
    )(embedded, units)


def row_kernel(n_parts, *refs):
    parts, codes, out_ref = refs[:n_parts], refs[n_parts:-1], refs[-1]
    scale = col_scale(parts)
    for k, code in enumerate(codes):
        total = 0.0
        for j in range(scale.shape[0]):
            total = total + code[:, j * 128 : (j + 1) * 128] * scale[j : j + 1, :]
        out_ref[k : k + 1, :] = to_lanes(jnp.sum(total, axis=1, keepdims=True))


def row_pass(parts, codes):
    rows, protos = codes[0].shape
    n = len(codes)
    return pl.pallas_call(
        functools.partial(row_kernel, len(parts)),
        out_shape=jax.ShapeDtypeStruct((n, rows), F32),
        compiler_params=params(),
        cost_estimate=cost(2 * n * rows * protos, 4 * n * rows * protos),
        name="row_pass",
    )(*parts, *codes)


def col_kernel(n_parts, n_codes, *refs):
    parts, codes, refs = refs[:n_parts], refs[n_parts : n_parts + n_codes], refs[n_parts + n_codes :]
    scale = 1.0 / add_parts([p[...] for p in parts])
    total = 0.0
    for k, code in enumerate(codes):
        total = total + jnp.sum(code[...] * to_column(scale[k : k + 1, :]), axis=0, keepdims=True)
    if len(refs) == 1:
        put_blocks(refs[0], 0, total)
    else:
        put_blocks(refs[1], 0, total)
        for k, out in enumerate(refs[2:]):
            out[0 : refs[1].shape[0], :] = refs[1][...]
            out[refs[1].shape[0] :, :] = refs[0][k + 1]


def col_pass(parts, codes, columns=None):
    rows, protos = codes[0].shape
    n = len(codes)
    lines = protos // 128
    extra = () if columns is None else (columns,)
    shapes = [(lines, 128)] + [(lines + c.shape[1], 128) for c in extra for _ in range(c.shape[0] - 1)]
    return pl.pallas_call(
        functools.partial(col_kernel, len(parts), n),
        out_shape=[jax.ShapeDtypeStruct(shape, F32) for shape in shapes],
        compiler_params=params(),
        cost_estimate=cost(2 * n * rows * protos, 4 * n * rows * protos),
        name="col_pass",
    )(*parts, *codes, *extra)


def target_kernel(n_parts, halves, *refs):
    parts = refs[:n_parts]
    codes_ref, u_ref, partner_ref, at_ref = refs[n_parts : n_parts + 4]
    outs, table_all, mass_all, low = refs[n_parts + 4 : -3], refs[-3], refs[-2], refs[-1]
    rows = codes_ref.shape[0]
    scale = col_scale(parts)
    total = 0.0
    for j in range(scale.shape[0]):
        weighted = codes_ref[:, j * 128 : (j + 1) * 128] * scale[j : j + 1, :]
        low[:, j * 128 : (j + 1) * 128] = weighted.astype(BF16)
        total = total + weighted
    mass = jnp.sum(total, axis=1, keepdims=True)
    table = jnp.dot(low[...], u_ref[...], preferred_element_type=F32)
    chosen = partner_ref[...] == lax.broadcasted_iota(jnp.int32, (rows, rows), 0)
    table_all[...] = dot(jnp.where(chosen, 1.0, 0.0).astype(F32), table, ((1,), (0,)), HIGHEST)
    mass_all[...] = jnp.sum(jnp.where(chosen, to_lanes(mass), 0.0), axis=1, keepdims=True)
    size = rows // halves
    for k in range(halves):
        at = pl.ds(pl.multiple_of((at_ref[2] ^ k) * size, size), size)
        pack(table_all[at, :], to_lanes(mass_all[at, :]), outs[k])


def target_sum(parts, codes, units, partner, at, halves):
    rows, protos = codes.shape
    width = units.shape[1]
    n_vmem = len(parts) + 3
    return pl.pallas_call(
        functools.partial(target_kernel, len(parts), halves),
        in_specs=[pl.BlockSpec(memory_space=pltpu.VMEM)] * n_vmem + [pl.BlockSpec(memory_space=pltpu.SMEM)],
        out_shape=[jax.ShapeDtypeStruct((rows // halves + 8, width), F32)] * halves,
        scratch_shapes=[
            pltpu.VMEM((rows, width), F32),
            pltpu.VMEM((rows, 1), F32),
            pltpu.VMEM((rows, protos), BF16),
        ],
        compiler_params=params(),
        cost_estimate=cost(2 * rows * protos * width, 4 * rows * protos + 2 * protos * width),
        name="target_sum",
    )(*parts, codes, units, partner, at)


def loss_kernel(n_raw, n_logit, n_target, *refs):
    core_ref, refs = refs[0], refs[1:]
    raws, refs = refs[:n_raw], refs[n_raw:]
    logits, refs = refs[:n_logit], refs[n_logit:]
    target = add_parts([p[...] for p in refs[:n_target]])
    grad_ref, loss_ref = refs[n_target:]
    rows = raws[0].shape[0]
    size = grad_ref.shape[0]
    at = pl.ds(pl.multiple_of(core_ref[2] * size, size), size)
    raw = add_parts([p[at, :] for p in raws])
    logit = add_parts([p[at, :] for p in logits])
    denoms = to_column(add_parts([p[rows : rows + 1, 0:rows] for p in logits]))
    denom = jnp.where(core_ref[2] == 0, denoms[0:size], denoms[rows - size :])
    embedded, inv_norm = embed(raw)
    row_scale = to_column(1.0 / target[size : size + 1, 0:size])
    wanted = target[0:size, :] * row_scale
    emb_low = embedded.astype(BF16).astype(F32)
    cross = jnp.sum(wanted * emb_low, axis=1, keepdims=True)
    loss_ref[...] = to_lanes(jnp.log(denom) - cross / sharpness_divisor)
    emb_grad = penalty_weighting * (logit / denom - wanted) / sharpness_divisor
    inner = jnp.sum(embedded * emb_grad, 1, keepdims=True)
    grad_ref[...] = (emb_grad - embedded * inner) * inv_norm


def loss_grad(raw_parts, logit_parts, target_parts, core):
    width = raw_parts[0].shape[1]
    rows = target_parts[0].shape[0] - 8
    n_vmem = len(raw_parts) + len(logit_parts) + len(target_parts)
    return pl.pallas_call(
        functools.partial(loss_kernel, len(raw_parts), len(logit_parts), len(target_parts)),
        in_specs=[pl.BlockSpec(memory_space=pltpu.SMEM)] + [pl.BlockSpec(memory_space=pltpu.VMEM)] * n_vmem,
        out_shape=[jax.ShapeDtypeStruct((rows, width), F32), jax.ShapeDtypeStruct((1, rows), F32)],
        compiler_params=params(),
        cost_estimate=cost(20 * rows * width, 24 * rows * width),
        name="loss_grad",
    )(core, *raw_parts, *logit_parts, *target_parts)


def pick_kernel(f_ref, at_ref, keep_ref, send_ref):
    n_z, height, rows = keep_ref.shape
    depth = f_ref.shape[1]
    shape = (n_z * height, depth)
    row = lax.broadcasted_iota(jnp.int32, shape, 0)
    col = lax.broadcasted_iota(jnp.int32, shape, 1)
    d_cols = depth // (2 * n_z)
    me, share = at_ref[0], at_ref[1] * height
    for out, y in ((keep_ref, me & 1), (send_ref, (me & 1) ^ 1)):
        first = jnp.zeros(shape, jnp.int32)
        for k in range(n_z):
            owner = (((me >> 1) ^ k) << 1) + y
            first = jnp.where(row >= k * height, owner * d_cols + share - k * height, first)
        chosen = jnp.where(col == first + row, 1.0, 0.0).astype(BF16)
        out[...] = dot(chosen, f_ref[...], ((1,), (1,))).reshape(n_z, height, rows)


def columns_pick(features, at, n_batch, n_proto):
    rows, depth = features.shape
    shape = jax.ShapeDtypeStruct((n_batch // 2, depth // (n_batch * n_proto), rows), F32)
    return pl.pallas_call(
        pick_kernel,
        in_specs=[pl.BlockSpec(memory_space=pltpu.VMEM), pl.BlockSpec(memory_space=pltpu.SMEM)],
        out_shape=[shape, shape],
        compiler_params=params(),
        cost_estimate=cost(2 * depth * depth // n_proto * rows, 8 * rows * depth),
        name="columns_pick",
    )(features, at)


def join_kernel(n_z, keep_ref, got_ref, *refs):
    out_ref, height = refs[-1], keep_ref.shape[1]
    out_ref[0, 0] = keep_ref[0]
    out_ref[0, 1] = got_ref[0]
    for k in range(2 * n_z - 2):
        out_ref[0, 2 + k] = refs[k][refs[k].shape[0] - height :, :]


def columns_join(keep, got, first, second):
    n_z, height, rows = keep.shape
    return pl.pallas_call(
        functools.partial(join_kernel, n_z),
        out_shape=jax.ShapeDtypeStruct((1, 2 * n_z, height, rows), F32),
        compiler_params=params(),
        cost_estimate=cost(0, 16 * n_z * height * rows),
        name="columns_join",
    )(keep, got, *[m for pair in zip(first, second) for m in pair])


def columns_kernel(masks, at_ref, *refs):
    out_ref = refs[-1]
    inner = len(masks) // (len(refs) - 1)
    for k, mask in enumerate(masks):
        _, n_batch, height, rows = refs[k // inner].shape
        row = pl.multiple_of((at_ref[1] ^ mask) * height, height)
        for i in range(n_batch):
            out_ref[at_ref[0] ^ i, pl.ds(row, height), :] = refs[k // inner][k % inner, i].astype(BF16)


def columns_all(own, other, at):
    n_proto = 2 * own.shape[0]
    _, n_batch, height, rows = own.shape
    smem = pl.BlockSpec(memory_space=pltpu.SMEM)
    vmem = pl.BlockSpec(memory_space=pltpu.VMEM)
    return pl.pallas_call(
        functools.partial(columns_kernel, (0, 2, 1, 3)),
        in_specs=[smem, vmem, vmem],
        out_shape=jax.ShapeDtypeStruct((n_batch, n_proto * height, rows), BF16),
        compiler_params=params(),
        cost_estimate=cost(0, 6 * n_proto * height * n_batch * rows),
        name="columns_all",
    )(at, own, other)


def cast_kernel(in_ref, out_ref):
    out_ref[...] = in_ref[...].T.astype(BF16)


def columns_cast(columns):
    return pl.pallas_call(
        cast_kernel,
        out_shape=jax.ShapeDtypeStruct(columns.shape[::-1], BF16),
        compiler_params=params(),
        name="columns_cast",
    )(columns)


def centre_of(sums, crops):
    return [jnp.sum(sums[k], axis=0, keepdims=True) / crops for k in range(2)]


def tail_half(refs, grads, odd, n_batch, sums_ref, centre, grad_all, low_all, cols_all, *wide):
    at_ref, pre_ref, cols_ref, stats, gain, shift, w_ref = refs
    unit, width = pre_ref.shape[1], grad_all.shape[1]
    size, n = unit // 2, n_batch // 2
    e_rows = 16 * (-(-(width // n_batch) // 16))
    for k in range(n):
        for flip in range(2):
            place = pl.multiple_of(k * unit + (at_ref[2] ^ flip) * size, size)
            own, rest = grads[2 * flip], grads[2 * flip + 1]
            grad_all[pl.ds(place, size), :] = (rest[k - 1] if k else own[0]).astype(BF16)
    mine = lax.broadcasted_iota(jnp.int32, (e_rows, width), 0) + at_ref[0] * (width // n_batch)
    chosen = jnp.where(mine == lax.broadcasted_iota(jnp.int32, (e_rows, width), 1), 1.0, 0.0).astype(BF16)
    w2 = 0.0
    for k in range(n):
        rows = slice(k * unit, (k + 1) * unit)
        block = at_ref[0] ^ (2 * k + odd)
        normed, shifted = batch_norm(pre_ref[block], stats, gain, shift)
        grad = grad_all[rows, :]
        picked = dot(chosen, grad, ((1,), (1,))).astype(BF16)
        hidden = jnp.maximum(shifted, 0.0).astype(BF16)
        w2 = w2 + jnp.dot(picked, hidden, preferred_element_type=F32)
        hidden_grad = dot(grad, w_ref[...], ((1,), (1,)))
        bn_grad = jnp.where(shifted > 0, hidden_grad, 0.0)
        sums_ref[0, pl.ds(block, 1), :] = jnp.sum(bn_grad, axis=0, keepdims=True)
        sums_ref[1, pl.ds(block, 1), :] = jnp.sum(bn_grad * normed, axis=0, keepdims=True)
        if centre is None:
            wide[0][rows, :] = bn_grad
        else:
            low_all[rows, :] = (bn_grad - centre[0] - normed * centre[1]).astype(BF16)
        cols_all[:, rows] = cols_ref[block]
    if centre is None:
        centre = centre_of(sums_ref, n * unit)
        for k in range(n):
            rows = slice(k * unit, (k + 1) * unit)
            normed, _ = batch_norm(pre_ref[at_ref[0] ^ (2 * k + odd)], stats, gain, shift)
            low_all[rows, :] = (wide[0][rows, :] - centre[0] - normed * centre[1]).astype(BF16)
    return jnp.dot(cols_all[...], low_all[...], preferred_element_type=F32), w2


def near_kernel(n_batch, n_grads, *refs):
    ins, grads, refs = refs[:7], refs[7 : 7 + n_grads], refs[7 + n_grads :]
    w1_ref, w2_ref, sums_ref, wide, *scratch = refs
    sums_ref[...] = jnp.zeros_like(sums_ref)
    ins = ins[:3] + tuple(r[...] for r in ins[3:6]) + ins[6:]
    w1_ref[...], w2_ref[...] = tail_half(ins, grads, 0, n_batch, sums_ref, None, *scratch, wide)


def far_kernel(crops_all, n_batch, n_grads, *refs):
    ins, grads, refs = refs[:7], refs[7 : 7 + n_grads], refs[7 + n_grads :]
    near_w1, near_w2, near_sums, flat_ref, total_ref = refs[:5]
    w1_ref, w2_ref, gain_grad_ref, shift_grad_ref, sums, *scratch = refs[5:]
    ins = ins[:3] + tuple(r[...] for r in ins[3:6]) + ins[6:]
    stats, gain = ins[3:5]
    sums[...] = near_sums[...]
    centre = centre_of(near_sums[...], crops_all // 2)
    w1, w2 = tail_half(ins, grads, 1, n_batch, sums, centre, *scratch)
    w2_ref[...] = (near_w2[...] + w2)[0 : w2_ref.shape[0], :]
    shift_grad = jnp.sum(sums[0], axis=0, keepdims=True)
    gain_grad = jnp.sum(sums[1], axis=0, keepdims=True)
    shift_grad_ref[...] = shift_grad
    gain_grad_ref[...] = gain_grad
    flat = total_ref[...] * (shift_grad / crops_all - centre[0])
    flat = flat + flat_ref[...] * (gain_grad / crops_all - centre[1])
    w1_ref[...] = gain * stats[1:2, :] * (near_w1[...] + w1 - flat)


def tail_call(kernel, outs, scratch, at, pre_all, columns, stats, gain, shift, w_second, grads, more, name):
    n_batch, unit, hidden = pre_all.shape
    width, d_cols = w_second.shape[1], columns.shape[1]
    crops = n_batch * unit // 2
    vmem = pl.BlockSpec(memory_space=pltpu.VMEM)
    return pl.pallas_call(
        functools.partial(kernel, n_batch, len(grads)),
        in_specs=[pl.BlockSpec(memory_space=pltpu.SMEM)] + [vmem] * (6 + len(grads) + len(more)),
        out_shape=[jax.ShapeDtypeStruct(n, F32) for n in outs],
        scratch_shapes=[pltpu.VMEM(n, F32) for n in scratch]
        + [
            pltpu.VMEM((crops, width), BF16),
            pltpu.VMEM((crops, hidden), BF16),
            pltpu.VMEM((d_cols, crops), BF16),
        ],
        compiler_params=params(20),
        cost_estimate=cost(2 * crops * hidden * (width + 256), 4 * crops * hidden),
        name=name,
    )(at, pre_all, columns, stats, gain, shift, w_second, *grads, *more)


def flat_kernel(pre_ref, cols_ref, stats_ref, gain_ref, shift_ref, flat_ref, total_ref):
    stats, gain, shift = stats_ref[...], gain_ref[...], shift_ref[...]
    total = 0.0
    for k in range(pre_ref.shape[0]):
        total = total + jnp.sum(cols_ref[k].astype(F32), axis=1, keepdims=True)
        normed, _ = batch_norm(pre_ref[k], stats, gain, shift)
        part = jnp.dot(cols_ref[k], normed.astype(BF16), preferred_element_type=F32)
        if k == 0:
            flat_ref[...] = part
        else:
            flat_ref[...] += part
    total_ref[...] = total


def flat_sums(pre_all, columns, stats, gain, shift):
    n_batch, unit, hidden = pre_all.shape
    d_cols = columns.shape[1]
    return pl.pallas_call(
        flat_kernel,
        out_shape=[jax.ShapeDtypeStruct((d_cols, hidden), F32), jax.ShapeDtypeStruct((d_cols, 1), F32)],
        compiler_params=params(20),
        cost_estimate=cost(2 * n_batch * unit * hidden * d_cols, 4 * n_batch * unit * hidden),
        name="flat_sums",
    )(pre_all, columns, stats, gain, shift)


def whole_tail_kernel(crops_all, e_cols, *refs):
    at_ref, pre_ref, cols_ref, stats_ref, gain_ref, shift_ref, w_ref, raw_ref = refs[:8]
    w1_ref, w2_ref, gain_grad_ref, shift_grad_ref, grad_all, grad_cols = refs[8:]

    @pl.when(pl.program_id(0) == 0)
    def _():
        grad_all[...] = raw_ref[...].astype(BF16)
        shape = (grad_cols.shape[0], grad_all.shape[1])
        mine = lax.broadcasted_iota(jnp.int32, shape, 0) + at_ref[0] * e_cols
        chosen = jnp.where(mine == lax.broadcasted_iota(jnp.int32, shape, 1), 1.0, 0.0).astype(BF16)
        grad_cols[...] = dot(chosen, grad_all[...], ((1,), (1,))).astype(BF16)

    stats, gain = stats_ref[...], gain_ref[...]
    normed, shifted = batch_norm(pre_ref[...], stats, gain, shift_ref[...])
    hidden = jnp.maximum(shifted, 0.0).astype(BF16)
    w2_ref[...] = jnp.dot(grad_cols[...], hidden, preferred_element_type=F32)[0:e_cols, :]
    hidden_grad = dot(grad_all[...], w_ref[...], ((1,), (1,)))
    bn_grad = jnp.where(shifted > 0, hidden_grad, 0.0)
    shift_grad = jnp.sum(bn_grad, axis=0, keepdims=True)
    gain_grad = jnp.sum(bn_grad * normed, axis=0, keepdims=True)
    shift_grad_ref[...] = shift_grad
    gain_grad_ref[...] = gain_grad
    scale = gain * stats[1:2, :]
    pre_grad = scale * (bn_grad - shift_grad / crops_all - normed * (gain_grad / crops_all))
    w1_ref[...] = jnp.dot(cols_ref[...], pre_grad.astype(BF16), preferred_element_type=F32)


def whole_tail(pre_all, columns, stats, gain, shift, w_second, raw, at, e_cols):
    crops_all, hidden = pre_all.shape
    width, d_cols = w_second.shape[1], columns.shape[0]
    blk = min(hidden, max(128, 256 * 1024 // crops_all))
    smem = pl.BlockSpec(memory_space=pltpu.SMEM)
    vmem = pl.BlockSpec(memory_space=pltpu.VMEM)

    def cols(n):
        return pl.BlockSpec((n, blk), lambda j: (0, j))

    return pl.pallas_call(
        functools.partial(whole_tail_kernel, crops_all, e_cols),
        grid=(hidden // blk,),
        in_specs=[smem, cols(crops_all), vmem, cols(2), cols(1), cols(1)]
        + [pl.BlockSpec((blk, width), lambda j: (j, 0)), vmem],
        out_specs=[cols(d_cols), cols(e_cols), cols(1), cols(1)],
        out_shape=[jax.ShapeDtypeStruct((n, hidden), F32) for n in (d_cols, e_cols, 1, 1)],
        scratch_shapes=[
            pltpu.VMEM((crops_all, width), BF16),
            pltpu.VMEM((-(-e_cols // 16) * 16, crops_all), BF16),
        ],
        compiler_params=params(58),
        cost_estimate=cost(2 * crops_all * hidden * (width + d_cols), 4 * crops_all * hidden),
        name="whole_tail",
    )(at, pre_all, columns, stats, gain, shift, w_second, raw)


def after(value, *others):
    return lax.optimization_barrier((value,) + others)[0]


def body(features, w_first, bn_gain, bn_shift, w_second, prototypes, partner):
    n_batch, n_proto = lax.axis_size("batch"), lax.axis_size("proto")
    me, proto_me = lax.axis_index("batch").astype(jnp.int32), lax.axis_index("proto").astype(jnp.int32)
    rows, depth = features.shape
    width = w_second.shape[1]
    crops_all = rows * n_batch
    d_cols, e_cols = depth // n_batch, width // n_batch
    gain, shift = bn_gain[None, :], bn_shift[None, :]
    short = n_batch == 8 and n_proto == 4 and depth % 512 == 0
    at = jnp.stack([me, proto_me, proto_me & 1 if short else proto_me * 0])

    pre, pre_again, moments = first_layer(features, w_first, n_batch if short else 1)
    pre_all = lax.all_gather(pre, "batch", tiled=True)
    moment_parts = [lax.all_to_all(moments, "batch", 0, 0)] if short else batch_parts(moments)
    units = unit_rows(prototypes)
    emb_part, stats = second_layer(crops_all, moment_parts, pre_again, gain, shift, w_second)
    first, emb_part = lax.optimization_barrier((at[2] == 0, emb_part))
    raw_parts = proto_parts(emb_part)
    if short:
        keep, send = columns_pick(after(features, emb_part), at, n_batch, n_proto)
        raw_parts[0], keep, send, units = lax.optimization_barrier((raw_parts[0], keep, send, units))
    embedded = embed_rows(raw_parts)

    if short:
        partner_emb = swap(embedded, "batch", 1)
        own_codes, own_col = score(embedded, units)
        logit = logit_sum(embedded, units)
        partner_emb, own_col, logit = lax.optimization_barrier((partner_emb, own_col, logit))
        logit = logit + swap(logit, "proto", 1)
        more_codes, *cols = score(partner_emb, units, (own_col, keep))
        cols[0], logit = lax.optimization_barrier((cols[0], logit))
        codes = [own_codes, more_codes]
    else:
        codes, *cols = score(embedded, units)
        codes = [codes]
        logit = logit_sum(embedded, units)
    moved = []
    for iteration in range(ITERS):
        if short and iteration < 2:
            moved.append([swap(c, "batch", 2 * k + 2) for k, c in enumerate(cols[1:])])
            col_parts = [cols[0]] + moved[-1]
        else:
            col_parts = batch_parts(cols[0], 2 if short else 1)
        if iteration == 0:
            logit_parts = proto_parts(logit, 2 if short else 1)
            col_parts[0], *logit_parts = lax.optimization_barrier((col_parts[0], *logit_parts))
        if short and iteration == 0:
            got = swap(after(send, cols[0]), "batch", 1)
            col_parts[0], got = lax.optimization_barrier((col_parts[0], got))
        if short and iteration == 2:
            columns = columns_join(after(keep, cols[0]), got, *moved)
            columns = [columns, swap(columns, "proto", 2)]
            col_parts[0], *columns = lax.optimization_barrier((col_parts[0], *columns))
        if iteration < ITERS - 1:
            row_parts = proto_small(row_pass(col_parts, codes))
            cols = col_pass(row_parts, codes, got if short and iteration == 0 else None)
    if short:
        own_half, send = target_sum(col_parts, codes[0], units, partner[None, :], at, 2)
        columns = after(jnp.concatenate(columns), own_half)
        own_half = own_half + swap(send, "proto", 1)
        columns = [columns, swap(columns, "proto", 1)]
        target_parts = proto_parts(own_half, 2)
        columns = columns_all(*columns, at)
        target_parts[0], columns = lax.optimization_barrier((target_parts[0], columns))
    else:
        target_parts = proto_parts(target_sum(col_parts, codes[0], units, partner[None, :], at, 1)[0])
    raw_grad, penalty = loss_grad(raw_parts, logit_parts, target_parts, at)

    if short:
        pre_all = after(pre_all, raw_grad)
        ins = (at, pre_all.reshape(n_batch, rows, -1), columns, stats, gain, shift, w_second)
        e_rows, hidden = -(-e_cols // 16) * 16, w_second.shape[0]
        table = (2, n_batch, hidden)
        flat = flat_sums(*ins[1:-1])
        own = raw_grad[None]
        rest = [swap(raw_grad, "batch", k) for k in (2, 4, 6)]
        rest = jnp.stack([rest[0]] + [after(piece, *flat) for piece in rest[1:]])
        far_own, own_core = swap(own, "batch", 1), swap(own, "proto", 1)
        far_own_core = swap(far_own, "proto", 1)
        rest, far_own, own_core, far_own_core = lax.optimization_barrier((rest, far_own, own_core, far_own_core))
        far, rest_core = swap(rest, "batch", 1), swap(rest, "proto", 1)
        other_penalty = swap(after(penalty, rest), "proto", 1)
        penalty = jnp.concatenate(
            [jnp.where(first, penalty, other_penalty), jnp.where(first, other_penalty, penalty)], axis=1
        )
        half = tail_call(
            near_kernel, [(d_cols, hidden), (e_rows, hidden), table], [(crops_all // 2, hidden)],
            *ins, [own, rest, own_core, rest_core], [], "tail_near",
        )
        far, penalty, *half = lax.optimization_barrier((far, penalty, *half, *flat))
        grad_w1, grad_w2, grad_gain, grad_shift = tail_call(
            functools.partial(far_kernel, crops_all),
            [(d_cols, hidden), (e_cols, hidden), (1, hidden), (1, hidden)], [table],
            *ins, [far_own, far, far_own_core, swap(far, "proto", 1)], half, "tail_far",
        )
    else:
        by_owner = jnp.swapaxes(features.astype(F32).reshape(rows, n_batch, d_cols), 0, 1)
        columns = columns_cast(lax.all_to_all(by_owner, "batch", 0, 0).reshape(crops_all, d_cols))
        raw_all = lax.all_gather(raw_grad, "batch", tiled=True)
        grad_w1, grad_w2, grad_gain, grad_shift = whole_tail(
            pre_all, columns, stats, gain, shift, w_second, raw_all, at, e_cols
        )
    return (penalty[0], grad_w1, grad_gain[0], grad_shift[0], grad_w2.T)


def solution(mesh):
    return jax.shard_map(
        body,
        mesh=mesh,
        in_specs=(
            P("batch", None),
            P(None, "proto"),
            P("proto"),
            P("proto"),
            P("proto", None),
            P("proto", None),
            P("batch"),
        ),
        out_specs=(P("batch"), P("batch", "proto"), P("proto"), P("proto"), P("proto", "batch")),
        check_vma=False,
    )
```

```python
import functools

import jax
import jax.numpy as jnp
from jax import lax
from jax.experimental import pallas as pl
from jax.experimental.pallas import tpu as pltpu
from jax.sharding import PartitionSpec as P

ITERS = 3
F32 = jnp.float32
BF16 = jnp.bfloat16
HIGHEST = lax.Precision.HIGHEST

balancing_epsilon = 0.05
sharpness_divisor = 0.1
penalty_weighting = 64.0


def stages(n, first, stride=1):
    out, radix = [], first
    while stride < n:
        radix = min(radix, n // stride)
        out.append((stride, radix))
        stride *= radix
        radix = 4 if (n // stride) % 4 == 0 else 2
    return out


def swap(v, axis, mask):
    n = lax.axis_size(axis)
    return lax.ppermute(v, axis, [(i, i ^ mask) for i in range(n)])


def add_parts(parts):
    if len(parts) == 4:
        return (parts[0] + parts[1]) + (parts[2] + parts[3])
    return functools.reduce(lambda x, y: x + y, parts)


def exchange(v, axis, first, stride=1):
    n = lax.axis_size(axis)
    parts = [v]
    for step, radix in stages(n, first, stride):
        v = add_parts(parts)
        parts = [v] + [swap(v, axis, k * step) for k in range(1, radix)]
    return parts


def batch_parts(v, stride=1):
    steps = (lax.axis_size("batch") // stride).bit_length() - 1
    return exchange(v, "batch", 2 if steps % 2 else 4, stride)


def proto_parts(v, stride=1):
    return exchange(v, "proto", 2, stride)


def proto_small(v):
    return exchange(v, "proto", 4 if lax.axis_size("proto") == 4 else 2)


def whole(shape):
    return pl.BlockSpec(shape, lambda *_: (0,) * len(shape))


def params(mib=24):
    return pltpu.CompilerParams(vmem_limit_bytes=mib * 1024 * 1024)


def cost(flops, nbytes, trans=0):
    return pl.CostEstimate(flops=int(flops), bytes_accessed=int(nbytes), transcendentals=int(trans))


def dot(a, b, dims, precision=None):
    return lax.dot_general(a, b, ((dims[0], dims[1]), ((), ())), precision=precision, preferred_element_type=F32)


def eye(n):
    return lax.broadcasted_iota(jnp.int32, (n, n), 0) == lax.broadcasted_iota(jnp.int32, (n, n), 1)


def to_lanes(col):
    n = col.shape[0]
    return jnp.sum(jnp.where(eye(n), col, 0.0), axis=0, keepdims=True)


def to_column(row):
    n = row.shape[1]
    return jnp.sum(jnp.where(eye(n), row, 0.0), axis=1, keepdims=True)


def first_kernel(f_hbm, w_hbm, pre_ref, again_ref, mom_ref, f_ref, w_ref, sems):
    depth, hidden = w_ref.shape
    n = sems.shape[0] - 1
    step = depth // n
    copies = [pltpu.make_async_copy(f_hbm, f_ref, sems.at[n])]
    for k in range(n):
        at = pl.ds(k * step, step)
        copies.append(pltpu.make_async_copy(w_hbm.at[at, :], w_ref.at[at, :], sems.at[k]))
    for copy in copies:
        copy.start()
    copies[0].wait()
    for k in range(n):
        copies[k + 1].wait()
        at = slice(k * step, (k + 1) * step)
        part = jnp.dot(f_ref[:, at], w_ref[at, :], preferred_element_type=F32)
        if k == 0:
            pre_ref[...] = part
        else:
            pre_ref[...] += part
    pre = pre_ref[...]
    again_ref[...] = pre
    first = jnp.sum(pre, axis=0, keepdims=True)
    second = jnp.sum(pre * pre, axis=0, keepdims=True)
    for k in range(mom_ref.shape[0]):
        mom_ref[k, :, 0:hidden] = first
        mom_ref[k, :, hidden:] = second


def first_layer(features, w_first, spread):
    rows, depth = features.shape
    hidden = w_first.shape[1]
    steps = 6 if depth % (6 * 128) == 0 else 1
    return pl.pallas_call(
        first_kernel,
        in_specs=[pl.BlockSpec(memory_space=pl.ANY)] * 2,
        out_shape=[jax.ShapeDtypeStruct((rows, hidden), F32)] * 2
        + [jax.ShapeDtypeStruct((spread, 1, 2 * hidden), F32)],
        scratch_shapes=[
            pltpu.VMEM((rows, depth), BF16),
            pltpu.VMEM((depth, hidden), BF16),
            pltpu.SemaphoreType.DMA((steps + 1,)),
        ],
        compiler_params=params(52),
        cost_estimate=cost(2 * rows * depth * hidden, 2 * depth * hidden + 4 * rows * hidden),
        name="first_layer",
    )(features, w_first)


def batch_norm(pre, stats, gain, shift):
    normed = (pre - stats[0:1, :]) * stats[1:2, :]
    return normed, gain * normed + shift


def second_kernel(crops_all, n_parts, *refs):
    parts = refs[:n_parts]
    pre_ref, gain_ref, shift_ref, w_ref, emb_ref, stats_ref = refs[n_parts:]
    hidden = pre_ref.shape[1]
    moments = add_parts([p[k] for p in parts for k in range(p.shape[0])]) / crops_all
    mean = moments[:, 0:hidden]
    var = moments[:, hidden:] - mean * mean
    stats_ref[0:1, :] = mean
    stats_ref[1:2, :] = lax.rsqrt(var + 1e-05)
    _, shifted = batch_norm(pre_ref[...], stats_ref[...], gain_ref[...], shift_ref[...])
    low = jnp.maximum(shifted, 0.0).astype(BF16)
    emb_ref[...] = jnp.dot(low, w_ref[...], preferred_element_type=F32)


def second_layer(crops_all, parts, pre, gain, shift, w_second):
    rows, hidden = pre.shape
    width = w_second.shape[1]
    return pl.pallas_call(
        functools.partial(second_kernel, crops_all, len(parts)),
        out_shape=[jax.ShapeDtypeStruct((rows, width), F32), jax.ShapeDtypeStruct((2, hidden), F32)],
        compiler_params=params(),
        cost_estimate=cost(2 * rows * hidden * width, 4 * rows * hidden + 2 * hidden * width),
        name="second_layer",
    )(*parts, pre, gain, shift, w_second)


def unit_kernel(p_ref, u_ref):
    wide = p_ref[...].astype(F32)
    u_ref[...] = (wide * lax.rsqrt(jnp.sum(wide * wide, 1, keepdims=True) + 1e-06)).astype(BF16)


def unit_rows(prototypes):
    rows, width = prototypes.shape
    blk = min(1024, rows)
    return pl.pallas_call(
        unit_kernel,
        grid=(rows // blk,),
        in_specs=[pl.BlockSpec((blk, width), lambda j: (j, 0))],
        out_specs=pl.BlockSpec((blk, width), lambda j: (j, 0)),
        out_shape=jax.ShapeDtypeStruct((rows, width), BF16),
        compiler_params=params(),
        cost_estimate=cost(4 * rows * width, 4 * rows * width),
        name="unit_rows",
    )(prototypes)


def embed(raw):
    inv_norm = lax.rsqrt(jnp.sum(raw * raw, 1, keepdims=True) + 1e-06)
    return raw * inv_norm, inv_norm


def embed_kernel(*refs):
    refs[-1][...] = embed(add_parts([p[...] for p in refs[:-1]]))[0]


def embed_rows(parts):
    return pl.pallas_call(
        embed_kernel,
        out_shape=jax.ShapeDtypeStruct(parts[0].shape, F32),
        compiler_params=params(),
        cost_estimate=cost(8 * parts[0].size, 12 * parts[0].size),
        name="embed_rows",
    )(*parts)


def put_blocks(out_ref, row, value):
    for k in range(value.shape[1] // 128):
        out_ref[row + k : row + k + 1, :] = value[:, k * 128 : (k + 1) * 128]


def score_kernel(n, *refs):
    piece, u_ref = refs[:2]
    code_ref, col_ref = refs[-2:] if n == 0 else refs[4:6]
    low = piece[...].astype(BF16)
    protos = u_ref.shape[0]
    step = min(512, protos)
    for j in range(protos // step):
        at = slice(j * step, (j + 1) * step)
        code = jnp.exp(dot(low, u_ref[at, :], ((1,), (1,))) / balancing_epsilon)
        code_ref[:, at] = code
        put_blocks(col_ref, j * step // 128, jnp.sum(code, axis=0, keepdims=True))
    if n:
        col_ref[...] += refs[2][...]
        lines = col_ref.shape[0]
        for k, out in enumerate(refs[6:]):
            out[0:lines, :] = col_ref[...]
            out[lines:, :] = refs[3][k + 1]


def score(piece, units, more=None):
    rows, width = piece.shape
    protos = units.shape[0]
    lines = protos // 128
    n, extra = 0, ()
    out_shape = [jax.ShapeDtypeStruct((rows, protos), F32), jax.ShapeDtypeStruct((lines, 128), F32)]
    if more is not None:
        n, extra = more[1].shape[0] - 1, more
        out_shape += [jax.ShapeDtypeStruct((lines + more[1].shape[1], 128), F32)] * n
    return pl.pallas_call(
        functools.partial(score_kernel, n),
        out_shape=out_shape,
        compiler_params=params(),
        cost_estimate=cost(2 * rows * protos * width, 4 * rows * protos, rows * protos),
        name="score",
    )(piece, units, *extra)


def col_scale(parts):
    lines = parts[0].shape[0]
    return 1.0 / add_parts([p[0:lines, :] for p in parts])


def pack(table, lane_row, out_ref):
    rows, width = table.shape
    out_ref[0:rows, :] = table
    out_ref[rows:, :] = jnp.zeros((8, width), F32)
    out_ref[rows : rows + 1, 0:rows] = lane_row


def logit_kernel(emb_ref, u_ref, out_ref):
    low = emb_ref[...].astype(BF16)
    protos = u_ref.shape[0]
    step = min(512, protos)
    total, mass = 0.0, 0.0
    for j in range(protos // step):
        units = u_ref[j * step : (j + 1) * step, :]
        logits = jnp.exp(dot(low, units, ((1,), (1,))) / sharpness_divisor)
        total = total + jnp.dot(logits.astype(BF16), units, preferred_element_type=F32)
        mass = mass + jnp.sum(logits, axis=1, keepdims=True)
    pack(total, to_lanes(mass), out_ref)


def logit_sum(embedded, units):
    rows, width = embedded.shape
    protos = units.shape[0]
    return pl.pallas_call(
        logit_kernel,
        out_shape=jax.ShapeDtypeStruct((rows + 8, width), F32),
        compiler_params=params(),
        cost_estimate=cost(4 * rows * protos * width, 2 * protos * width, rows * protos),
        name="logit_sum",
    )(embedded, units)


def row_kernel(n_parts, *refs):
    parts, codes, out_ref = refs[:n_parts], refs[n_parts:-1], refs[-1]
    scale = col_scale(parts)
    for k, code in enumerate(codes):
        total = 0.0
        for j in range(scale.shape[0]):
            total = total + code[:, j * 128 : (j + 1) * 128] * scale[j : j + 1, :]
        out_ref[k : k + 1, :] = to_lanes(jnp.sum(total, axis=1, keepdims=True))


def row_pass(parts, codes):
    rows, protos = codes[0].shape
    n = len(codes)
    return pl.pallas_call(
        functools.partial(row_kernel, len(parts)),
        out_shape=jax.ShapeDtypeStruct((n, rows), F32),
        compiler_params=params(),
        cost_estimate=cost(2 * n * rows * protos, 4 * n * rows * protos),
        name="row_pass",
    )(*parts, *codes)


def col_kernel(n_parts, n_codes, *refs):
    parts, codes, refs = refs[:n_parts], refs[n_parts : n_parts + n_codes], refs[n_parts + n_codes :]
    scale = 1.0 / add_parts([p[...] for p in parts])
    total = 0.0
    for k, code in enumerate(codes):
        total = total + jnp.sum(code[...] * to_column(scale[k : k + 1, :]), axis=0, keepdims=True)
    if len(refs) == 1:
        put_blocks(refs[0], 0, total)
    else:
        put_blocks(refs[1], 0, total)
        for k, out in enumerate(refs[2:]):
            out[0 : refs[1].shape[0], :] = refs[1][...]
            out[refs[1].shape[0] :, :] = refs[0][k + 1]


def col_pass(parts, codes, columns=None):
    rows, protos = codes[0].shape
    n = len(codes)
    lines = protos // 128
    extra = () if columns is None else (columns,)
    shapes = [(lines, 128)] + [(lines + c.shape[1], 128) for c in extra for _ in range(c.shape[0] - 1)]
    return pl.pallas_call(
        functools.partial(col_kernel, len(parts), n),
        out_shape=[jax.ShapeDtypeStruct(shape, F32) for shape in shapes],
        compiler_params=params(),
        cost_estimate=cost(2 * n * rows * protos, 4 * n * rows * protos),
        name="col_pass",
    )(*parts, *codes, *extra)


def target_kernel(n_parts, halves, *refs):
    parts = refs[:n_parts]
    codes_ref, u_ref, partner_ref, at_ref = refs[n_parts : n_parts + 4]
    outs, table_all, mass_all, low = refs[n_parts + 4 : -3], refs[-3], refs[-2], refs[-1]
    rows = codes_ref.shape[0]
    scale = col_scale(parts)
    total = 0.0
    for j in range(scale.shape[0]):
        weighted = codes_ref[:, j * 128 : (j + 1) * 128] * scale[j : j + 1, :]
        low[:, j * 128 : (j + 1) * 128] = weighted.astype(BF16)
        total = total + weighted
    mass = jnp.sum(total, axis=1, keepdims=True)
    table = jnp.dot(low[...], u_ref[...], preferred_element_type=F32)
    chosen = partner_ref[...] == lax.broadcasted_iota(jnp.int32, (rows, rows), 0)
    table_all[...] = dot(jnp.where(chosen, 1.0, 0.0).astype(F32), table, ((1,), (0,)), HIGHEST)
    mass_all[...] = jnp.sum(jnp.where(chosen, to_lanes(mass), 0.0), axis=1, keepdims=True)
    size = rows // halves
    for k in range(halves):
        at = pl.ds(pl.multiple_of((at_ref[2] ^ k) * size, size), size)
        pack(table_all[at, :], to_lanes(mass_all[at, :]), outs[k])


def target_sum(parts, codes, units, partner, at, halves):
    rows, protos = codes.shape
    width = units.shape[1]
    n_vmem = len(parts) + 3
    return pl.pallas_call(
        functools.partial(target_kernel, len(parts), halves),
        in_specs=[pl.BlockSpec(memory_space=pltpu.VMEM)] * n_vmem + [pl.BlockSpec(memory_space=pltpu.SMEM)],
        out_shape=[jax.ShapeDtypeStruct((rows // halves + 8, width), F32)] * halves,
        scratch_shapes=[
            pltpu.VMEM((rows, width), F32),
            pltpu.VMEM((rows, 1), F32),
            pltpu.VMEM((rows, protos), BF16),
        ],
        compiler_params=params(),
        cost_estimate=cost(2 * rows * protos * width, 4 * rows * protos + 2 * protos * width),
        name="target_sum",
    )(*parts, codes, units, partner, at)


def loss_kernel(n_raw, n_logit, n_target, *refs):
    core_ref, refs = refs[0], refs[1:]
    raws, refs = refs[:n_raw], refs[n_raw:]
    logits, refs = refs[:n_logit], refs[n_logit:]
    target = add_parts([p[...] for p in refs[:n_target]])
    grad_ref, loss_ref = refs[n_target:]
    rows = raws[0].shape[0]
    size = grad_ref.shape[0]
    at = pl.ds(pl.multiple_of(core_ref[2] * size, size), size)
    raw = add_parts([p[at, :] for p in raws])
    logit = add_parts([p[at, :] for p in logits])
    denoms = to_column(add_parts([p[rows : rows + 1, 0:rows] for p in logits]))
    denom = jnp.where(core_ref[2] == 0, denoms[0:size], denoms[rows - size :])
    embedded, inv_norm = embed(raw)
    row_scale = to_column(1.0 / target[size : size + 1, 0:size])
    wanted = target[0:size, :] * row_scale
    emb_low = embedded.astype(BF16).astype(F32)
    cross = jnp.sum(wanted * emb_low, axis=1, keepdims=True)
    loss_ref[...] = to_lanes(jnp.log(denom) - cross / sharpness_divisor)
    emb_grad = penalty_weighting * (logit / denom - wanted) / sharpness_divisor
    inner = jnp.sum(embedded * emb_grad, 1, keepdims=True)
    grad_ref[...] = (emb_grad - embedded * inner) * inv_norm


def loss_grad(raw_parts, logit_parts, target_parts, core):
    width = raw_parts[0].shape[1]
    rows = target_parts[0].shape[0] - 8
    n_vmem = len(raw_parts) + len(logit_parts) + len(target_parts)
    return pl.pallas_call(
        functools.partial(loss_kernel, len(raw_parts), len(logit_parts), len(target_parts)),
        in_specs=[pl.BlockSpec(memory_space=pltpu.SMEM)] + [pl.BlockSpec(memory_space=pltpu.VMEM)] * n_vmem,
        out_shape=[jax.ShapeDtypeStruct((rows, width), F32), jax.ShapeDtypeStruct((1, rows), F32)],
        compiler_params=params(),
        cost_estimate=cost(20 * rows * width, 24 * rows * width),
        name="loss_grad",
    )(core, *raw_parts, *logit_parts, *target_parts)


def pick_kernel(f_ref, at_ref, keep_ref, send_ref):
    n_z, height, rows = keep_ref.shape
    depth = f_ref.shape[1]
    shape = (n_z * height, depth)
    row = lax.broadcasted_iota(jnp.int32, shape, 0)
    col = lax.broadcasted_iota(jnp.int32, shape, 1)
    d_cols = depth // (2 * n_z)
    me, share = at_ref[0], at_ref[1] * height
    for out, y in ((keep_ref, me & 1), (send_ref, (me & 1) ^ 1)):
        first = jnp.zeros(shape, jnp.int32)
        for k in range(n_z):
            owner = (((me >> 1) ^ k) << 1) + y
            first = jnp.where(row >= k * height, owner * d_cols + share - k * height, first)
        chosen = jnp.where(col == first + row, 1.0, 0.0).astype(BF16)
        out[...] = dot(chosen, f_ref[...], ((1,), (1,))).reshape(n_z, height, rows)


def columns_pick(features, at, n_batch, n_proto):
    rows, depth = features.shape
    shape = jax.ShapeDtypeStruct((n_batch // 2, depth // (n_batch * n_proto), rows), F32)
    return pl.pallas_call(
        pick_kernel,
        in_specs=[pl.BlockSpec(memory_space=pltpu.VMEM), pl.BlockSpec(memory_space=pltpu.SMEM)],
        out_shape=[shape, shape],
        compiler_params=params(),
        cost_estimate=cost(2 * depth * depth // n_proto * rows, 8 * rows * depth),
        name="columns_pick",
    )(features, at)


def join_kernel(n_z, keep_ref, got_ref, *refs):
    out_ref, height = refs[-1], keep_ref.shape[1]
    out_ref[0, 0] = keep_ref[0]
    out_ref[0, 1] = got_ref[0]
    for k in range(2 * n_z - 2):
        out_ref[0, 2 + k] = refs[k][refs[k].shape[0] - height :, :]


def columns_join(keep, got, first, second):
    n_z, height, rows = keep.shape
    return pl.pallas_call(
        functools.partial(join_kernel, n_z),
        out_shape=jax.ShapeDtypeStruct((1, 2 * n_z, height, rows), F32),
        compiler_params=params(),
        cost_estimate=cost(0, 16 * n_z * height * rows),
        name="columns_join",
    )(keep, got, *[m for pair in zip(first, second) for m in pair])


def columns_kernel(masks, at_ref, *refs):
    out_ref = refs[-1]
    inner = len(masks) // (len(refs) - 1)
    for k, mask in enumerate(masks):
        _, n_batch, height, rows = refs[k // inner].shape
        row = pl.multiple_of((at_ref[1] ^ mask) * height, height)
        for i in range(n_batch):
            out_ref[at_ref[0] ^ i, pl.ds(row, height), :] = refs[k // inner][k % inner, i].astype(BF16)


def columns_all(own, other, at):
    n_proto = 2 * own.shape[0]
    _, n_batch, height, rows = own.shape
    smem = pl.BlockSpec(memory_space=pltpu.SMEM)
    vmem = pl.BlockSpec(memory_space=pltpu.VMEM)
    return pl.pallas_call(
        functools.partial(columns_kernel, (0, 2, 1, 3)),
        in_specs=[smem, vmem, vmem],
        out_shape=jax.ShapeDtypeStruct((n_batch, n_proto * height, rows), BF16),
        compiler_params=params(),
        cost_estimate=cost(0, 6 * n_proto * height * n_batch * rows),
        name="columns_all",
    )(at, own, other)


def cast_kernel(in_ref, out_ref):
    out_ref[...] = in_ref[...].T.astype(BF16)


def columns_cast(columns):
    return pl.pallas_call(
        cast_kernel,
        out_shape=jax.ShapeDtypeStruct(columns.shape[::-1], BF16),
        compiler_params=params(),
        name="columns_cast",
    )(columns)


def centre_of(sums, crops):
    return [jnp.sum(sums[k], axis=0, keepdims=True) / crops for k in range(2)]


def tail_half(refs, grads, odd, n_batch, sums_ref, centre, grad_all, low_all, cols_all, *wide):
    at_ref, pre_ref, cols_ref, stats, gain, shift, w_ref = refs
    unit, width = pre_ref.shape[1], grad_all.shape[1]
    size, n = unit // 2, n_batch // 2
    e_rows = 16 * (-(-(width // n_batch) // 16))
    for k in range(n):
        for flip in range(2):
            place = pl.multiple_of(k * unit + (at_ref[2] ^ flip) * size, size)
            own, rest = grads[2 * flip], grads[2 * flip + 1]
            grad_all[pl.ds(place, size), :] = (rest[k - 1] if k else own[0]).astype(BF16)
    mine = lax.broadcasted_iota(jnp.int32, (e_rows, width), 0) + at_ref[0] * (width // n_batch)
    chosen = jnp.where(mine == lax.broadcasted_iota(jnp.int32, (e_rows, width), 1), 1.0, 0.0).astype(BF16)
    w2 = 0.0
    for k in range(n):
        rows = slice(k * unit, (k + 1) * unit)
        block = at_ref[0] ^ (2 * k + odd)
        normed, shifted = batch_norm(pre_ref[block], stats, gain, shift)
        grad = grad_all[rows, :]
        picked = dot(chosen, grad, ((1,), (1,))).astype(BF16)
        hidden = jnp.maximum(shifted, 0.0).astype(BF16)
        w2 = w2 + jnp.dot(picked, hidden, preferred_element_type=F32)
        hidden_grad = dot(grad, w_ref[...], ((1,), (1,)))
        bn_grad = jnp.where(shifted > 0, hidden_grad, 0.0)
        sums_ref[0, pl.ds(block, 1), :] = jnp.sum(bn_grad, axis=0, keepdims=True)
        sums_ref[1, pl.ds(block, 1), :] = jnp.sum(bn_grad * normed, axis=0, keepdims=True)
        if centre is None:
            wide[0][rows, :] = bn_grad
        else:
            low_all[rows, :] = (bn_grad - centre[0] - normed * centre[1]).astype(BF16)
        cols_all[:, rows] = cols_ref[block]
    if centre is None:
        centre = centre_of(sums_ref, n * unit)
        for k in range(n):
            rows = slice(k * unit, (k + 1) * unit)
            normed, _ = batch_norm(pre_ref[at_ref[0] ^ (2 * k + odd)], stats, gain, shift)
            low_all[rows, :] = (wide[0][rows, :] - centre[0] - normed * centre[1]).astype(BF16)
    return jnp.dot(cols_all[...], low_all[...], preferred_element_type=F32), w2


def near_kernel(n_batch, n_grads, *refs):
    ins, grads, refs = refs[:7], refs[7 : 7 + n_grads], refs[7 + n_grads :]
    w1_ref, w2_ref, sums_ref, wide, *scratch = refs
    sums_ref[...] = jnp.zeros_like(sums_ref)
    ins = ins[:3] + tuple(r[...] for r in ins[3:6]) + ins[6:]
    w1_ref[...], w2_ref[...] = tail_half(ins, grads, 0, n_batch, sums_ref, None, *scratch, wide)


def far_kernel(crops_all, n_batch, n_grads, *refs):
    ins, grads, refs = refs[:7], refs[7 : 7 + n_grads], refs[7 + n_grads :]
    near_w1, near_w2, near_sums, flat_ref, total_ref = refs[:5]
    w1_ref, w2_ref, gain_grad_ref, shift_grad_ref, sums, *scratch = refs[5:]
    ins = ins[:3] + tuple(r[...] for r in ins[3:6]) + ins[6:]
    stats, gain = ins[3:5]
    sums[...] = near_sums[...]
    centre = centre_of(near_sums[...], crops_all // 2)
    w1, w2 = tail_half(ins, grads, 1, n_batch, sums, centre, *scratch)
    w2_ref[...] = (near_w2[...] + w2)[0 : w2_ref.shape[0], :]
    shift_grad = jnp.sum(sums[0], axis=0, keepdims=True)
    gain_grad = jnp.sum(sums[1], axis=0, keepdims=True)
    shift_grad_ref[...] = shift_grad
    gain_grad_ref[...] = gain_grad
    flat = total_ref[...] * (shift_grad / crops_all - centre[0])
    flat = flat + flat_ref[...] * (gain_grad / crops_all - centre[1])
    w1_ref[...] = gain * stats[1:2, :] * (near_w1[...] + w1 - flat)


def tail_call(kernel, outs, scratch, at, pre_all, columns, stats, gain, shift, w_second, grads, more, name):
    n_batch, unit, hidden = pre_all.shape
    width, d_cols = w_second.shape[1], columns.shape[1]
    crops = n_batch * unit // 2
    vmem = pl.BlockSpec(memory_space=pltpu.VMEM)
    return pl.pallas_call(
        functools.partial(kernel, n_batch, len(grads)),
        in_specs=[pl.BlockSpec(memory_space=pltpu.SMEM)] + [vmem] * (6 + len(grads) + len(more)),
        out_shape=[jax.ShapeDtypeStruct(n, F32) for n in outs],
        scratch_shapes=[pltpu.VMEM(n, F32) for n in scratch]
        + [
            pltpu.VMEM((crops, width), BF16),
            pltpu.VMEM((crops, hidden), BF16),
            pltpu.VMEM((d_cols, crops), BF16),
        ],
        compiler_params=params(20),
        cost_estimate=cost(2 * crops * hidden * (width + 256), 4 * crops * hidden),
        name=name,
    )(at, pre_all, columns, stats, gain, shift, w_second, *grads, *more)


def flat_kernel(pre_ref, cols_ref, stats_ref, gain_ref, shift_ref, flat_ref, total_ref):
    stats, gain, shift = stats_ref[...], gain_ref[...], shift_ref[...]
    total = 0.0
    for k in range(pre_ref.shape[0]):
        total = total + jnp.sum(cols_ref[k].astype(F32), axis=1, keepdims=True)
        normed, _ = batch_norm(pre_ref[k], stats, gain, shift)
        part = jnp.dot(cols_ref[k], normed.astype(BF16), preferred_element_type=F32)
        if k == 0:
            flat_ref[...] = part
        else:
            flat_ref[...] += part
    total_ref[...] = total


def flat_sums(pre_all, columns, stats, gain, shift):
    n_batch, unit, hidden = pre_all.shape
    d_cols = columns.shape[1]
    return pl.pallas_call(
        flat_kernel,
        out_shape=[jax.ShapeDtypeStruct((d_cols, hidden), F32), jax.ShapeDtypeStruct((d_cols, 1), F32)],
        compiler_params=params(20),
        cost_estimate=cost(2 * n_batch * unit * hidden * d_cols, 4 * n_batch * unit * hidden),
        name="flat_sums",
    )(pre_all, columns, stats, gain, shift)


def whole_tail_kernel(crops_all, e_cols, *refs):
    at_ref, pre_ref, cols_ref, stats_ref, gain_ref, shift_ref, w_ref, raw_ref = refs[:8]
    w1_ref, w2_ref, gain_grad_ref, shift_grad_ref, grad_all, grad_cols = refs[8:]

    @pl.when(pl.program_id(0) == 0)
    def _():
        grad_all[...] = raw_ref[...].astype(BF16)
        shape = (grad_cols.shape[0], grad_all.shape[1])
        mine = lax.broadcasted_iota(jnp.int32, shape, 0) + at_ref[0] * e_cols
        chosen = jnp.where(mine == lax.broadcasted_iota(jnp.int32, shape, 1), 1.0, 0.0).astype(BF16)
        grad_cols[...] = dot(chosen, grad_all[...], ((1,), (1,))).astype(BF16)

    stats, gain = stats_ref[...], gain_ref[...]
    normed, shifted = batch_norm(pre_ref[...], stats, gain, shift_ref[...])
    hidden = jnp.maximum(shifted, 0.0).astype(BF16)
    w2_ref[...] = jnp.dot(grad_cols[...], hidden, preferred_element_type=F32)[0:e_cols, :]
    hidden_grad = dot(grad_all[...], w_ref[...], ((1,), (1,)))
    bn_grad = jnp.where(shifted > 0, hidden_grad, 0.0)
    shift_grad = jnp.sum(bn_grad, axis=0, keepdims=True)
    gain_grad = jnp.sum(bn_grad * normed, axis=0, keepdims=True)
    shift_grad_ref[...] = shift_grad
    gain_grad_ref[...] = gain_grad
    scale = gain * stats[1:2, :]
    pre_grad = scale * (bn_grad - shift_grad / crops_all - normed * (gain_grad / crops_all))
    w1_ref[...] = jnp.dot(cols_ref[...], pre_grad.astype(BF16), preferred_element_type=F32)


def whole_tail(pre_all, columns, stats, gain, shift, w_second, raw, at, e_cols):
    crops_all, hidden = pre_all.shape
    width, d_cols = w_second.shape[1], columns.shape[0]
    blk = min(hidden, max(128, 256 * 1024 // crops_all))
    smem = pl.BlockSpec(memory_space=pltpu.SMEM)
    vmem = pl.BlockSpec(memory_space=pltpu.VMEM)

    def cols(n):
        return pl.BlockSpec((n, blk), lambda j: (0, j))

    return pl.pallas_call(
        functools.partial(whole_tail_kernel, crops_all, e_cols),
        grid=(hidden // blk,),
        in_specs=[smem, cols(crops_all), vmem, cols(2), cols(1), cols(1)]
        + [pl.BlockSpec((blk, width), lambda j: (j, 0)), vmem],
        out_specs=[cols(d_cols), cols(e_cols), cols(1), cols(1)],
        out_shape=[jax.ShapeDtypeStruct((n, hidden), F32) for n in (d_cols, e_cols, 1, 1)],
        scratch_shapes=[
            pltpu.VMEM((crops_all, width), BF16),
            pltpu.VMEM((-(-e_cols // 16) * 16, crops_all), BF16),
        ],
        compiler_params=params(58),
        cost_estimate=cost(2 * crops_all * hidden * (width + d_cols), 4 * crops_all * hidden),
        name="whole_tail",
    )(at, pre_all, columns, stats, gain, shift, w_second, raw)


def after(value, *others):
    return lax.optimization_barrier((value,) + others)[0]


def body(features, w_first, bn_gain, bn_shift, w_second, prototypes, partner):
    n_batch, n_proto = lax.axis_size("batch"), lax.axis_size("proto")
    me, proto_me = lax.axis_index("batch").astype(jnp.int32), lax.axis_index("proto").astype(jnp.int32)
    rows, depth = features.shape
    width = w_second.shape[1]
    crops_all = rows * n_batch
    d_cols, e_cols = depth // n_batch, width // n_batch
    gain, shift = bn_gain[None, :], bn_shift[None, :]
    short = n_batch == 8 and n_proto == 4 and depth % 512 == 0
    at = jnp.stack([me, proto_me, proto_me & 1 if short else proto_me * 0])

    pre, pre_again, moments = first_layer(features, w_first, n_batch if short else 1)
    pre_all = lax.all_gather(pre, "batch", tiled=True)
    moment_parts = [lax.all_to_all(moments, "batch", 0, 0)] if short else batch_parts(moments)
    units = unit_rows(prototypes)
    emb_part, stats = second_layer(crops_all, moment_parts, pre_again, gain, shift, w_second)
    first, emb_part = lax.optimization_barrier((at[2] == 0, emb_part))
    raw_parts = proto_parts(emb_part)
    if short:
        keep, send = columns_pick(after(features, emb_part), at, n_batch, n_proto)
        raw_parts[0], keep, send, units = lax.optimization_barrier((raw_parts[0], keep, send, units))
    embedded = embed_rows(raw_parts)

    if short:
        partner_emb = swap(embedded, "batch", 1)
        own_codes, own_col = score(embedded, units)
        logit = logit_sum(embedded, units)
        partner_emb, own_col, logit = lax.optimization_barrier((partner_emb, own_col, logit))
        logit = logit + swap(logit, "proto", 1)
        more_codes, *cols = score(partner_emb, units, (own_col, keep))
        cols[0], logit = lax.optimization_barrier((cols[0], logit))
        codes = [own_codes, more_codes]
    else:
        codes, *cols = score(embedded, units)
        codes = [codes]
        logit = logit_sum(embedded, units)
    moved = []
    for iteration in range(ITERS):
        if short and iteration < 2:
            moved.append([swap(c, "batch", 2 * k + 2) for k, c in enumerate(cols[1:])])
            col_parts = [cols[0]] + moved[-1]
        else:
            col_parts = batch_parts(cols[0], 2 if short else 1)
        if iteration == 0:
            logit_parts = proto_parts(logit, 2 if short else 1)
            col_parts[0], *logit_parts = lax.optimization_barrier((col_parts[0], *logit_parts))
        if short and iteration == 0:
            got = swap(after(send, cols[0]), "batch", 1)
            col_parts[0], got = lax.optimization_barrier((col_parts[0], got))
        if short and iteration == 2:
            columns = columns_join(after(keep, cols[0]), got, *moved)
            columns = [columns, swap(columns, "proto", 2)]
            col_parts[0], *columns = lax.optimization_barrier((col_parts[0], *columns))
        if iteration < ITERS - 1:
            row_parts = proto_small(row_pass(col_parts, codes))
            cols = col_pass(row_parts, codes, got if short and iteration == 0 else None)
    if short:
        own_half, send = target_sum(col_parts, codes[0], units, partner[None, :], at, 2)
        columns = after(jnp.concatenate(columns), own_half)
        own_half = own_half + swap(send, "proto", 1)
        columns = [columns, swap(columns, "proto", 1)]
        target_parts = proto_parts(own_half, 2)
        columns = columns_all(*columns, at)
        target_parts[0], columns = lax.optimization_barrier((target_parts[0], columns))
    else:
        target_parts = proto_parts(target_sum(col_parts, codes[0], units, partner[None, :], at, 1)[0])
    raw_grad, penalty = loss_grad(raw_parts, logit_parts, target_parts, at)

    if short:
        pre_all = after(pre_all, raw_grad)
        ins = (at, pre_all.reshape(n_batch, rows, -1), columns, stats, gain, shift, w_second)
        e_rows, hidden = -(-e_cols // 16) * 16, w_second.shape[0]
        table = (2, n_batch, hidden)
        flat = flat_sums(*ins[1:-1])
        own = raw_grad[None]
        rest = [swap(raw_grad, "batch", k) for k in (2, 4, 6)]
        rest = jnp.stack([rest[0]] + [after(piece, *flat) for piece in rest[1:]])
        far_own, own_core = swap(own, "batch", 1), swap(own, "proto", 1)
        far_own_core = swap(far_own, "proto", 1)
        rest, far_own, own_core, far_own_core = lax.optimization_barrier((rest, far_own, own_core, far_own_core))
        far, rest_core = swap(rest, "batch", 1), swap(rest, "proto", 1)
        other_penalty = swap(after(penalty, rest), "proto", 1)
        penalty = jnp.concatenate(
            [jnp.where(first, penalty, other_penalty), jnp.where(first, other_penalty, penalty)], axis=1
        )
        half = tail_call(
            near_kernel, [(d_cols, hidden), (e_rows, hidden), table], [(crops_all // 2, hidden)],
            *ins, [own, rest, own_core, rest_core], [], "tail_near",
        )
        far, penalty, *half = lax.optimization_barrier((far, penalty, *half, *flat))
        grad_w1, grad_w2, grad_gain, grad_shift = tail_call(
            functools.partial(far_kernel, crops_all),
            [(d_cols, hidden), (e_cols, hidden), (1, hidden), (1, hidden)], [table],
            *ins, [far_own, far, far_own_core, swap(far, "proto", 1)], half, "tail_far",
        )
    else:
        by_owner = jnp.swapaxes(features.astype(F32).reshape(rows, n_batch, d_cols), 0, 1)
        columns = columns_cast(lax.all_to_all(by_owner, "batch", 0, 0).reshape(crops_all, d_cols))
        raw_all = lax.all_gather(raw_grad, "batch", tiled=True)
        grad_w1, grad_w2, grad_gain, grad_shift = whole_tail(
            pre_all, columns, stats, gain, shift, w_second, raw_all, at, e_cols
        )
    return (penalty[0], grad_w1, grad_gain[0], grad_shift[0], grad_w2.T)


def solution(mesh):
    return jax.shard_map(
        body,
        mesh=mesh,
        in_specs=(
            P("batch", None),
            P(None, "proto"),
            P("proto"),
            P("proto"),
            P("proto", None),
            P("proto", None),
            P("batch"),
        ),
        out_specs=(P("batch"), P("batch", "proto"), P("proto"), P("proto"), P("proto", "batch")),
        check_vma=False,
    )
```

```python
import functools

import jax
import jax.numpy as jnp
from jax import lax
from jax.experimental import pallas as pl
from jax.experimental.pallas import tpu as pltpu
from jax.sharding import PartitionSpec as P

ITERS = 3
F32 = jnp.float32
BF16 = jnp.bfloat16
HIGHEST = lax.Precision.HIGHEST

balancing_epsilon = 0.05
sharpness_divisor = 0.1
penalty_weighting = 64.0


def stages(n, first, stride=1):
    out, radix = [], first
    while stride < n:
        radix = min(radix, n // stride)
        out.append((stride, radix))
        stride *= radix
        radix = 4 if (n // stride) % 4 == 0 else 2
    return out


def swap(v, axis, mask):
    n = lax.axis_size(axis)
    return lax.ppermute(v, axis, [(i, i ^ mask) for i in range(n)])


def add_parts(parts):
    if len(parts) == 4:
        return (parts[0] + parts[1]) + (parts[2] + parts[3])
    return functools.reduce(lambda x, y: x + y, parts)


def exchange(v, axis, first, stride=1):
    n = lax.axis_size(axis)
    parts = [v]
    for step, radix in stages(n, first, stride):
        v = add_parts(parts)
        parts = [v] + [swap(v, axis, k * step) for k in range(1, radix)]
    return parts


def batch_parts(v, stride=1):
    steps = (lax.axis_size("batch") // stride).bit_length() - 1
    return exchange(v, "batch", 2 if steps % 2 else 4, stride)


def proto_parts(v, stride=1):
    return exchange(v, "proto", 2, stride)


def proto_small(v):
    return exchange(v, "proto", 4 if lax.axis_size("proto") == 4 else 2)


def whole(shape):
    return pl.BlockSpec(shape, lambda *_: (0,) * len(shape))


def params(mib=24):
    return pltpu.CompilerParams(vmem_limit_bytes=mib * 1024 * 1024)


def cost(flops, nbytes, trans=0):
    return pl.CostEstimate(flops=int(flops), bytes_accessed=int(nbytes), transcendentals=int(trans))


def dot(a, b, dims, precision=None):
    return lax.dot_general(a, b, ((dims[0], dims[1]), ((), ())), precision=precision, preferred_element_type=F32)


def eye(n):
    return lax.broadcasted_iota(jnp.int32, (n, n), 0) == lax.broadcasted_iota(jnp.int32, (n, n), 1)


def to_lanes(col):
    n = col.shape[0]
    return jnp.sum(jnp.where(eye(n), col, 0.0), axis=0, keepdims=True)


def to_column(row):
    n = row.shape[1]
    return jnp.sum(jnp.where(eye(n), row, 0.0), axis=1, keepdims=True)


def first_kernel(f_hbm, w_hbm, pre_ref, again_ref, mom_ref, f_ref, w_ref, sems):
    depth, hidden = w_ref.shape
    n = sems.shape[0] - 1
    step = depth // n
    copies = [pltpu.make_async_copy(f_hbm, f_ref, sems.at[n])]
    for k in range(n):
        at = pl.ds(k * step, step)
        copies.append(pltpu.make_async_copy(w_hbm.at[at, :], w_ref.at[at, :], sems.at[k]))
    for copy in copies:
        copy.start()
    copies[0].wait()
    for k in range(n):
        copies[k + 1].wait()
        at = slice(k * step, (k + 1) * step)
        part = jnp.dot(f_ref[:, at], w_ref[at, :], preferred_element_type=F32)
        if k == 0:
            pre_ref[...] = part
        else:
            pre_ref[...] += part
    pre = pre_ref[...]
    again_ref[...] = pre
    first = jnp.sum(pre, axis=0, keepdims=True)
    second = jnp.sum(pre * pre, axis=0, keepdims=True)
    for k in range(mom_ref.shape[0]):
        mom_ref[k, :, 0:hidden] = first
        mom_ref[k, :, hidden:] = second


def first_layer(features, w_first, spread):
    rows, depth = features.shape
    hidden = w_first.shape[1]
    steps = 6 if depth % (6 * 128) == 0 else 1
    return pl.pallas_call(
        first_kernel,
        in_specs=[pl.BlockSpec(memory_space=pl.ANY)] * 2,
        out_shape=[jax.ShapeDtypeStruct((rows, hidden), F32)] * 2
        + [jax.ShapeDtypeStruct((spread, 1, 2 * hidden), F32)],
        scratch_shapes=[
            pltpu.VMEM((rows, depth), BF16),
            pltpu.VMEM((depth, hidden), BF16),
            pltpu.SemaphoreType.DMA((steps + 1,)),
        ],
        compiler_params=params(52),
        cost_estimate=cost(2 * rows * depth * hidden, 2 * depth * hidden + 4 * rows * hidden),
        name="first_layer",
    )(features, w_first)


def batch_norm(pre, stats, gain, shift):
    normed = (pre - stats[0:1, :]) * stats[1:2, :]
    return normed, gain * normed + shift


def second_kernel(crops_all, n_parts, *refs):
    parts = refs[:n_parts]
    pre_ref, gain_ref, shift_ref, w_ref, emb_ref, stats_ref = refs[n_parts:]
    hidden = pre_ref.shape[1]
    moments = add_parts([p[k] for p in parts for k in range(p.shape[0])]) / crops_all
    mean = moments[:, 0:hidden]
    var = moments[:, hidden:] - mean * mean
    stats_ref[0:1, :] = mean
    stats_ref[1:2, :] = lax.rsqrt(var + 1e-05)
    _, shifted = batch_norm(pre_ref[...], stats_ref[...], gain_ref[...], shift_ref[...])
    low = jnp.maximum(shifted, 0.0).astype(BF16)
    emb_ref[...] = jnp.dot(low, w_ref[...], preferred_element_type=F32)


def second_layer(crops_all, parts, pre, gain, shift, w_second):
    rows, hidden = pre.shape
    width = w_second.shape[1]
    return pl.pallas_call(
        functools.partial(second_kernel, crops_all, len(parts)),
        out_shape=[jax.ShapeDtypeStruct((rows, width), F32), jax.ShapeDtypeStruct((2, hidden), F32)],
        compiler_params=params(),
        cost_estimate=cost(2 * rows * hidden * width, 4 * rows * hidden + 2 * hidden * width),
        name="second_layer",
    )(*parts, pre, gain, shift, w_second)


def unit_kernel(p_ref, u_ref):
    wide = p_ref[...].astype(F32)
    u_ref[...] = (wide * lax.rsqrt(jnp.sum(wide * wide, 1, keepdims=True) + 1e-06)).astype(BF16)


def unit_rows(prototypes):
    rows, width = prototypes.shape
    blk = min(1024, rows)
    return pl.pallas_call(
        unit_kernel,
        grid=(rows // blk,),
        in_specs=[pl.BlockSpec((blk, width), lambda j: (j, 0))],
        out_specs=pl.BlockSpec((blk, width), lambda j: (j, 0)),
        out_shape=jax.ShapeDtypeStruct((rows, width), BF16),
        compiler_params=params(),
        cost_estimate=cost(4 * rows * width, 4 * rows * width),
        name="unit_rows",
    )(prototypes)


def embed(raw):
    inv_norm = lax.rsqrt(jnp.sum(raw * raw, 1, keepdims=True) + 1e-06)
    return raw * inv_norm, inv_norm


def embed_kernel(*refs):
    refs[-1][...] = embed(add_parts([p[...] for p in refs[:-1]]))[0]


def embed_rows(parts):
    return pl.pallas_call(
        embed_kernel,
        out_shape=jax.ShapeDtypeStruct(parts[0].shape, F32),
        compiler_params=params(),
        cost_estimate=cost(8 * parts[0].size, 12 * parts[0].size),
        name="embed_rows",
    )(*parts)


def put_blocks(out_ref, row, value):
    for k in range(value.shape[1] // 128):
        out_ref[row + k : row + k + 1, :] = value[:, k * 128 : (k + 1) * 128]


def score_kernel(n, *refs):
    piece, u_ref = refs[:2]
    code_ref, col_ref = refs[-2:] if n == 0 else refs[4:6]
    low = piece[...].astype(BF16)
    protos = u_ref.shape[0]
    step = min(512, protos)
    for j in range(protos // step):
        at = slice(j * step, (j + 1) * step)
        code = jnp.exp(dot(low, u_ref[at, :], ((1,), (1,))) / balancing_epsilon)
        code_ref[:, at] = code
        put_blocks(col_ref, j * step // 128, jnp.sum(code, axis=0, keepdims=True))
    if n:
        col_ref[...] += refs[2][...]
        lines = col_ref.shape[0]
        for k, out in enumerate(refs[6:]):
            out[0:lines, :] = col_ref[...]
            out[lines:, :] = refs[3][k + 1]


def score(piece, units, more=None):
    rows, width = piece.shape
    protos = units.shape[0]
    lines = protos // 128
    n, extra = 0, ()
    out_shape = [jax.ShapeDtypeStruct((rows, protos), F32), jax.ShapeDtypeStruct((lines, 128), F32)]
    if more is not None:
        n, extra = more[1].shape[0] - 1, more
        out_shape += [jax.ShapeDtypeStruct((lines + more[1].shape[1], 128), F32)] * n
    return pl.pallas_call(
        functools.partial(score_kernel, n),
        out_shape=out_shape,
        compiler_params=params(),
        cost_estimate=cost(2 * rows * protos * width, 4 * rows * protos, rows * protos),
        name="score",
    )(piece, units, *extra)


def col_scale(parts):
    lines = parts[0].shape[0]
    return 1.0 / add_parts([p[0:lines, :] for p in parts])


def pack(table, lane_row, out_ref):
    rows, width = table.shape
    out_ref[0:rows, :] = table
    out_ref[rows:, :] = jnp.zeros((8, width), F32)
    out_ref[rows : rows + 1, 0:rows] = lane_row


def logit_kernel(emb_ref, u_ref, out_ref):
    low = emb_ref[...].astype(BF16)
    protos = u_ref.shape[0]
    step = min(512, protos)
    total, mass = 0.0, 0.0
    for j in range(protos // step):
        units = u_ref[j * step : (j + 1) * step, :]
        logits = jnp.exp(dot(low, units, ((1,), (1,))) / sharpness_divisor)
        total = total + jnp.dot(logits.astype(BF16), units, preferred_element_type=F32)
        mass = mass + jnp.sum(logits, axis=1, keepdims=True)
    pack(total, to_lanes(mass), out_ref)


def logit_sum(embedded, units):
    rows, width = embedded.shape
    protos = units.shape[0]
    return pl.pallas_call(
        logit_kernel,
        out_shape=jax.ShapeDtypeStruct((rows + 8, width), F32),
        compiler_params=params(),
        cost_estimate=cost(4 * rows * protos * width, 2 * protos * width, rows * protos),
        name="logit_sum",
    )(embedded, units)


def row_kernel(n_parts, *refs):
    parts, codes, out_ref = refs[:n_parts], refs[n_parts:-1], refs[-1]
    scale = col_scale(parts)
    for k, code in enumerate(codes):
        total = 0.0
        for j in range(scale.shape[0]):
            total = total + code[:, j * 128 : (j + 1) * 128] * scale[j : j + 1, :]
        out_ref[k : k + 1, :] = to_lanes(jnp.sum(total, axis=1, keepdims=True))


def row_pass(parts, codes):
    rows, protos = codes[0].shape
    n = len(codes)
    return pl.pallas_call(
        functools.partial(row_kernel, len(parts)),
        out_shape=jax.ShapeDtypeStruct((n, rows), F32),
        compiler_params=params(),
        cost_estimate=cost(2 * n * rows * protos, 4 * n * rows * protos),
        name="row_pass",
    )(*parts, *codes)


def col_kernel(n_parts, n_codes, *refs):
    parts, codes, refs = refs[:n_parts], refs[n_parts : n_parts + n_codes], refs[n_parts + n_codes :]
    scale = 1.0 / add_parts([p[...] for p in parts])
    total = 0.0
    for k, code in enumerate(codes):
        total = total + jnp.sum(code[...] * to_column(scale[k : k + 1, :]), axis=0, keepdims=True)
    if len(refs) == 1:
        put_blocks(refs[0], 0, total)
    else:
        put_blocks(refs[1], 0, total)
        for k, out in enumerate(refs[2:]):
            out[0 : refs[1].shape[0], :] = refs[1][...]
            out[refs[1].shape[0] :, :] = refs[0][k + 1]


def col_pass(parts, codes, columns=None):
    rows, protos = codes[0].shape
    n = len(codes)
    lines = protos // 128
    extra = () if columns is None else (columns,)
    shapes = [(lines, 128)] + [(lines + c.shape[1], 128) for c in extra for _ in range(c.shape[0] - 1)]
    return pl.pallas_call(
        functools.partial(col_kernel, len(parts), n),
        out_shape=[jax.ShapeDtypeStruct(shape, F32) for shape in shapes],
        compiler_params=params(),
        cost_estimate=cost(2 * n * rows * protos, 4 * n * rows * protos),
        name="col_pass",
    )(*parts, *codes, *extra)


def target_kernel(n_parts, halves, *refs):
    parts = refs[:n_parts]
    codes_ref, u_ref, partner_ref, at_ref = refs[n_parts : n_parts + 4]
    outs, table_all, mass_all, low = refs[n_parts + 4 : -3], refs[-3], refs[-2], refs[-1]
    rows = codes_ref.shape[0]
    scale = col_scale(parts)
    total, table = 0.0, 0.0
    lines = scale.shape[0]
    step = min(8, lines)
    for i in range(lines // step):
        for j in range(i * step, (i + 1) * step):
            weighted = codes_ref[:, j * 128 : (j + 1) * 128] * scale[j : j + 1, :]
            low[:, j * 128 : (j + 1) * 128] = weighted.astype(BF16)
            total = total + weighted
        at = slice(i * step * 128, (i + 1) * step * 128)
        table = table + jnp.dot(low[:, at], u_ref[at, :], preferred_element_type=F32)
    mass = jnp.sum(total, axis=1, keepdims=True)
    chosen = partner_ref[...] == lax.broadcasted_iota(jnp.int32, (rows, rows), 0)
    table_all[...] = dot(jnp.where(chosen, 1.0, 0.0).astype(F32), table, ((1,), (0,)), HIGHEST)
    mass_all[...] = jnp.sum(jnp.where(chosen, to_lanes(mass), 0.0), axis=1, keepdims=True)
    size = rows // halves
    for k in range(halves):
        at = pl.ds(pl.multiple_of((at_ref[2] ^ k) * size, size), size)
        pack(table_all[at, :], to_lanes(mass_all[at, :]), outs[k])


def target_sum(parts, codes, units, partner, at, halves):
    rows, protos = codes.shape
    width = units.shape[1]
    n_vmem = len(parts) + 3
    return pl.pallas_call(
        functools.partial(target_kernel, len(parts), halves),
        in_specs=[pl.BlockSpec(memory_space=pltpu.VMEM)] * n_vmem + [pl.BlockSpec(memory_space=pltpu.SMEM)],
        out_shape=[jax.ShapeDtypeStruct((rows // halves + 8, width), F32)] * halves,
        scratch_shapes=[
            pltpu.VMEM((rows, width), F32),
            pltpu.VMEM((rows, 1), F32),
            pltpu.VMEM((rows, protos), BF16),
        ],
        compiler_params=params(),
        cost_estimate=cost(2 * rows * protos * width, 4 * rows * protos + 2 * protos * width),
        name="target_sum",
    )(*parts, codes, units, partner, at)


def loss_kernel(n_raw, n_logit, n_target, *refs):
    core_ref, refs = refs[0], refs[1:]
    raws, refs = refs[:n_raw], refs[n_raw:]
    logits, refs = refs[:n_logit], refs[n_logit:]
    target = add_parts([p[...] for p in refs[:n_target]])
    grad_ref, loss_ref = refs[n_target:]
    rows = raws[0].shape[0]
    size = grad_ref.shape[0]
    at = pl.ds(pl.multiple_of(core_ref[2] * size, size), size)
    raw = add_parts([p[at, :] for p in raws])
    logit = add_parts([p[at, :] for p in logits])
    denoms = to_column(add_parts([p[rows : rows + 1, 0:rows] for p in logits]))
    denom = jnp.where(core_ref[2] == 0, denoms[0:size], denoms[rows - size :])
    embedded, inv_norm = embed(raw)
    row_scale = to_column(1.0 / target[size : size + 1, 0:size])
    wanted = target[0:size, :] * row_scale
    emb_low = embedded.astype(BF16).astype(F32)
    cross = jnp.sum(wanted * emb_low, axis=1, keepdims=True)
    loss_ref[...] = to_lanes(jnp.log(denom) - cross / sharpness_divisor)
    emb_grad = penalty_weighting * (logit / denom - wanted) / sharpness_divisor
    inner = jnp.sum(embedded * emb_grad, 1, keepdims=True)
    grad_ref[...] = (emb_grad - embedded * inner) * inv_norm


def loss_grad(raw_parts, logit_parts, target_parts, core):
    width = raw_parts[0].shape[1]
    rows = target_parts[0].shape[0] - 8
    n_vmem = len(raw_parts) + len(logit_parts) + len(target_parts)
    return pl.pallas_call(
        functools.partial(loss_kernel, len(raw_parts), len(logit_parts), len(target_parts)),
        in_specs=[pl.BlockSpec(memory_space=pltpu.SMEM)] + [pl.BlockSpec(memory_space=pltpu.VMEM)] * n_vmem,
        out_shape=[jax.ShapeDtypeStruct((rows, width), F32), jax.ShapeDtypeStruct((1, rows), F32)],
        compiler_params=params(),
        cost_estimate=cost(20 * rows * width, 24 * rows * width),
        name="loss_grad",
    )(core, *raw_parts, *logit_parts, *target_parts)


def pick_kernel(f_ref, at_ref, keep_ref, send_ref):
    n_z, height, rows = keep_ref.shape
    depth = f_ref.shape[1]
    shape = (n_z * height, depth)
    row = lax.broadcasted_iota(jnp.int32, shape, 0)
    col = lax.broadcasted_iota(jnp.int32, shape, 1)
    d_cols = depth // (2 * n_z)
    me, share = at_ref[0], at_ref[1] * height
    for out, y in ((keep_ref, me & 1), (send_ref, (me & 1) ^ 1)):
        first = jnp.zeros(shape, jnp.int32)
        for k in range(n_z):
            owner = (((me >> 1) ^ k) << 1) + y
            first = jnp.where(row >= k * height, owner * d_cols + share - k * height, first)
        chosen = jnp.where(col == first + row, 1.0, 0.0).astype(BF16)
        out[...] = dot(chosen, f_ref[...], ((1,), (1,))).reshape(n_z, height, rows)


def columns_pick(features, at, n_batch, n_proto):
    rows, depth = features.shape
    shape = jax.ShapeDtypeStruct((n_batch // 2, depth // (n_batch * n_proto), rows), F32)
    return pl.pallas_call(
        pick_kernel,
        in_specs=[pl.BlockSpec(memory_space=pltpu.VMEM), pl.BlockSpec(memory_space=pltpu.SMEM)],
        out_shape=[shape, shape],
        compiler_params=params(),
        cost_estimate=cost(2 * depth * depth // n_proto * rows, 8 * rows * depth),
        name="columns_pick",
    )(features, at)


def join_kernel(n_z, keep_ref, got_ref, *refs):
    out_ref, height = refs[-1], keep_ref.shape[1]
    out_ref[0, 0] = keep_ref[0]
    out_ref[0, 1] = got_ref[0]
    for k in range(2 * n_z - 2):
        out_ref[0, 2 + k] = refs[k][refs[k].shape[0] - height :, :]


def columns_join(keep, got, first, second):
    n_z, height, rows = keep.shape
    return pl.pallas_call(
        functools.partial(join_kernel, n_z),
        out_shape=jax.ShapeDtypeStruct((1, 2 * n_z, height, rows), F32),
        compiler_params=params(),
        cost_estimate=cost(0, 16 * n_z * height * rows),
        name="columns_join",
    )(keep, got, *[m for pair in zip(first, second) for m in pair])


def columns_kernel(masks, at_ref, *refs):
    out_ref = refs[-1]
    inner = len(masks) // (len(refs) - 1)
    for k, mask in enumerate(masks):
        _, n_batch, height, rows = refs[k // inner].shape
        row = pl.multiple_of((at_ref[1] ^ mask) * height, height)
        for i in range(n_batch):
            out_ref[at_ref[0] ^ i, pl.ds(row, height), :] = refs[k // inner][k % inner, i].astype(BF16)


def columns_all(own, other, at):
    n_proto = 2 * own.shape[0]
    _, n_batch, height, rows = own.shape
    smem = pl.BlockSpec(memory_space=pltpu.SMEM)
    vmem = pl.BlockSpec(memory_space=pltpu.VMEM)
    return pl.pallas_call(
        functools.partial(columns_kernel, (0, 2, 1, 3)),
        in_specs=[smem, vmem, vmem],
        out_shape=jax.ShapeDtypeStruct((n_batch, n_proto * height, rows), BF16),
        compiler_params=params(),
        cost_estimate=cost(0, 6 * n_proto * height * n_batch * rows),
        name="columns_all",
    )(at, own, other)


def cast_kernel(in_ref, out_ref):
    out_ref[...] = in_ref[...].T.astype(BF16)


def columns_cast(columns):
    return pl.pallas_call(
        cast_kernel,
        out_shape=jax.ShapeDtypeStruct(columns.shape[::-1], BF16),
        compiler_params=params(),
        name="columns_cast",
    )(columns)


def centre_of(sums, crops):
    return [jnp.sum(sums[k], axis=0, keepdims=True) / crops for k in range(2)]


def tail_half(refs, grads, odd, n_batch, sums_ref, centre, grad_all, low_all, cols_all, *wide):
    at_ref, pre_ref, cols_ref, stats, gain, shift, w_ref = refs
    unit, width = pre_ref.shape[1], grad_all.shape[1]
    size, n = unit // 2, n_batch // 2
    e_rows = 16 * (-(-(width // n_batch) // 16))
    for k in range(n):
        for flip in range(2):
            place = pl.multiple_of(k * unit + (at_ref[2] ^ flip) * size, size)
            own, rest = grads[2 * flip], grads[2 * flip + 1]
            grad_all[pl.ds(place, size), :] = (rest[k - 1] if k else own[0]).astype(BF16)
    mine = lax.broadcasted_iota(jnp.int32, (e_rows, width), 0) + at_ref[0] * (width // n_batch)
    chosen = jnp.where(mine == lax.broadcasted_iota(jnp.int32, (e_rows, width), 1), 1.0, 0.0).astype(BF16)
    w2 = 0.0
    for k in range(n):
        rows = slice(k * unit, (k + 1) * unit)
        block = at_ref[0] ^ (2 * k + odd)
        normed, shifted = batch_norm(pre_ref[block], stats, gain, shift)
        grad = grad_all[rows, :]
        picked = dot(chosen, grad, ((1,), (1,))).astype(BF16)
        hidden = jnp.maximum(shifted, 0.0).astype(BF16)
        w2 = w2 + jnp.dot(picked, hidden, preferred_element_type=F32)
        hidden_grad = dot(grad, w_ref[...], ((1,), (1,)))
        bn_grad = jnp.where(shifted > 0, hidden_grad, 0.0)
        sums_ref[0, pl.ds(block, 1), :] = jnp.sum(bn_grad, axis=0, keepdims=True)
        sums_ref[1, pl.ds(block, 1), :] = jnp.sum(bn_grad * normed, axis=0, keepdims=True)
        if centre is None:
            wide[0][rows, :] = bn_grad
        else:
            low_all[rows, :] = (bn_grad - centre[0] - normed * centre[1]).astype(BF16)
        cols_all[:, rows] = cols_ref[block]
    if centre is None:
        centre = centre_of(sums_ref, n * unit)
        for k in range(n):
            rows = slice(k * unit, (k + 1) * unit)
            normed, _ = batch_norm(pre_ref[at_ref[0] ^ (2 * k + odd)], stats, gain, shift)
            low_all[rows, :] = (wide[0][rows, :] - centre[0] - normed * centre[1]).astype(BF16)
    return jnp.dot(cols_all[...], low_all[...], preferred_element_type=F32), w2


def near_kernel(n_batch, n_grads, *refs):
    ins, grads, refs = refs[:7], refs[7 : 7 + n_grads], refs[7 + n_grads :]
    w1_ref, w2_ref, sums_ref, wide, *scratch = refs
    sums_ref[...] = jnp.zeros_like(sums_ref)
    ins = ins[:3] + tuple(r[...] for r in ins[3:6]) + ins[6:]
    w1_ref[...], w2_ref[...] = tail_half(ins, grads, 0, n_batch, sums_ref, None, *scratch, wide)


def far_kernel(crops_all, n_batch, n_grads, *refs):
    ins, grads, refs = refs[:7], refs[7 : 7 + n_grads], refs[7 + n_grads :]
    near_w1, near_w2, near_sums, flat_ref, total_ref = refs[:5]
    w1_ref, w2_ref, gain_grad_ref, shift_grad_ref, sums, *scratch = refs[5:]
    ins = ins[:3] + tuple(r[...] for r in ins[3:6]) + ins[6:]
    stats, gain = ins[3:5]
    sums[...] = near_sums[...]
    centre = centre_of(near_sums[...], crops_all // 2)
    w1, w2 = tail_half(ins, grads, 1, n_batch, sums, centre, *scratch)
    w2_ref[...] = (near_w2[...] + w2)[0 : w2_ref.shape[0], :]
    shift_grad = jnp.sum(sums[0], axis=0, keepdims=True)
    gain_grad = jnp.sum(sums[1], axis=0, keepdims=True)
    shift_grad_ref[...] = shift_grad
    gain_grad_ref[...] = gain_grad
    flat = total_ref[...] * (shift_grad / crops_all - centre[0])
    flat = flat + flat_ref[...] * (gain_grad / crops_all - centre[1])
    w1_ref[...] = gain * stats[1:2, :] * (near_w1[...] + w1 - flat)


def tail_call(kernel, outs, scratch, at, pre_all, columns, stats, gain, shift, w_second, grads, more, name):
    n_batch, unit, hidden = pre_all.shape
    width, d_cols = w_second.shape[1], columns.shape[1]
    crops = n_batch * unit // 2
    vmem = pl.BlockSpec(memory_space=pltpu.VMEM)
    return pl.pallas_call(
        functools.partial(kernel, n_batch, len(grads)),
        in_specs=[pl.BlockSpec(memory_space=pltpu.SMEM)] + [vmem] * (6 + len(grads) + len(more)),
        out_shape=[jax.ShapeDtypeStruct(n, F32) for n in outs],
        scratch_shapes=[pltpu.VMEM(n, F32) for n in scratch]
        + [
            pltpu.VMEM((crops, width), BF16),
            pltpu.VMEM((crops, hidden), BF16),
            pltpu.VMEM((d_cols, crops), BF16),
        ],
        compiler_params=params(20),
        cost_estimate=cost(2 * crops * hidden * (width + 256), 4 * crops * hidden),
        name=name,
    )(at, pre_all, columns, stats, gain, shift, w_second, *grads, *more)


def flat_kernel(pre_ref, cols_ref, stats_ref, gain_ref, shift_ref, flat_ref, total_ref):
    stats, gain, shift = stats_ref[...], gain_ref[...], shift_ref[...]
    total = 0.0
    for k in range(pre_ref.shape[0]):
        total = total + jnp.sum(cols_ref[k].astype(F32), axis=1, keepdims=True)
        normed, _ = batch_norm(pre_ref[k], stats, gain, shift)
        part = jnp.dot(cols_ref[k], normed.astype(BF16), preferred_element_type=F32)
        if k == 0:
            flat_ref[...] = part
        else:
            flat_ref[...] += part
    total_ref[...] = total


def flat_sums(pre_all, columns, stats, gain, shift):
    n_batch, unit, hidden = pre_all.shape
    d_cols = columns.shape[1]
    return pl.pallas_call(
        flat_kernel,
        out_shape=[jax.ShapeDtypeStruct((d_cols, hidden), F32), jax.ShapeDtypeStruct((d_cols, 1), F32)],
        compiler_params=params(20),
        cost_estimate=cost(2 * n_batch * unit * hidden * d_cols, 4 * n_batch * unit * hidden),
        name="flat_sums",
    )(pre_all, columns, stats, gain, shift)


def whole_tail_kernel(crops_all, e_cols, *refs):
    at_ref, pre_ref, cols_ref, stats_ref, gain_ref, shift_ref, w_ref, raw_ref = refs[:8]
    w1_ref, w2_ref, gain_grad_ref, shift_grad_ref, grad_all, grad_cols = refs[8:]

    @pl.when(pl.program_id(0) == 0)
    def _():
        grad_all[...] = raw_ref[...].astype(BF16)
        shape = (grad_cols.shape[0], grad_all.shape[1])
        mine = lax.broadcasted_iota(jnp.int32, shape, 0) + at_ref[0] * e_cols
        chosen = jnp.where(mine == lax.broadcasted_iota(jnp.int32, shape, 1), 1.0, 0.0).astype(BF16)
        grad_cols[...] = dot(chosen, grad_all[...], ((1,), (1,))).astype(BF16)

    stats, gain = stats_ref[...], gain_ref[...]
    normed, shifted = batch_norm(pre_ref[...], stats, gain, shift_ref[...])
    hidden = jnp.maximum(shifted, 0.0).astype(BF16)
    w2_ref[...] = jnp.dot(grad_cols[...], hidden, preferred_element_type=F32)[0:e_cols, :]
    hidden_grad = dot(grad_all[...], w_ref[...], ((1,), (1,)))
    bn_grad = jnp.where(shifted > 0, hidden_grad, 0.0)
    shift_grad = jnp.sum(bn_grad, axis=0, keepdims=True)
    gain_grad = jnp.sum(bn_grad * normed, axis=0, keepdims=True)
    shift_grad_ref[...] = shift_grad
    gain_grad_ref[...] = gain_grad
    scale = gain * stats[1:2, :]
    pre_grad = scale * (bn_grad - shift_grad / crops_all - normed * (gain_grad / crops_all))
    w1_ref[...] = jnp.dot(cols_ref[...], pre_grad.astype(BF16), preferred_element_type=F32)


def whole_tail(pre_all, columns, stats, gain, shift, w_second, raw, at, e_cols):
    crops_all, hidden = pre_all.shape
    width, d_cols = w_second.shape[1], columns.shape[0]
    blk = min(hidden, max(128, 256 * 1024 // crops_all))
    smem = pl.BlockSpec(memory_space=pltpu.SMEM)
    vmem = pl.BlockSpec(memory_space=pltpu.VMEM)

    def cols(n):
        return pl.BlockSpec((n, blk), lambda j: (0, j))

    return pl.pallas_call(
        functools.partial(whole_tail_kernel, crops_all, e_cols),
        grid=(hidden // blk,),
        in_specs=[smem, cols(crops_all), vmem, cols(2), cols(1), cols(1)]
        + [pl.BlockSpec((blk, width), lambda j: (j, 0)), vmem],
        out_specs=[cols(d_cols), cols(e_cols), cols(1), cols(1)],
        out_shape=[jax.ShapeDtypeStruct((n, hidden), F32) for n in (d_cols, e_cols, 1, 1)],
        scratch_shapes=[
            pltpu.VMEM((crops_all, width), BF16),
            pltpu.VMEM((-(-e_cols // 16) * 16, crops_all), BF16),
        ],
        compiler_params=params(58),
        cost_estimate=cost(2 * crops_all * hidden * (width + d_cols), 4 * crops_all * hidden),
        name="whole_tail",
    )(at, pre_all, columns, stats, gain, shift, w_second, raw)


def after(value, *others):
    return lax.optimization_barrier((value,) + others)[0]


def body(features, w_first, bn_gain, bn_shift, w_second, prototypes, partner):
    n_batch, n_proto = lax.axis_size("batch"), lax.axis_size("proto")
    me, proto_me = lax.axis_index("batch").astype(jnp.int32), lax.axis_index("proto").astype(jnp.int32)
    rows, depth = features.shape
    width = w_second.shape[1]
    crops_all = rows * n_batch
    d_cols, e_cols = depth // n_batch, width // n_batch
    gain, shift = bn_gain[None, :], bn_shift[None, :]
    short = n_batch == 8 and n_proto == 4 and depth % 512 == 0
    at = jnp.stack([me, proto_me, proto_me & 1 if short else proto_me * 0])

    pre, pre_again, moments = first_layer(features, w_first, n_batch if short else 1)
    pre_all = lax.all_gather(pre, "batch", tiled=True)
    moment_parts = [lax.all_to_all(moments, "batch", 0, 0)] if short else batch_parts(moments)
    units = unit_rows(prototypes)
    emb_part, stats = second_layer(crops_all, moment_parts, pre_again, gain, shift, w_second)
    first, emb_part = lax.optimization_barrier((at[2] == 0, emb_part))
    raw_parts = proto_parts(emb_part)
    if short:
        keep, send = columns_pick(after(features, emb_part), at, n_batch, n_proto)
        raw_parts[0], keep, send, units = lax.optimization_barrier((raw_parts[0], keep, send, units))
    embedded = embed_rows(raw_parts)

    if short:
        partner_emb = swap(embedded, "batch", 1)
        own_codes, own_col = score(embedded, units)
        logit = logit_sum(embedded, units)
        partner_emb, own_col, logit = lax.optimization_barrier((partner_emb, own_col, logit))
        logit = logit + swap(logit, "proto", 1)
        more_codes, *cols = score(partner_emb, units, (own_col, keep))
        cols[0], logit = lax.optimization_barrier((cols[0], logit))
        codes = [own_codes, more_codes]
    else:
        codes, *cols = score(embedded, units)
        codes = [codes]
        logit = logit_sum(embedded, units)
    moved = []
    for iteration in range(ITERS):
        if short and iteration < 2:
            moved.append([swap(c, "batch", 2 * k + 2) for k, c in enumerate(cols[1:])])
            col_parts = [cols[0]] + moved[-1]
        else:
            col_parts = batch_parts(cols[0], 2 if short else 1)
        if iteration == 0:
            logit_parts = proto_parts(logit, 2 if short else 1)
            col_parts[0], *logit_parts = lax.optimization_barrier((col_parts[0], *logit_parts))
        if short and iteration == 0:
            got = swap(after(send, cols[0]), "batch", 1)
            col_parts[0], got = lax.optimization_barrier((col_parts[0], got))
        if short and iteration == 2:
            columns = columns_join(after(keep, cols[0]), got, *moved)
            columns = [columns, swap(columns, "proto", 2)]
            col_parts[0], *columns = lax.optimization_barrier((col_parts[0], *columns))
        if iteration < ITERS - 1:
            row_parts = proto_small(row_pass(col_parts, codes))
            cols = col_pass(row_parts, codes, got if short and iteration == 0 else None)
    if short:
        own_half, send = target_sum(col_parts, codes[0], units, partner[None, :], at, 2)
        columns = after(jnp.concatenate(columns), own_half)
        own_half = own_half + swap(send, "proto", 1)
        columns = [columns, swap(columns, "proto", 1)]
        target_parts = proto_parts(own_half, 2)
        columns = columns_all(*columns, at)
        target_parts[0], columns = lax.optimization_barrier((target_parts[0], columns))
    else:
        target_parts = proto_parts(target_sum(col_parts, codes[0], units, partner[None, :], at, 1)[0])
    raw_grad, penalty = loss_grad(raw_parts, logit_parts, target_parts, at)

    if short:
        pre_all = after(pre_all, raw_grad)
        ins = (at, pre_all.reshape(n_batch, rows, -1), columns, stats, gain, shift, w_second)
        e_rows, hidden = -(-e_cols // 16) * 16, w_second.shape[0]
        table = (2, n_batch, hidden)
        flat = flat_sums(*ins[1:-1])
        own = raw_grad[None]
        rest = [swap(raw_grad, "batch", k) for k in (2, 4, 6)]
        rest = jnp.stack([rest[0]] + [after(piece, *flat) for piece in rest[1:]])
        far_own, own_core = swap(own, "batch", 1), swap(own, "proto", 1)
        far_own_core = swap(far_own, "proto", 1)
        rest, far_own, own_core, far_own_core = lax.optimization_barrier((rest, far_own, own_core, far_own_core))
        far, rest_core = swap(rest, "batch", 1), swap(rest, "proto", 1)
        other_penalty = swap(after(penalty, rest), "proto", 1)
        penalty = jnp.concatenate(
            [jnp.where(first, penalty, other_penalty), jnp.where(first, other_penalty, penalty)], axis=1
        )
        half = tail_call(
            near_kernel, [(d_cols, hidden), (e_rows, hidden), table], [(crops_all // 2, hidden)],
            *ins, [own, rest, own_core, rest_core], [], "tail_near",
        )
        far, penalty, *half = lax.optimization_barrier((far, penalty, *half, *flat))
        grad_w1, grad_w2, grad_gain, grad_shift = tail_call(
            functools.partial(far_kernel, crops_all),
            [(d_cols, hidden), (e_cols, hidden), (1, hidden), (1, hidden)], [table],
            *ins, [far_own, far, far_own_core, swap(far, "proto", 1)], half, "tail_far",
        )
    else:
        by_owner = jnp.swapaxes(features.astype(F32).reshape(rows, n_batch, d_cols), 0, 1)
        columns = columns_cast(lax.all_to_all(by_owner, "batch", 0, 0).reshape(crops_all, d_cols))
        raw_all = lax.all_gather(raw_grad, "batch", tiled=True)
        grad_w1, grad_w2, grad_gain, grad_shift = whole_tail(
            pre_all, columns, stats, gain, shift, w_second, raw_all, at, e_cols
        )
    return (penalty[0], grad_w1, grad_gain[0], grad_shift[0], grad_w2.T)


def solution(mesh):
    return jax.shard_map(
        body,
        mesh=mesh,
        in_specs=(
            P("batch", None),
            P(None, "proto"),
            P("proto"),
            P("proto"),
            P("proto", None),
            P("proto", None),
            P("batch"),
        ),
        out_specs=(P("batch"), P("batch", "proto"), P("proto"), P("proto"), P("proto", "batch")),
        check_vma=False,
    )
```
